32 devices in a mesh: rows: 8 (over z, y), batch: 4 (over x, core).
Axes of the slice: x: 2, y: 2, z: 4, core: 2. Of those that a mesh axis runs over, the one named last changes fastest.
Arguments:
- features: bfloat16 [3, 4, 208, 14, 1024], P(None, 'batch', 'rows'), may hold values from -29 to 29
- view_kind: int32 [3, 4, 24], P(None, 'batch'), may hold values from 0 to 1, as said below
- narrow_one: bfloat16 [1024, 256], P('rows'), may hold values from -0.1875 to 0.1875
- spatial_one: bfloat16 [2304, 256], P('rows'), may hold values from -0.125 to 0.125
- expand_one: bfloat16 [256, 1024], P('rows'), may hold values from -0.375 to 0.375
- gains_one: float32 [1536], replicated, may hold values from 0.1 to 1.9
- biases_one: float32 [1536], replicated, may hold values from -2.5 to 2.5
- narrow_two: bfloat16 [1024, 512], P('rows'), may hold values from -0.1875 to 0.1875
- spatial_two: bfloat16 [4608, 512], P('rows'), may hold values from -0.09375 to 0.09375
- expand_two: bfloat16 [512, 2048], P('rows'), may hold values from -0.25 to 0.25
- shortcut: bfloat16 [1024, 2048], P('rows'), may hold values from -0.1875 to 0.1875
- gains_two: float32 [5120], replicated, may hold values from 0.1 to 1.9
- biases_two: float32 [5120], replicated, may hold values from -2.5 to 2.5
- cotangent: bfloat16 [3, 4, 152, 7, 2048], P(None, 'batch', 'rows'), may hold values from -6 to 6
Outputs:
- outputs: bfloat16 [3, 4, 152, 7, 2048], P(None, 'batch', 'rows')
- grad_input: float32 [3, 4, 208, 14, 1024], P(None, 'batch', 'rows')
- grad_narrow_one: float32 [1024, 256], P('rows')
- grad_spatial_one: float32 [2304, 256], P('rows')
- grad_expand_one: float32 [256, 1024], P('rows')
- grad_gains_one: float32 [1536], replicated
- grad_biases_one: float32 [1536], replicated
- grad_narrow_two: float32 [1024, 512], P('rows')
- grad_spatial_two: float32 [4608, 512], P('rows')
- grad_expand_two: float32 [512, 2048], P('rows')
- grad_shortcut: float32 [1024, 2048], P('rows')
- grad_gains_two: float32 [5120], replicated
- grad_biases_two: float32 [5120], replicated
The draws below stay inside these ranges and needn't reach their ends.
Inputs may be any that keep to these rules, and one draw needn't show every extreme that they name: `view_kind`: for each micro-batch and image group exactly 8 entries are 1 and 16 are 0, so the views fill the 208 stacked rows exactly.
All inputs are finite; a program needn't handle non-finite values.
Results may differ from the reference program's by a relative error of at most 0.02.
Values may be sent and summed in bfloat16 or wider, within the bound.
No kernel may reach another device: no remote copies, remote signals or barrier semaphores. Data moves between devices by JAX's collectives and lax.ppermute only.
A program may use at most 256 MiB of HBM per device.

```python
import jax
import jax.numpy as jnp
from jax import lax

FEAT = 1024
MID_ONE = 256
MID_TWO = 512
OUT_TWO = 2048
WIDE = 14
MB = 3
RDEV = 26
BGRP = 4
ROWS = 208
SRC = 4
VIEWS = 24
HALF = 19
OUTROWS = 152
N_ROWS = 8


def draw_features(key, part):
    key = jax.random.fold_in(key, 3)
    base_key, row_key, chan_key = jax.random.split(key, 3)
    shape = (MB, BGRP, ROWS, WIDE, FEAT)
    position = jnp.arange(ROWS, dtype=jnp.float32) / ROWS
    rising = jnp.exp(jnp.log(3.0) * position)
    row_scale = jnp.exp(jnp.log(10.0) * 0.5 * (jax.random.uniform(row_key, (MB, BGRP, ROWS), jnp.float32) - 0.5))
    chan_scale = jnp.exp(jnp.log(10.0) * 0.5 * (jax.random.uniform(chan_key, (FEAT,), jnp.float32) - 0.5))
    scale = 0.5 * rising[None, None, :, None, None] * row_scale[..., None, None] * chan_scale
    base = jax.random.normal(base_key, shape, jnp.float32)
    return (jnp.clip(base, -6.0, 6.0) * scale).astype(jnp.bfloat16)


def draw_view_kind(key, part):
    key = jax.random.fold_in(key, 7)
    ordered = jnp.broadcast_to(jnp.arange(VIEWS, dtype=jnp.int32), (MB, BGRP, VIEWS))
    shuffled = jax.random.permutation(key, ordered, axis=2, independent=True)
    return (shuffled < 2 * SRC).astype(jnp.int32)


def steps_of(own_key, extent, cuts, least, top_value):
    level = 1.0
    for dim, shards_of in cuts:
        steps = jax.random.uniform(jax.random.fold_in(jax.random.fold_in(own_key, 6), dim), (shards_of,), jnp.float32, least / len(cuts), top_value / len(cuts))
        level = level * jnp.repeat(jnp.exp(steps), extent[dim] // shards_of).reshape((-1,) + (1,) * (len(extent) - 1 - dim))
    return level


def bell_draw(rng, extent, scale, reach, cuts=(), kind=jnp.bfloat16):
    drawn = scale * jax.random.normal(rng, extent, jnp.float32)
    if cuts:
        drawn = drawn * steps_of(rng, extent, cuts, -0.22, 0.18)
    return jnp.clip(drawn, -reach, reach).astype(kind)


def setup_inputs(seed: int = 0) -> dict:
    key_list = jax.random.split(jax.random.key(seed), 15)
    features = draw_features(jax.random.fold_in(key_list[14], 71), 0)
    view_kind = draw_view_kind(jax.random.fold_in(key_list[14], 71), 0)
    narrow_one = bell_draw(key_list[2], (FEAT, MID_ONE), FEAT ** -0.5, 0.1875, ((0, 8),))
    spatial_one = bell_draw(key_list[3], (9 * MID_ONE, MID_ONE), (9 * MID_ONE) ** -0.5, 0.125, ((0, 8),))
    expand_one = bell_draw(key_list[4], (MID_ONE, FEAT), MID_ONE ** -0.5, 0.375, ((0, 8),))
    gains_one = jnp.clip(1.0 + 0.18 * jax.random.normal(key_list[5], (2 * MID_ONE + FEAT,), jnp.float32), 0.1, 1.9)
    biases_one = bell_draw(key_list[6], (2 * MID_ONE + FEAT,), 0.5, 2.5, (), jnp.float32)
    narrow_two = bell_draw(key_list[7], (FEAT, MID_TWO), FEAT ** -0.5, 0.1875, ((0, 8),))
    spatial_two = bell_draw(key_list[8], (9 * MID_TWO, MID_TWO), (9 * MID_TWO) ** -0.5, 0.09375, ((0, 8),))
    expand_two = bell_draw(key_list[9], (MID_TWO, OUT_TWO), MID_TWO ** -0.5, 0.25, ((0, 8),))
    shortcut = bell_draw(key_list[10], (FEAT, OUT_TWO), FEAT ** -0.5, 0.1875, ((0, 8),))
    gains_two = jnp.clip(1.0 + 0.18 * jax.random.normal(key_list[11], (2 * MID_TWO + 2 * OUT_TWO,), jnp.float32), 0.1, 1.9)
    biases_two = bell_draw(key_list[12], (2 * MID_TWO + 2 * OUT_TWO,), 0.5, 2.5, (), jnp.float32)
    cotangent = bell_draw(key_list[13], (MB, BGRP, OUTROWS, WIDE // 2, OUT_TWO), 1.0, 6.0, ((1, 4), (2, 8)))
    return {"features": features, "view_kind": view_kind, "narrow_one": narrow_one, "spatial_one": spatial_one, "expand_one": expand_one, "gains_one": gains_one, "biases_one": biases_one, "narrow_two": narrow_two, "spatial_two": spatial_two, "expand_two": expand_two, "shortcut": shortcut, "gains_two": gains_two, "biases_two": biases_two, "cotangent": cotangent}


EPS = 1e-05
HIGHEST = lax.Precision.HIGHEST

@jax.custom_vjp
def low(v):
    return lax.optimization_barrier(v.astype(jnp.bfloat16)).astype(jnp.float32)

@jax.custom_vjp
def low_back(v):
    return v

def low_keep(v):
    return (low(v), None)

def low_pass(kept, grad):
    return (grad,)

def back_keep(v):
    return (v, None)

def back_low(kept, grad):
    return (low(grad),)
low.defvjp(low_keep, low_pass)
low_back.defvjp(back_keep, back_low)

def layout(view_kinds, row_ids):
    heights = 6 + 8 * view_kinds
    row_ends = jnp.cumsum(heights, dtype=jnp.int32)
    starts = row_ends - heights
    inside = ((starts[None, :] <= row_ids[:, None]) & (row_ids[:, None] < row_ends[None, :])).astype(jnp.int32)
    widths = lax.optimization_barrier(jnp.sum(inside * heights[None, :], axis=1, dtype=jnp.int32))
    firsts = lax.optimization_barrier(jnp.sum(inside * starts[None, :], axis=1, dtype=jnp.int32))
    return (widths, firsts)

def product(left, right):
    return jnp.einsum('...k,kn->...n', left, right, precision=HIGHEST)

def normalize(pre_value, cell_mask, gain_part, bias_part, population):
    masked = cell_mask[..., None]
    average = lax.optimization_barrier(jnp.sum(pre_value * masked, axis=(0, 1, 2))) / population
    squares = lax.optimization_barrier(jnp.sum(pre_value * pre_value * masked, axis=(0, 1, 2))) / population
    inv_std = lax.rsqrt(squares - average * average + EPS)
    return gain_part * ((pre_value - average) * inv_std) + bias_part

def conv_one(planes, upper_ok, lower_ok, weight):
    across = planes.shape[2]
    middle = planes.shape[3]
    zero_row = jnp.zeros_like(planes[:, :1])
    above = jnp.concatenate([zero_row, planes[:, :-1]], 1) * upper_ok[..., None, None]
    below = jnp.concatenate([planes[:, 1:], zero_row], 1) * lower_ok[..., None, None]
    summed = 0.0
    tap_id = 0
    for rowset in (above, planes, below):
        framed = jnp.pad(rowset, ((0, 0), (0, 0), (1, 1), (0, 0)))
        for offset in range(3):
            summed = summed + product(framed[:, :, offset:offset + across], weight[tap_id * middle:(tap_id + 1) * middle])
            tap_id += 1
    return summed

def conv_two(planes, not_first, weight):
    groups, row_count, across, middle = planes.shape
    paired = planes.reshape(groups, row_count // 2, 2, across, middle)
    even_rows = paired[:, :, 0]
    odd_rows = paired[:, :, 1]
    prior_rows = jnp.concatenate([jnp.zeros_like(odd_rows[:, :1]), odd_rows[:, :-1]], 1) * not_first[..., None, None]
    summed = 0.0
    tap_id = 0
    for rowset in (prior_rows, even_rows, odd_rows):
        split_cols = rowset.reshape(groups, row_count // 2, across // 2, 2, middle)
        even_cols = split_cols[:, :, :, 0]
        odd_cols = split_cols[:, :, :, 1]
        left_cols = jnp.concatenate([jnp.zeros_like(odd_cols[:, :, :1]), odd_cols[:, :, :-1]], 2)
        for piece_now in (left_cols, even_cols, odd_cols):
            summed = summed + product(piece_now, weight[tap_id * middle:(tap_id + 1) * middle])
            tap_id += 1
    return summed

def block_one(incoming, cell_mask, upper_ok, lower_ok, narrow, spatial, expand, gain_all, biases):
    population = BGRP * SRC * 536
    gain_parts = jnp.split(gain_all, [MID_ONE, 2 * MID_ONE])
    bias_parts = jnp.split(biases, [MID_ONE, 2 * MID_ONE])
    masked = cell_mask[..., None]
    entry_rows = incoming * masked
    pre_one = low_back(product(entry_rows, narrow))
    act_one = low(jax.nn.gelu(normalize(pre_one, cell_mask, gain_parts[0], bias_parts[0], population)) * masked)
    pre_two = low_back(conv_one(act_one, upper_ok, lower_ok, spatial))
    act_two = low(jax.nn.gelu(normalize(pre_two, cell_mask, gain_parts[1], bias_parts[1], population)) * masked)
    pre_three = low_back(product(act_two, expand))
    summed_one = normalize(pre_three, cell_mask, gain_parts[2], bias_parts[2], population) + entry_rows
    return low(low_back(jax.nn.gelu(summed_one) * masked))

def block_two(block_out, cell_mask, half_mask, not_first, narrow, spatial, expand, bypass, gain_all, biases):
    full_population = BGRP * SRC * 536
    half_population = BGRP * SRC * 134
    cuts = [MID_TWO, 2 * MID_TWO, 2 * MID_TWO + OUT_TWO]
    gain_parts = jnp.split(gain_all, cuts)
    bias_parts = jnp.split(biases, cuts)
    masked = cell_mask[..., None]
    masked_half = half_mask[..., None]
    pre_four = low_back(product(block_out, narrow))
    act_four = low(jax.nn.gelu(normalize(pre_four, cell_mask, gain_parts[0], bias_parts[0], full_population)) * masked)
    pre_five = low_back(conv_two(act_four, not_first, spatial))
    act_five = low(jax.nn.gelu(normalize(pre_five, half_mask, gain_parts[1], bias_parts[1], half_population)) * masked_half)
    pre_six = low_back(product(act_five, expand))
    groups = block_out.shape[0]
    corner = block_out.reshape(groups, ROWS // 2, 2, WIDE // 2, 2, FEAT)[:, :, 0, :, 0]
    pre_seven = low_back(product(corner, bypass))
    joined = normalize(pre_six, half_mask, gain_parts[2], bias_parts[2], half_population) + normalize(pre_seven, half_mask, gain_parts[3], bias_parts[3], half_population)
    return jax.nn.gelu(joined) * masked_half

def to_windows(stacked, firsts):
    slots = jnp.arange(N_ROWS * HALF, dtype=jnp.int32)
    device_of = slots // HALF
    position = slots % HALF
    source_row = device_of * (RDEV // 2) + position
    present = source_row < ROWS // 2
    clipped = jnp.minimum(source_row, ROWS // 2 - 1)
    owner_ids = firsts[:, 0::2][:, clipped] // RDEV
    keep_mask = (present[None, :] & (owner_ids == device_of[None, :])).astype(jnp.float32)
    return stacked[:, clipped] * keep_mask[..., None, None]

def reference(features, view_kind, narrow_one, spatial_one, expand_one, gains_one, biases_one, narrow_two, spatial_two, expand_two, shortcut, gains_two, biases_two, cotangent):
    row_ids = jnp.arange(ROWS, dtype=jnp.int32)
    columns = jnp.arange(WIDE, dtype=jnp.int32)
    half_columns = jnp.arange(WIDE // 2, dtype=jnp.int32)
    params = (narrow_one.astype(jnp.float32), spatial_one.astype(jnp.float32), expand_one.astype(jnp.float32), gains_one.astype(jnp.float32), biases_one.astype(jnp.float32), narrow_two.astype(jnp.float32), spatial_two.astype(jnp.float32), expand_two.astype(jnp.float32), shortcut.astype(jnp.float32), gains_two.astype(jnp.float32), biases_two.astype(jnp.float32))

    def forward(inputs, weights):
        results = []
        for micro_id in range(MB):
            widths, firsts = jax.vmap(layout, in_axes=(0, None))(view_kind[micro_id], row_ids)
            cell_mask = (columns[None, None, :] < widths[:, :, None]).astype(jnp.float32)
            same_prev = (firsts[:, :-1] == firsts[:, 1:]).astype(jnp.float32)
            upper_ok = jnp.pad(same_prev, ((0, 0), (1, 0)))
            lower_ok = jnp.pad(same_prev, ((0, 0), (0, 1)))
            half_mask = (half_columns[None, None, :] < (widths[:, 0::2] // 2)[:, :, None]).astype(jnp.float32)
            not_first = (firsts[:, 0::2] != row_ids[None, 0::2]).astype(jnp.float32)
            block_out = jax.checkpoint(block_one)(inputs[micro_id], cell_mask, upper_ok, lower_ok, weights[0], weights[1], weights[2], weights[3], weights[4])
            stacked = jax.checkpoint(block_two)(block_out, cell_mask, half_mask, not_first, weights[5], weights[6], weights[7], weights[8], weights[9], weights[10])
            results.append(to_windows(stacked, firsts))
        return jnp.stack(results)
    outcome, pullback = jax.vjp(forward, features.astype(jnp.float32), params)
    grad_in, grad_params = pullback(cotangent.astype(jnp.float32))
    return (outcome.astype(jnp.bfloat16), grad_in, grad_params[0], grad_params[1], grad_params[2], grad_params[3], grad_params[4], grad_params[5], grad_params[6], grad_params[7], grad_params[8], grad_params[9], grad_params[10])
```

```python
import functools

import jax
import jax.numpy as jnp
from jax import lax
from jax.experimental import pallas as pl
from jax.experimental.pallas import tpu as pltpu
from jax.sharding import PartitionSpec as P

SPILL = 12
WIN = 40
COLS = 16
EPS = 1e-05
AXES = ("rows", "batch")
BF = jnp.bfloat16
F32 = jnp.float32
CHUNK = 32
TANH_SCALE = 0.7978845608028654
TANH_CUBE = 0.044715


def gelu(x):
    return 0.5 * x * (1.0 + jnp.tanh(TANH_SCALE * (x + TANH_CUBE * x * x * x)))


def gelu_slope(x):
    square = x * x
    t = jnp.tanh(TANH_SCALE * x * (1.0 + TANH_CUBE * square))
    return 0.5 * (1.0 + t) + 0.5 * TANH_SCALE * x * (1.0 - t * t) * (1.0 + 3.0 * TANH_CUBE * square)


def nn(a, b):
    return lax.dot_general(a, b, (((1,), (0,)), ((), ())), preferred_element_type=F32)


def nt(a, b):
    return lax.dot_general(a, b, (((1,), (1,)), ((), ())), preferred_element_type=F32)


def pick(ref, row, start=0, width=None):
    table = ref[:, start : start + (width or ref.shape[1])]
    rows = lax.broadcasted_iota(jnp.int32, table.shape, 0)
    return jnp.sum(jnp.where(rows == row, table, 0.0), axis=0, keepdims=True)


def moments(ref, m, population):
    average = pick(ref, 2 * m) * (1.0 / population)
    inv = lax.rsqrt(pick(ref, 2 * m + 1) * (1.0 / population) - average * average + EPS)
    return average, inv


def means(ref, m, population, start=0, width=None):
    share = 1.0 / population
    return pick(ref, 2 * m, start, width) * share, pick(ref, 2 * m + 1, start, width) * share


def put_sums(ref, m, first, second, start=0):
    c = first.shape[1]
    at = slice(start, start + c)

    @pl.when(m == 0)
    def _():
        ref[:, at] = jnp.zeros((ref.shape[0], c), F32)

    first = jnp.sum(first, axis=0, keepdims=True)
    second = jnp.sum(second, axis=0, keepdims=True)
    rows = lax.broadcasted_iota(jnp.int32, (ref.shape[0], c), 0)
    ref[:, at] = jnp.where(rows == 2 * m, first, jnp.where(rows == 2 * m + 1, second, ref[:, at]))


def fold(x):
    return jnp.sum(x.reshape(-1, 8, x.shape[-1]), axis=0)


def over(count, step, body, carry=None):
    def run(i, c):
        return body(pl.multiple_of(i * step, step), c)

    if carry is None:
        lax.fori_loop(0, count // step, lambda i, c: (run(i, None), 0)[1], 0)
        return None
    return lax.fori_loop(0, count // step, run, carry)


LANES = 128


def put_tall(ref, rows, value):
    for j in range(ref.shape[0]):
        ref[j, rows, :] = value[:, j * LANES : (j + 1) * LANES]


def get_tall(ref, rows):
    return jnp.concatenate([ref[j, rows, :] for j in range(ref.shape[0])], 1)


def zero_pair(c):
    return jnp.zeros((8, c), F32), jnp.zeros((8, c), F32)


def sum_pair(carry, a, b):
    return carry[0] + fold(a), carry[1] + fold(a * b)


OWN, MINE, UPPER, LOWER = 0, 1, 2, 3
HALF, INNER = 0, 1


def lane(ref, which, rows):
    return ref[0, rows, which : which + 1]


def k_masks(own, anchor, kinds, full, halved):
    first = anchor[0]
    height_of = lambda m, v: 6 + 8 * kinds[m, 0, v]
    for m in range(full.shape[0]):
        rows = full.shape[1] // COLS
        row = first + lax.broadcasted_iota(jnp.int32, (rows, LANES), 0)

        def view(v, c):
            at, width, start, last = c
            height = height_of(m, v)
            inside = (row >= at) & (row < at + height)
            return (
                at + height,
                jnp.where(inside, height, width),
                jnp.where(inside, at, start),
                jnp.where(inside, at + height - 1, last),
            )

        zero = jnp.zeros((rows, LANES), jnp.int32)
        _, width, start, last = lax.fori_loop(0, kinds.shape[2], view, (jnp.int32(0), zero, zero, zero))
        owned = (start >= first) & (start < first + own) & (width > 0)
        mine = jnp.where(owned, width, 0)
        above = (start != row).astype(F32)
        below = (last != row).astype(F32)
        cells = lambda v, n: jnp.broadcast_to(v[:, None, :], (v.shape[0], n, LANES))
        shape = (rows, COLS, LANES)
        column = lax.broadcasted_iota(jnp.int32, shape, 1)
        lanes = lax.broadcasted_iota(jnp.int32, shape, 2)
        value = jnp.where(lanes == OWN, (column < cells(width, COLS)).astype(F32), 0.0)
        value = jnp.where(lanes == MINE, (column < cells(mine, COLS)).astype(F32), value)
        value = jnp.where(lanes == UPPER, cells(above, COLS), value)
        value = jnp.where(lanes == LOWER, cells(below, COLS), value)
        full[m] = value.reshape(rows * COLS, LANES)
        shape = (rows, COLS // 2, LANES)
        column = lax.broadcasted_iota(jnp.int32, shape, 1)
        lanes = lax.broadcasted_iota(jnp.int32, shape, 2)
        value = jnp.where(lanes == HALF, (2 * column < cells(mine, COLS // 2)).astype(F32), 0.0)
        value = jnp.where(lanes == INNER, cells(above, COLS // 2), value)
        value = value.reshape(rows // 2, 2, COLS // 2, LANES)[:, 0]
        halved[m] = value.reshape(rows * COLS // 4, LANES)


def k_first(pieces, place, features, mask, *refs):
    parts, (pre, head, total, weight, rows) = refs[:pieces], refs[pieces:]
    m = pl.program_id(0)
    own, across = features.shape[2], features.shape[3]

    @pl.when(m == 0)
    def _():
        if pieces == 1:
            weight[...] = parts[0][...]
        else:
            size = parts[0].shape[0]
            half = size // 2
            weight[pl.ds(pl.multiple_of(place[0] * size, size), size), :] = parts[0][...]
            for k in range(1, pieces // 2 + 1):
                for side in range(2):
                    at = jnp.bitwise_xor(place[0], k) * size + jnp.bitwise_xor(place[1], side) * half
                    weight[pl.ds(pl.multiple_of(at, half), half), :] = parts[2 * k - 1 + side][...]
        rows[...] = jnp.zeros_like(rows)

    for r in range(own):
        rows[r * COLS : r * COLS + across, :] = features[0, 0, r]
    pre[0] = nn(rows[...] * lane(mask, OWN, slice(0, own * COLS)).astype(BF), weight[...])
    head[0] = pre[0, 0 : head.shape[1], :].astype(BF)

    def add(r, c):
        p = pre[0, pl.ds(r, CHUNK), :]
        return sum_pair(c, p, p)

    put_sums(total, m, *over(own * COLS, CHUNK, add, zero_pair(pre.shape[2])))


def k_entry(features, mask, *refs):
    spills, (entry, rows) = refs[:-2], refs[-2:]
    m = pl.program_id(0)
    own, across = features.shape[2], features.shape[3]

    @pl.when(m == 0)
    def _():
        rows[...] = jnp.zeros_like(rows)

    for r in range(own):
        rows[r * COLS : r * COLS + across, :] = features[0, 0, r]
    for k, spill in enumerate(spills):

        @pl.when(m == k)
        def _():
            for r in range(spill.shape[0]):
                at = (own + r) * COLS
                rows[at : at + across, :] = spill[r]

    entry[0] = rows[...] * lane(mask, MINE, slice(None)).astype(BF)


def load_pre_one(own, spill, r, size):
    edge = own.shape[1]
    if r < edge:
        return own[0, r : r + size, :]
    if r - edge < spill.shape[1]:
        return spill[0, r - edge : r - edge + size, :].astype(F32)
    return jnp.zeros((size, own.shape[2]), F32)


def spread_trio(source, trio, cells):
    c = source.shape[1]
    trio[0:COLS, :] = jnp.zeros((COLS, 3 * c), BF)
    trio[COLS + cells : 2 * COLS + cells, :] = jnp.zeros((COLS, 3 * c), BF)
    for r in range(0, cells, CHUNK):
        for tap in range(3):
            part = source[COLS + r + tap - 1 : COLS + r + tap - 1 + CHUNK, :]
            trio[COLS + r : COLS + r + CHUNK, tap * c : (tap + 1) * c] = part.astype(BF)


def conv_rows(trio, mask, weight, cells):
    width = trio.shape[1]
    upper = lane(mask, UPPER, slice(None)).astype(BF)
    lower = lane(mask, LOWER, slice(None)).astype(BF)
    above = trio[0:cells, :] * upper
    here = trio[COLS : COLS + cells, :]
    below = trio[2 * COLS : 2 * COLS + cells, :] * lower
    total = (
        nn(above, weight[0:width, :])
        + nn(here, weight[width : 2 * width, :])
        + nn(below, weight[2 * width : 3 * width, :])
    )
    return total, (above, here, below)


def k_second(count, own, spill, total, gain, bias, mask, weight, pre, patch, out_total, act, trio):
    m = pl.program_id(0)
    cells, c = mask.shape[1], own.shape[2]
    average, inv = moments(total, m, count)
    scale = inv * gain[...]
    act[0:COLS, :] = jnp.zeros((COLS, c), F32)
    act[COLS + cells : 2 * COLS + cells, :] = jnp.zeros((COLS, c), F32)
    for r in range(0, cells, CHUNK):
        x = (load_pre_one(own, spill, r, CHUNK) - average) * scale + bias[...]
        act[COLS + r : COLS + r + CHUNK, :] = gelu(x) * lane(mask, MINE, slice(r, r + CHUNK))
    spread_trio(act, trio, cells)
    result, parts = conv_rows(trio, mask, weight, cells)
    pre[0] = result
    for k, part in enumerate(parts):
        patch[0, :, k * 3 * c : (k + 1) * 3 * c] = part

    def add(r, carry):
        p = pre[0, pl.ds(r, CHUNK), :]
        return sum_pair(carry, p * lane(mask, MINE, pl.ds(r, CHUNK)), p)

    put_sums(out_total, m, *over(cells, CHUNK, add, zero_pair(c)))


def k_third(count, which, pre_in, total, gain, bias, mask, weight, act, pre, out_total):
    m = pl.program_id(0)
    cells = pre_in.shape[1]
    average, inv = moments(total, m, count)
    scale = inv * gain[...]

    def step(r, _):
        x = (pre_in[0, pl.ds(r, CHUNK), :] - average) * scale + bias[...]
        act[0, pl.ds(r, CHUNK), :] = (gelu(x) * lane(mask, which, pl.ds(r, CHUNK))).astype(BF)

    over(cells, CHUNK, step)
    pre[0] = nn(act[0], weight[...])

    def add(r, carry):
        p = pre[0, pl.ds(r, CHUNK), :]
        return sum_pair(carry, p, p)

    put_sums(out_total, m, *over(cells, CHUNK, add, zero_pair(pre.shape[2])))


def k_fourth(count, pre_in, entry, total, gain, bias, mask, weight, block, corner, pre, out_total, full):
    m = pl.program_id(0)
    cells, c = pre_in.shape[1], pre_in.shape[2]
    average, inv = moments(total, m, count)
    scale = inv * gain[...]

    def step(r, _):
        for k in range(4):
            at = pl.ds(r + k * COLS, COLS)
            x = (pre_in[0, at, :] - average) * scale + bias[...] + entry[0, at, :].astype(F32)
            y = gelu(x) * lane(mask, MINE, at)
            put_tall(full, slice(k * COLS, (k + 1) * COLS), y)
            block[0, at, :] = y.astype(BF)
        pair = [get_tall(full, pl.ds(k * COLS, COLS // 2, stride=2)) for k in (0, 2)]
        corner[0, pl.ds(pl.multiple_of(r // 4, COLS), COLS), :] = jnp.concatenate(pair, 0).astype(BF)

    over(cells, 4 * COLS, step)
    pre[0] = nn(block[0], weight[...])

    def add(r, carry):
        p = pre[0, pl.ds(r, CHUNK), :]
        return sum_pair(carry, p, p)

    put_sums(out_total, m, *over(cells, CHUNK, add, zero_pair(pre.shape[2])))


def k_seventh(corner, weight, pre, out_total):
    m = pl.program_id(1)
    pre[0] = nn(corner[0], weight[...])

    def add(r, carry):
        p = pre[0, pl.ds(r, CHUNK), :]
        return sum_pair(carry, p, p)

    put_sums(out_total, m, *over(pre.shape[1], CHUNK, add, zero_pair(pre.shape[2])))


def k_fifth(count, pre_in, total, gain, bias, mask, half_mask, weight, pre, patch, out_total, act, eo, oe, oo):
    m = pl.program_id(0)
    cells, c = pre_in.shape[1], pre_in.shape[2]
    half = cells // 4
    wide = COLS // 2
    average, inv = moments(total, m, count)
    scale = inv * gain[...]

    def step(r, _):
        x = (pre_in[0, pl.ds(r, CHUNK), :] - average) * scale + bias[...]
        put_tall(act, pl.ds(r, CHUNK), gelu(x) * lane(mask, MINE, pl.ds(r, CHUNK)))

    over(cells, CHUNK, step)
    pad = 2 * wide
    for buf in (eo, oe, oo):
        buf[0:pad, :] = jnp.zeros((pad, c), F32)
    for j in range(c // LANES):
        lanes = slice(j * LANES, (j + 1) * LANES)
        even = act[j, pl.ds(0, cells // 2, stride=2), :].reshape(half // wide, 2, wide, LANES)
        odd = act[j, pl.ds(1, cells // 2, stride=2), :].reshape(half // wide, 2, wide, LANES)
        patch[0, :, 4 * c + j * LANES : 4 * c + (j + 1) * LANES] = even[:, 0].reshape(half, LANES).astype(BF)
        oe[pad : pad + half, lanes] = even[:, 1].reshape(half, LANES)
        eo[pad : pad + half, lanes] = odd[:, 0].reshape(half, LANES)
        oo[pad : pad + half, lanes] = odd[:, 1].reshape(half, LANES)
    first = lane(half_mask, INNER, slice(None))
    take = lambda buf, back: buf[pad - back : pad - back + half, :]
    taps = (
        take(oo, wide + 1) * first, take(oe, wide) * first, take(oo, wide) * first,
        take(eo, 1), None, take(eo, 0),
        take(oo, 1), take(oe, 0), take(oo, 0),
    )
    for k, tap in enumerate(taps):
        if tap is not None:
            patch[0, :, k * c : (k + 1) * c] = tap.astype(BF)
    pre[0] = nn(patch[0], weight[...])

    def add(r, carry):
        p = pre[0, pl.ds(r, CHUNK), :]
        return sum_pair(carry, p * lane(half_mask, HALF, pl.ds(r, CHUNK)), p)

    put_sums(out_total, m, *over(half, CHUNK, add, zero_pair(pre.shape[2])))


def k_last(count, six, seven, tot6, tot7, g6, b6, g7, b7, half_mask, cot, out, slope, total, line):
    m = pl.program_id(0)
    half, c = six.shape[1], six.shape[2]
    wide = COLS // 2
    shown, across = out.shape[2], out.shape[3]
    avg6, inv6 = moments(tot6, m, count)
    avg7, inv7 = moments(tot7, m, count)
    line[...] = jnp.zeros_like(line)

    def step(p, carry):
        at = pl.ds(pl.multiple_of(p * wide, wide), wide)
        mask = lane(half_mask, HALF, at)
        n6 = (six[0, at, :] - avg6) * inv6
        n7 = (seven[0, at, :] - avg7) * inv7
        joined = g6[...] * n6 + b6[...] + g7[...] * n7 + b7[...]
        out[0, 0, p] = (gelu(joined) * mask)[:across].astype(BF)
        line[0:across, :] = cot[0, 0, p].astype(F32)
        d = gelu_slope(joined) * (line[...] * mask)
        slope[0, at, :] = d
        return carry[0] + d, carry[1] + d * n6, carry[2] + d * n7

    zero = jnp.zeros((wide, c), F32)
    first, second, third = lax.fori_loop(0, shown, step, (zero, zero, zero))
    slope[0, shown * wide :, :] = jnp.zeros((half - shown * wide, c), F32)
    put_sums(total, m, first, second)
    put_sums(total, m, first, third, c)


def k_back_six(
    count, slope, six, seven, tot6, tot7, back, g6, g7, five, tot5, g5, b5, half_mask, weight,
    d_six, d_seven, d_five, out_total,
):
    m = pl.program_id(0)
    half, c = six.shape[1], six.shape[2]
    avg6, inv6 = moments(tot6, m, count)
    avg7, inv7 = moments(tot7, m, count)
    bias6, gain6 = means(back, m, count, 0, c)
    bias7, gain7 = means(back, m, count, c, c)
    scale6, scale7 = g6[...] * inv6, g7[...] * inv7

    def step(r, _):
        at = pl.ds(r, COLS)
        d = slope[0, at, :]
        mask = lane(half_mask, HALF, at)
        n6 = (six[0, at, :] - avg6) * inv6
        d_six[0, at, :] = (scale6 * (d - bias6 - n6 * gain6) * mask).astype(BF)
        n7 = (seven[0, at, :] - avg7) * inv7
        d_seven[0, at, :] = (scale7 * (d - bias7 - n7 * gain7) * mask).astype(BF)

    over(half, COLS, step)
    d_five[0] = nt(d_six[0], weight[...])
    avg5, inv5 = moments(tot5, m, count)

    def add(r, carry):
        at = pl.ds(r, CHUNK)
        n = (five[0, at, :] - avg5) * inv5
        d = gelu_slope(g5[...] * n + b5[...]) * d_five[0, at, :] * lane(half_mask, HALF, at)
        d_five[0, at, :] = d
        return sum_pair(carry, d, n)

    put_sums(out_total, m, *over(half, CHUNK, add, zero_pair(d_five.shape[2])))


def k_corner(d_seven, weight, d_corner):
    d_corner[0] = nt(d_seven[0], weight[...])


def k_back_five(
    half_count, full_count, d_five, five, tot5, back5, g5, half_mask, weight, four, tot4, g4, b4, mask,
    d_pre, d_four, out_total, grid_scratch, shifted,
):
    m = pl.program_id(0)
    half, c = five.shape[1], five.shape[2]
    cells = 4 * half
    wide = COLS // 2
    avg5, inv5 = moments(tot5, m, half_count)
    bias5, gain5 = means(back5, m, half_count)
    n5 = (five[0] - avg5) * inv5
    d = (g5[...] * inv5 * (d_five[0] - bias5 - n5 * gain5) * lane(half_mask, HALF, slice(None))).astype(BF)
    d_pre[0] = d
    wide_d = d.astype(F32)
    tail = 2 * wide
    shifted[half : half + tail, :] = jnp.zeros((tail, c), F32)
    shifted[0:half, :] = wide_d
    right = shifted[1 : 1 + half, :].astype(BF)
    shifted[0:half, :] = wide_d * lane(half_mask, INNER, slice(None))
    down = shifted[wide : wide + half, :].astype(BF)
    down_right = shifted[wide + 1 : wide + 1 + half, :].astype(BF)
    w = lambda tap: weight[tap * c : (tap + 1) * c, :]
    ee = nt(d, w(4))
    eo = nt(d, w(5)) + nt(right, w(3))
    oe = nt(d, w(7)) + nt(down, w(1))
    oo = nt(d, w(8)) + nt(right, w(6)) + nt(down, w(2)) + nt(down_right, w(0))
    rows = half // wide
    even = jnp.stack([ee.reshape(rows, wide, c), oe.reshape(rows, wide, c)], 1).reshape(cells // 2, c)
    odd = jnp.stack([eo.reshape(rows, wide, c), oo.reshape(rows, wide, c)], 1).reshape(cells // 2, c)
    put_tall(grid_scratch, pl.ds(0, cells // 2, stride=2), even)
    put_tall(grid_scratch, pl.ds(1, cells // 2, stride=2), odd)
    avg4, inv4 = moments(tot4, m, full_count)

    def add(r, carry):
        at = pl.ds(r, CHUNK)
        n = (four[0, at, :] - avg4) * inv4
        d = gelu_slope(g4[...] * n + b4[...]) * get_tall(grid_scratch, at) * lane(mask, MINE, at)
        d_four[0, at, :] = d
        return sum_pair(carry, d, n)

    put_sums(out_total, m, *over(cells, CHUNK, add, zero_pair(c)))


def k_back_four(
    count, d_four, four, tot4, back4, g4, mask, weight, d_corner, three, entry, tot3, g3, b3,
    d_pre, d_summed, out_total, placed,
):
    m = pl.program_id(0)
    cells, c = three.shape[1], three.shape[2]
    avg4, inv4 = moments(tot4, m, count)
    bias4, gain4 = means(back4, m, count)
    scale4 = g4[...] * inv4

    def step(r, _):
        at = pl.ds(r, CHUNK)
        n = (four[0, at, :] - avg4) * inv4
        d = scale4 * (d_four[0, at, :] - bias4 - n * gain4) * lane(mask, MINE, at)
        d_pre[0, at, :] = d.astype(BF)

    over(cells, CHUNK, step)
    d_summed[0] = nt(d_pre[0], weight[...])
    avg3, inv3 = moments(tot3, m, count)
    wide = COLS // 2
    placed[...] = jnp.zeros_like(placed)

    def add(r, carry):
        at = pl.ds(r, CHUNK)
        corner_at = pl.ds(pl.multiple_of(r // 4, wide), wide)
        put_tall(placed, pl.ds(0, wide, stride=2), d_corner[0, corner_at, :])
        for k in range(2):
            at = pl.ds(r + k * COLS, COLS)
            got = d_summed[0, at, :]
            if k == 0:
                got = got + get_tall(placed, slice(0, COLS))
            n = (three[0, at, :] - avg3) * inv3
            x = g3[...] * n + b3[...] + entry[0, at, :].astype(F32)
            d = gelu_slope(x) * (got.astype(BF).astype(F32) * lane(mask, MINE, at))
            d_summed[0, at, :] = d
            carry = sum_pair(carry, d, n)
        return carry

    put_sums(out_total, m, *over(cells, CHUNK, add, zero_pair(c)))


def k_back_three(count, d_summed, three, tot3, back3, g3, mask, weight, two, tot2, g2, b2, d_pre, d_two, out_total):
    m = pl.program_id(0)
    cells = three.shape[1]
    avg3, inv3 = moments(tot3, m, count)
    bias3, gain3 = means(back3, m, count)
    scale3 = g3[...] * inv3

    def step(r, _):
        at = pl.ds(r, COLS)
        n = (three[0, at, :] - avg3) * inv3
        d = scale3 * (d_summed[0, at, :] - bias3 - n * gain3) * lane(mask, MINE, at)
        d_pre[0, at, :] = d.astype(BF)

    over(cells, COLS, step)
    d_two[0] = nt(d_pre[0], weight[...])
    avg2, inv2 = moments(tot2, m, count)

    def add(r, carry):
        at = pl.ds(r, CHUNK)
        n = (two[0, at, :] - avg2) * inv2
        d = gelu_slope(g2[...] * n + b2[...]) * d_two[0, at, :] * lane(mask, MINE, at)
        d_two[0, at, :] = d
        return sum_pair(carry, d, n)

    put_sums(out_total, m, *over(cells, CHUNK, add, zero_pair(d_two.shape[2])))


def k_back_two(
    count, d_two, two, tot2, back2, g2, mask, weight, own, spill, tot1, g1, b1,
    d_pre, d_one, out_total, source, trio,
):
    m = pl.program_id(0)
    cells, c = two.shape[1], two.shape[2]
    avg2, inv2 = moments(tot2, m, count)
    bias2, gain2 = means(back2, m, count)
    scale2 = g2[...] * inv2
    source[0:COLS, :] = jnp.zeros((COLS, c), F32)
    source[COLS + cells : 2 * COLS + cells, :] = jnp.zeros((COLS, c), F32)
    for r in range(0, cells, CHUNK):
        n = (two[0, r : r + CHUNK, :] - avg2) * inv2
        d = scale2 * (d_two[0, r : r + CHUNK, :] - bias2 - n * gain2) * lane(mask, MINE, slice(r, r + CHUNK))
        d_pre[0, r : r + CHUNK, :] = d.astype(BF)
        source[COLS + r : COLS + r + CHUNK, :] = d
    spread_trio(source, trio, cells)
    d_one[0] = conv_rows(trio, mask, weight, cells)[0]
    avg1, inv1 = moments(tot1, m, count)
    carry = zero_pair(c)
    for r in range(0, cells, CHUNK):
        n = (load_pre_one(own, spill, r, CHUNK) - avg1) * inv1
        d = gelu_slope(g1[...] * n + b1[...]) * d_one[0, r : r + CHUNK, :] * lane(mask, MINE, slice(r, r + CHUNK))
        d_one[0, r : r + CHUNK, :] = d
        carry = sum_pair(carry, d, n)
    put_sums(out_total, m, *carry)


def k_back_one(count, d_one, own, spill, tot1, back1, g1, mask, d_pre):
    m = pl.program_id(0)
    cells = d_one.shape[1]
    avg1, inv1 = moments(tot1, m, count)
    bias1, gain1 = means(back1, m, count)
    scale1 = g1[...] * inv1
    for r in range(0, cells, CHUNK):
        n = (load_pre_one(own, spill, r, CHUNK) - avg1) * inv1
        d = scale1 * (d_one[0, r : r + CHUNK, :] - bias1 - n * gain1) * lane(mask, MINE, slice(r, r + CHUNK))
        d_pre[0, r : r + CHUNK, :] = d.astype(BF)


def k_input(d_pre, more_pre, d_summed, weight, *refs):
    more_summed, (out, both, sums) = refs[:-3], refs[-3:]
    m = pl.program_id(0)
    own, across = out.shape[2], out.shape[3]
    spilled = more_pre.shape[1]
    cells = own * COLS
    both[...] = d_pre[0, 0:cells, :]
    both[0:spilled, :] = d_pre[0, 0:spilled, :] + more_pre[0]
    sums[...] = nt(both[...], weight[...])
    for r in range(own):
        at = r * COLS
        line = sums[at : at + COLS, :] + d_summed[0, at : at + COLS, :]
        if at < spilled:
            extra = more_summed[0][at : at + COLS, :].astype(F32)
            for k in range(1, len(more_summed)):
                extra = jnp.where(m == k, more_summed[k][at : at + COLS, :].astype(F32), extra)
            line = line + extra
        out[0, 0, r] = line[:across]


def exchange(x, mask):
    total = lax.axis_size("rows") * lax.axis_size("batch")
    return lax.ppermute(x, AXES, [(i, i ^ mask) for i in range(total)])


def from_behind(x, by):
    devices = lax.axis_size("rows")
    pairs = [(i, i + by) for i in range(devices) if 0 <= i + by < devices]
    return lax.ppermute(x, "rows", pairs)


class Chain:
    def __init__(self, steps):
        self.steps, self.flying, self.done, self.result = steps, None, False, None
        self.ready = next(steps)

    def launch(self, array):
        self.flying = self.ready[1](array)

    def land(self):
        try:
            self.ready = self.steps.send(self.flying)
        except StopIteration as end:
            self.done, self.result = True, end.value
        self.flying = None

    def value(self):
        while not self.done:
            if self.flying is None:
                self.launch(self.ready[0])
            self.land()
        return self.result


def hook(x, start=(), finish=(), need=()):
    if not (start or finish or need):
        return x
    landed = []
    for chain in finish:
        if not chain.done:
            landed.append(chain.flying)
            chain.land()
    live = [chain for chain in start if not chain.done]
    tied = lax.optimization_barrier((x, [c.ready[0] for c in live], landed, list(need)))
    for chain, array in zip(live, tied[1]):
        chain.launch(array)
    return tied[0]


def global_sum(x, b=None, c=None, d=None):
    bits = device_bits()
    x = hook(x + exchange(x, 1), **(b or {}))
    step = 1
    while step < bits:
        low = 1 << step
        if step + 1 < bits:
            p, q, r = exchange(x, low), exchange(x, 2 * low), exchange(x, 3 * low)
            x = (x + p) + (q + r)
        else:
            x = x + exchange(x, low)
        if step == 1:
            x = hook(x, **(c or {}))
        step += 2
    return hook(x, **(d or {}))


def device_bits():
    total = lax.axis_size("rows") * lax.axis_size("batch")
    return total.bit_length() - 1


def my_bit(bit):
    number = lax.axis_index("rows") * lax.axis_size("batch") + lax.axis_index("batch")
    return (number >> bit) & 1


def batch_bits():
    return lax.axis_size("batch").bit_length() - 1


def across(bit):
    return lambda x: exchange(x, 1 << bit)


def gather_pieces(w):
    devices = lax.axis_size("rows")
    if devices > 8:
        return [lax.all_gather(w, "rows", axis=0, tiled=True)]
    half = lax.dynamic_slice_in_dim(w, my_bit(0) * (w.shape[0] // 2), w.shape[0] // 2)
    mine = [lax.ppermute(half, "rows", [(i, i ^ k) for i in range(devices)]) for k in range(1, devices)]
    return [w] + [p for m in mine for p in (m, exchange(m, 1))]


def lanes_of(w, parts):
    x = w.reshape(parts, -1, w.shape[1] // 256, 256)
    return x.transpose(0, 2, 1, 3).reshape(parts, -1, 256)


def from_lanes(x, c):
    parts = x.shape[0]
    x = x.reshape(parts, c // 256, -1, 256)
    return x.transpose(0, 2, 1, 3).reshape(-1, c)


def ordered(mine, other, bit, axis):
    upper = my_bit(bit) == 1
    return jnp.stack([jnp.where(upper, other, mine), jnp.where(upper, mine, other)], axis)


def gather_steps(packed):
    bits, low = device_bits(), batch_bits()
    x = lax.dynamic_index_in_dim(packed, lax.axis_index("batch"), 0, keepdims=False)
    for bit in list(range(low + 1, bits)) + [low]:
        got = yield x, across(bit)
        x = ordered(x, got, bit, 0 if bit > low else bits - low - 1)
    for bit in reversed(range(low)):
        got = yield x, across(bit)
        x = ordered(x, got, bit, x.ndim - 2)
    return x.reshape((-1,) + x.shape[-2:])


def gather_offloaded(w):
    quarters = lax.axis_size("batch")
    part = w.reshape(quarters, -1, w.shape[1])
    part = lax.dynamic_index_in_dim(part, lax.axis_index("batch"), 0, keepdims=False)
    return lax.all_gather(part, AXES, axis=0, tiled=True)


def sharded(grad, c):
    total = lax.axis_size("rows") * lax.axis_size("batch")
    if grad.shape[1] == c:
        return grad.reshape(total, -1, c)
    return lanes_of(grad, total)


def spread_steps(x):
    for bit in reversed(range(batch_bits())):
        got = yield x, across(bit)
        x = ordered(x, got, bit, x.ndim - 2)
    return x.reshape((-1,) + x.shape[-2:])


def reduce_steps(parts, first_bits):
    bits = device_bits()
    x = jnp.concatenate(parts, 1) if len(parts) > 1 else parts[0]
    x = x.reshape((2,) * bits + x.shape[1:])
    left = list(reversed(range(bits)))
    got = None
    for bit in list(first_bits) + [b for b in left if b not in first_bits]:
        axis = left.index(bit)
        left.remove(bit)
        half = lambda v, b: lax.dynamic_index_in_dim(v, b, axis, keepdims=False)
        keep, send = my_bit(bit), 1 - my_bit(bit)
        if got is None:
            x, give = half(x, keep), half(x, send)
        else:
            x, give = half(x, keep) + half(got, keep), half(x, send) + half(got, send)
        got = yield give, across(bit)
    return (yield from spread_steps(x + got))


def one_step(x, send):
    return (yield x, send)


def unpack(shard, shapes):
    devices = lax.axis_size("rows")
    out, at = [], 0
    for k, c in shapes:
        n = k * c // devices // shard.shape[0] // shard.shape[2]
        part = shard[:, at : at + n]
        out.append((from_lanes(part, c) if shard.shape[2] != c else part.reshape(-1, c)).astype(F32))
        at += n
    return out


def per_micro(shape):
    zeros = (0,) * (len(shape) - 1)
    return pl.BlockSpec((1,) + tuple(shape[1:]), lambda m: (m,) + zeros)


def whole(shape):
    zeros = (0,) * len(shape)
    return pl.BlockSpec(tuple(shape), lambda m: zeros, pipeline_mode=pl.Buffered(1))


def table(shape):
    zeros = (0,) * len(shape)
    return pl.BlockSpec(tuple(shape), lambda m: zeros)


def call(kernel, micro, ins, outs, scratch=(), limit=40, after=()):
    kind = {"m": per_micro, "w": whole, "s": lambda shape: pl.BlockSpec(memory_space=pltpu.SMEM)}
    in_specs = [k if isinstance(k, pl.BlockSpec) else kind[k](a.shape) for a, k in ins]
    in_specs += [pl.BlockSpec(memory_space=pl.ANY)] * len(after)
    out_specs = [per_micro(sh) if k == "m" else table(sh) for sh, _, k in outs]

    def run(*refs):
        kernel(*refs[: len(ins)], *refs[len(ins) + len(after) :])

    return pl.pallas_call(
        run,
        grid=(micro,),
        in_specs=in_specs,
        out_specs=out_specs,
        out_shape=[jax.ShapeDtypeStruct(sh, t) for sh, t, _ in outs],
        scratch_shapes=[pltpu.VMEM(sh, t) for sh, t in scratch],
        compiler_params=pltpu.CompilerParams(
            dimension_semantics=("arbitrary",), vmem_limit_bytes=limit * 1024 * 1024
        ),
        name=getattr(kernel, "func", kernel).__name__,
    )(*[a for a, _ in ins], *after)


def weight_term(left, right):
    k, n = left.shape[-1], right.shape[-1]
    return lax.dot_general(
        left.reshape(-1, k), right.reshape(-1, n), (((0,), (0,)), ((), ())), preferred_element_type=F32
    ).astype(BF)


def shards(
    features, view_kind, narrow_one, spatial_one, expand_one, gains_one, biases_one,
    narrow_two, spatial_two, expand_two, shortcut, gains_two, biases_two, cotangent,
):
    micro, _, own, across, channels = features.shape
    m1 = spatial_one.shape[1]
    m2 = spatial_two.shape[1]
    outward = shortcut.shape[1]
    sources = lax.axis_size("rows") * own // 52
    full_count = float(lax.axis_size("batch") * sources * 536)
    half_count = float(lax.axis_size("batch") * sources * 134)
    anchor = lax.axis_index("rows") * own
    cells, half = WIN * COLS, WIN * COLS // 4
    mine, more = own * COLS, SPILL * COLS

    pieces = gather_pieces(narrow_one)
    pack_a = [lanes_of(w, 4) for w in (spatial_one, expand_one)]
    chain_a = Chain(gather_steps(jnp.concatenate(pack_a, 1)))
    chain_n2 = Chain(gather_steps(narrow_two.reshape(4, -1, m2)))
    chain_e2 = Chain(gather_steps(expand_two.reshape(4, -1, outward)))
    spatial_b = gather_offloaded(spatial_two)
    bypass = gather_offloaded(shortcut)
    chain_f = [
        Chain(one_step(features[k, 0, :SPILL], lambda x: from_behind(x, -1))) for k in range(micro)
    ]
    g1, g2, g3 = (v[None] for v in jnp.split(gains_one, [m1, 2 * m1]))
    b1, b2, b3 = (v[None] for v in jnp.split(biases_one, [m1, 2 * m1]))
    cuts = [m2, 2 * m2, 2 * m2 + outward]
    g4, g5, g6, g7 = (v[None] for v in jnp.split(gains_two, cuts))
    b4, b5, b6, b7 = (v[None] for v in jnp.split(biases_two, cuts))
    mask, half_mask = pl.pallas_call(
        functools.partial(k_masks, own),
        in_specs=[pl.BlockSpec(memory_space=pltpu.SMEM)] * 2,
        out_shape=[
            jax.ShapeDtypeStruct((micro, cells, LANES), F32),
            jax.ShapeDtypeStruct((micro, half, LANES), F32),
        ],
        name="k_masks",
    )(anchor[None].astype(jnp.int32), view_kind)
    place = jnp.stack([lax.axis_index("rows"), my_bit(0)]).astype(jnp.int32)

    full_table = lambda c: ((8, c), F32, "t")
    per = lambda c, t=F32, n=cells: ((micro, n, c), t, "m")

    pre_one, head, t1, narrow_a = call(
        functools.partial(k_first, len(pieces)), micro,
        [(place, "s"), (features, "m"), (mask, "m")] + [(p, "w") for p in pieces],
        [per(m1, F32, mine), per(m1, BF, more), full_table(m1), ((channels, m1), BF, "t")],
        [((mine, channels), BF)],
    )
    chain_h = Chain(one_step(head, lambda x: from_behind(x, -1)))
    for _ in range(3):
        chain_a.launch(chain_a.ready[0])
        chain_a.land()
    t1 = global_sum(
        t1,
        c=dict(start=[chain_h, chain_a]),
        d=dict(finish=[chain_h, chain_a], start=[chain_a, chain_n2, chain_f[0]]),
    )
    pre_spill = chain_h.value()
    total_a = chain_a.value()
    spatial_a = total_a[:, : pack_a[0].shape[1]].reshape(-1, m1)
    expand_a = from_lanes(total_a[:, pack_a[0].shape[1] :], channels)
    flipped = spatial_a.reshape(9, m1, m1)[::-1].transpose(0, 2, 1).reshape(9 * m1, m1)
    pre_two, patch_one, t2 = call(
        functools.partial(k_second, full_count), micro,
        [(pre_one, "m"), (pre_spill, "m"), (t1, "w"), (g1, "w"), (b1, "w"), (mask, "m"),
         (spatial_a, "w")],
        [per(m1), per(9 * m1, BF), full_table(m1)],
        [((cells + 2 * COLS, m1), F32), ((cells + 2 * COLS, 3 * m1), BF)],
    )
    t2 = global_sum(
        t2,
        b=dict(finish=[chain_n2, chain_f[0]], start=[chain_n2]),
        c=dict(finish=[chain_n2], start=[chain_n2]),
        d=dict(finish=[chain_n2], start=[chain_n2, chain_e2, chain_f[1]]),
    )
    act_two, pre_three, t3 = call(
        functools.partial(k_third, full_count, MINE), micro,
        [(pre_two, "m"), (t2, "w"), (g2, "w"), (b2, "w"), (mask, "m"), (expand_a, "w")],
        [per(m1, BF), per(channels), full_table(channels)],
    )
    t3 = global_sum(
        t3,
        b=dict(finish=[chain_n2, chain_e2, chain_f[1]], start=[chain_n2, chain_e2]),
        c=dict(finish=[chain_n2, chain_e2], start=[chain_e2]),
        d=dict(finish=[chain_e2], start=[chain_e2] + chain_f[2:]),
    )
    narrow_b = chain_n2.value().reshape(-1, m2)
    (entry,) = call(
        k_entry, micro,
        [(features, "m"), (mask, "m")] + [(f.value(), "w") for f in chain_f],
        [per(channels, BF)], [((cells, channels), BF)],
    )
    block_out, corner, pre_four, t4 = call(
        functools.partial(k_fourth, full_count), micro,
        [(pre_three, "m"), (entry, "m"), (t3, "w"), (g3, "w"), (b3, "w"), (mask, "m"), (narrow_b, "w")],
        [per(channels, BF), per(channels, BF, half), per(m2), full_table(m2)],
        [((channels // LANES, 4 * COLS, LANES), F32)],
    )
    t4 = global_sum(t4, b=dict(finish=[chain_e2], start=[chain_e2]), c=dict(finish=[chain_e2]))
    expand_b = chain_e2.value().reshape(-1, outward)
    pre_five, patch_two, t5 = call(
        functools.partial(k_fifth, full_count), micro,
        [(pre_four, "m"), (t4, "w"), (g4, "w"), (b4, "w"), (mask, "m"), (half_mask, "m"),
         (spatial_b, "w")],
        [per(m2, F32, half), per(9 * m2, BF, half), full_table(m2)],
        [((m2 // LANES, cells, LANES), F32)] + [((half + COLS, m2), F32)] * 3,
    )
    t5 = global_sum(t5)
    act_five, pre_six, t6 = call(
        functools.partial(k_third, half_count, HALF), micro,
        [(pre_five, "m"), (t5, "w"), (g5, "w"), (b5, "w"), (half_mask, "m"), (expand_b, "w")],
        [per(m2, BF, half), per(outward, F32, half), full_table(outward)],
    )
    tile = outward // 4
    pre_seven, t7 = pl.pallas_call(
        k_seventh,
        grid=(4, micro),
        in_specs=[
            pl.BlockSpec((1, half, channels), lambda n, m: (m, 0, 0)),
            pl.BlockSpec((channels, tile), lambda n, m: (0, n)),
        ],
        out_specs=[
            pl.BlockSpec((1, half, tile), lambda n, m: (m, 0, n)),
            pl.BlockSpec((8, tile), lambda n, m: (0, n)),
        ],
        out_shape=[
            jax.ShapeDtypeStruct((micro, half, outward), F32),
            jax.ShapeDtypeStruct((8, outward), F32),
        ],
        compiler_params=pltpu.CompilerParams(vmem_limit_bytes=40 * 1024 * 1024),
    )(corner, bypass)
    t67 = global_sum(jnp.concatenate([t6, t7], 1))
    t6, t7 = t67[:, :outward], t67[:, outward:]
    outputs, slope, u67 = call(
        functools.partial(k_last, half_count), micro,
        [(pre_six, "m"), (pre_seven, "m"), (t6, "w"), (t7, "w"), (g6, "w"), (b6, "w"), (g7, "w"), (b7, "w"),
         (half_mask, "m"), (cotangent, "m")],
        [(cotangent.shape, BF, "m"), per(outward, F32, half), full_table(2 * outward)],
        [((COLS // 2, outward), F32)],
    )
    u67 = global_sum(u67)
    d_six, d_seven, d_five, u5 = call(
        functools.partial(k_back_six, half_count), micro,
        [(slope, "m"), (pre_six, "m"), (pre_seven, "m"), (t6, "w"), (t7, "w"), (u67, "w"), (g6, "w"), (g7, "w"),
         (pre_five, "m"), (t5, "w"), (g5, "w"), (b5, "w"), (half_mask, "m"), (expand_b, "w")],
        [per(outward, BF, half), per(outward, BF, half), per(m2, F32, half), full_table(m2)],
    )
    (d_corner,) = call(
        k_corner, micro, [(d_seven, "m"), (bypass, "w")], [per(channels, F32, half)]
    )
    grad_e2 = weight_term(act_five, d_six)
    grad_sc = weight_term(corner, d_seven)
    chain_re2 = Chain(reduce_steps([sharded(grad_e2, outward)], (0, 1, 2)))
    u5 = global_sum(u5, c=dict(need=[grad_sc, chain_re2.ready[0]]), d=dict(start=[chain_re2]))
    part_sc = lax.psum_scatter(grad_sc, AXES, scatter_dimension=0, tiled=True)
    d_pre_five, d_four, u4 = call(
        functools.partial(k_back_five, half_count, full_count), micro,
        [(d_five, "m"), (pre_five, "m"), (t5, "w"), (u5, "w"), (g5, "w"), (half_mask, "m"),
         (spatial_b, "w"), (pre_four, "m"), (t4, "w"), (g4, "w"), (b4, "w"), (mask, "m")],
        [per(m2, BF, half), per(m2), full_table(m2)],
        [((m2 // LANES, cells, LANES), F32), ((half + COLS, m2), F32)],
    )
    grad_s2 = sharded(weight_term(patch_two, d_pre_five), m2)
    cut = grad_s2.shape[1] // 32 * 16 or grad_s2.shape[1] // 2
    chain_rs = [
        Chain(reduce_steps([grad_s2[:, :cut]], (0, 2, 1))),
        Chain(reduce_steps([grad_s2[:, cut:]], (0, 1, 2))),
    ]
    u4 = global_sum(
        u4,
        b=dict(finish=[chain_re2]),
        c=dict(start=[chain_re2], need=[r.ready[0] for r in chain_rs]),
        d=dict(start=chain_rs),
    )
    d_pre_four, d_summed, u3 = call(
        functools.partial(k_back_four, full_count), micro,
        [(d_four, "m"), (pre_four, "m"), (t4, "w"), (u4, "w"), (g4, "w"), (mask, "m"), (narrow_b, "w"),
         (d_corner, "m"), (pre_three, "m"), (entry, "m"), (t3, "w"), (g3, "w"), (b3, "w")],
        [per(m2, BF), per(channels), full_table(channels)],
        [((channels // LANES, COLS, LANES), F32)],
    )
    grad_n2 = weight_term(block_out, d_pre_four)
    spilled = [d_summed[k, mine : mine + more].astype(BF) for k in range(micro)]
    chain_ds = [Chain(one_step(v, lambda x: from_behind(x, 1))) for v in spilled]
    u3 = global_sum(
        u3,
        b=dict(finish=[chain_re2] + chain_rs),
        c=dict(start=[chain_re2] + chain_rs, need=[grad_n2]),
        d=dict(finish=[chain_re2], start=[chain_re2, chain_ds[0]]),
    )
    d_pre_three, d_two, u2 = call(
        functools.partial(k_back_three, full_count), micro,
        [(d_summed, "m"), (pre_three, "m"), (t3, "w"), (u3, "w"), (g3, "w"), (mask, "m"), (expand_a, "w"),
         (pre_two, "m"), (t2, "w"), (g2, "w"), (b2, "w")],
        [per(channels, BF), per(m1), full_table(m1)],
    )
    grad_e1 = weight_term(act_two, d_pre_three)
    chain_rq = Chain(reduce_steps([sharded(grad_n2, 256), sharded(grad_e1, 256)], (0, 1, 2)))
    u2 = global_sum(
        u2,
        b=dict(finish=chain_rs + chain_ds[:1], start=[chain_rq]),
        c=dict(finish=[chain_re2, chain_rq], start=chain_rs),
        d=dict(finish=chain_rs, start=chain_rs + [chain_re2, chain_rq] + chain_ds[1:2]),
    )
    d_pre_two, d_one, u1 = call(
        functools.partial(k_back_two, full_count), micro,
        [(d_two, "m"), (pre_two, "m"), (t2, "w"), (u2, "w"), (g2, "w"), (mask, "m"),
         (flipped, "w"), (pre_one, "m"), (pre_spill, "m"), (t1, "w"), (g1, "w"), (b1, "w")],
        [per(m1, BF), per(m1), full_table(m1)],
        [((cells + 2 * COLS, m1), F32), ((cells + 2 * COLS, 3 * m1), BF)],
    )
    grad_s1 = weight_term(patch_one, d_pre_two)
    chain_r1 = Chain(reduce_steps([sharded(grad_s1, 256)], (0, 2, 1)))
    u1 = global_sum(
        u1,
        b=dict(finish=[chain_re2, chain_rq] + chain_ds[1:2], start=[chain_r1]),
        c=dict(finish=chain_rs + [chain_r1], start=[chain_re2, chain_rq]),
        d=dict(finish=[chain_re2, chain_rq], start=chain_rs + [chain_re2, chain_rq, chain_r1] + chain_ds[2:]),
    )
    (d_pre_one,) = call(
        functools.partial(k_back_one, full_count), micro,
        [(d_one, "m"), (pre_one, "m"), (pre_spill, "m"), (t1, "w"), (u1, "w"), (g1, "w"), (mask, "m")],
        [per(m1, BF)],
    )
    chain_dp = Chain(one_step(d_pre_one[:, mine : mine + more], lambda x: from_behind(x, 1)))
    grad_n1 = weight_term(entry, d_pre_one)
    chain_rn = Chain(reduce_steps([sharded(grad_n1, 256)], (0, 1, 2)))
    chain_rc = Chain(spread_steps(part_sc))
    out_n2, out_e1 = unpack(chain_rq.value(), [(channels, m2), (m1, channels)])
    (out_e2,) = unpack(chain_re2.value(), [(m2, outward)])
    (out_s2,) = unpack(jnp.concatenate([r.value() for r in chain_rs], 1), [(9 * m2, m2)])
    (out_s1,) = unpack(chain_r1.value(), [(9 * m1, m1)])
    (out_n1,) = unpack(chain_rn.value(), [(channels, m1)])
    (out_sc,) = unpack(chain_rc.value(), [(channels, outward)])
    (grad_input,) = call(
        k_input, micro,
        [(d_pre_one, "m"), (chain_dp.value(), "m"), (d_summed, "m"), (narrow_a, "w")]
        + [(c.value(), "w") for c in chain_ds],
        [(features.shape, F32, "m")],
        [((mine, m1), BF), ((mine, channels), F32)],
    )
    added = lambda k, us: jnp.concatenate([u[k] + u[k + 2] + u[k + 4] for u in us])
    first = (u1, u2, u3)
    later = (u4, u5, u67)
    return (
        outputs, grad_input, out_n1, out_s1, out_e1,
        added(1, first), added(0, first),
        out_n2, out_s2, out_e2, out_sc,
        added(1, later), added(0, later),
    )


def solution(mesh):
    wide = P(None, "batch", "rows", None, None)
    shard = P("rows", None)
    return jax.shard_map(
        shards,
        mesh=mesh,
        in_specs=(
            wide, P(None, "batch", None), shard, shard, shard, P(), P(),
            shard, shard, shard, shard, P(), P(), wide,
        ),
        out_specs=(
            wide, wide, shard, shard, shard, P(), P(),
            shard, shard, shard, shard, P(), P(),
        ),
        check_vma=False,
    )
```

```python
import functools

import jax
import jax.numpy as jnp
from jax import lax
from jax.experimental import pallas as pl
from jax.experimental.pallas import tpu as pltpu
from jax.sharding import PartitionSpec as P

SPILL = 12
WIN = 40
COLS = 16
EPS = 1e-05
AXES = ("rows", "batch")
BF = jnp.bfloat16
F32 = jnp.float32
CHUNK = 32
TANH_SCALE = 0.7978845608028654
TANH_CUBE = 0.044715


def gelu(x):
    t = jnp.tanh(x * (TANH_SCALE + TANH_SCALE * TANH_CUBE * (x * x)))
    return x * (0.5 + 0.5 * t)


def gelu_slope(x):
    square = x * x
    t = jnp.tanh(x * (TANH_SCALE + TANH_SCALE * TANH_CUBE * square))
    inner = x * (TANH_SCALE + 3.0 * TANH_SCALE * TANH_CUBE * square)
    return (0.5 + 0.5 * t) * (1.0 + inner * (1.0 - t))


def nn(a, b):
    return lax.dot_general(a, b, (((1,), (0,)), ((), ())), preferred_element_type=F32)


def nt(a, b):
    return lax.dot_general(a, b, (((1,), (1,)), ((), ())), preferred_element_type=F32)


def wide_of(ref):
    return ref[...].reshape(-1, ref.shape[-1])


def pick(ref, row, start=0, width=None):
    table = ref[:, start : start + (width or ref.shape[1])]
    rows = lax.broadcasted_iota(jnp.int32, table.shape, 0)
    return jnp.sum(jnp.where(rows == row, table, 0.0), axis=0, keepdims=True)


def moments(ref, m, population, start=0, width=None):
    share = 1.0 / population
    average = pick(ref, 2 * m, start, width) * share
    return average, lax.rsqrt(pick(ref, 2 * m + 1, start, width) * share - average * average + EPS)


def line(ref, m, population, gain, bias):
    average, inv = moments(ref, m, population)
    scale = inv * gain[...]
    return scale, bias[...] - average * scale


def back_line(ref, back, m, population, gain, start=0):
    average, inv = moments(ref, m, population)
    share = 1.0 / population
    width = ref.shape[1]
    mean_d = pick(back, 2 * m, start, width) * share
    mean_dn = pick(back, 2 * m + 1, start, width) * share
    by_d = gain[...] * inv
    by_p = -by_d * inv * mean_dn
    return by_d, by_p, -by_d * mean_d - by_p * average


def centred(ref, m, population, first, second):
    average, inv = moments(ref, m, population)
    first = jnp.sum(first, axis=0, keepdims=True)
    second = jnp.sum(second, axis=0, keepdims=True)
    return first, inv * (second - average * first)


def put_sums(ref, m, first, second, start=0):
    c = first.shape[1]
    at = slice(start, start + c)

    @pl.when(m == 0)
    def _():
        ref[:, at] = jnp.zeros((ref.shape[0], c), F32)

    first = jnp.sum(first, axis=0, keepdims=True)
    second = jnp.sum(second, axis=0, keepdims=True)
    rows = lax.broadcasted_iota(jnp.int32, (ref.shape[0], c), 0)
    ref[:, at] = jnp.where(rows == 2 * m, first, jnp.where(rows == 2 * m + 1, second, ref[:, at]))


def sweep(rows, c, vectors, body, sums=0, chunk=CHUNK, width=256):
    out = [[] for _ in range(sums)]
    for j in range(c // width):
        lanes = slice(j * width, (j + 1) * width)
        spread = [jnp.broadcast_to(v[:, lanes], (8, width))[None] for v in vectors]

        def step(i, carry):
            at = pl.ds(pl.multiple_of(i * chunk, chunk), chunk)
            return tuple(t + jnp.sum(v, axis=0) for t, v in zip(carry, body(at, lanes, spread) or ()))

        total = lax.fori_loop(0, rows // chunk, step, (jnp.zeros((8, width), F32),) * sums)
        for k in range(sums):
            out[k].append(total[k])
    return [jnp.concatenate(v, 1) for v in out]


def eight(x):
    return x.reshape(-1, 8, x.shape[-1])


def flat(x):
    return x.reshape(-1, x.shape[-1])


def get(ref, at, lanes):
    return eight(ref[0, at, lanes].astype(F32))


def get_mask(ref, at, lanes):
    m = eight(ref[0, at, :])
    times = (lanes.stop - lanes.start) // LANES
    return jnp.concatenate([m] * times, 2) if times > 1 else m


def put(ref, at, lanes, value):
    ref[0, at, lanes] = flat(value).astype(ref.dtype)


def count_up(ref, out_total, m, mask=None):
    def add(at, lanes, _):
        p = get(ref, at, lanes)
        q = p if mask is None else p * get_mask(mask, at, lanes)
        return q, q * p

    put_sums(out_total, m, *sweep(ref.shape[1], ref.shape[2], (), add, 2))


LANES = 128


def put_tall(ref, rows, value, first=0):
    for j in range(value.shape[1] // LANES):
        ref[first // LANES + j, rows, :] = value[:, j * LANES : (j + 1) * LANES]


def get_tall(ref, rows, lanes):
    return jnp.concatenate([ref[j, rows, :] for j in range(lanes.start // LANES, lanes.stop // LANES)], 1)


OWN, UPPER, LOWER, INNER = 0, 1, 2, 3


def lane(ref, which, rows):
    return ref[0, rows, which : which + 1]


def k_masks(own, anchor, kinds, mine_out, half_out, flags, inner):
    first = anchor[0]
    height_of = lambda m, v: 6 + 8 * kinds[m, 0, v]
    for m in range(flags.shape[0]):
        rows = flags.shape[1] // COLS
        row = first + lax.broadcasted_iota(jnp.int32, (rows, LANES), 0)

        def view(v, c):
            at, width, start, last = c
            height = height_of(m, v)
            inside = (row >= at) & (row < at + height)
            return (
                at + height,
                jnp.where(inside, height, width),
                jnp.where(inside, at, start),
                jnp.where(inside, at + height - 1, last),
            )

        zero = jnp.zeros((rows, LANES), jnp.int32)
        _, width, start, last = lax.fori_loop(0, kinds.shape[2], view, (jnp.int32(0), zero, zero, zero))
        owned = (start >= first) & (start < first + own) & (width > 0)
        mine = jnp.where(owned, width, 0)
        above = (start != row).astype(F32)
        below = (last != row).astype(F32)
        cells = lambda v, n: jnp.broadcast_to(v[:, None, :], (v.shape[0], n, LANES))
        shape = (rows, COLS, LANES)
        column = lax.broadcasted_iota(jnp.int32, shape, 1)
        lanes = lax.broadcasted_iota(jnp.int32, shape, 2)
        value = jnp.where(lanes == OWN, (column < cells(width, COLS)).astype(F32), 0.0)
        value = jnp.where(lanes == UPPER, cells(above, COLS), value)
        value = jnp.where(lanes == LOWER, cells(below, COLS), value)
        flags[m] = value.reshape(rows * COLS, LANES)
        mine_out[m] = (column < cells(mine, COLS)).astype(F32).reshape(rows * COLS, LANES)
        shape = (rows, COLS // 2, LANES)
        column = lax.broadcasted_iota(jnp.int32, shape, 1)
        even = lambda v: v.reshape(rows // 2, 2, COLS // 2, LANES)[:, 0].reshape(rows * COLS // 4, LANES)
        half_out[m] = even((2 * column < cells(mine, COLS // 2)).astype(F32))
        inner[m] = even(cells(above, COLS // 2))


def k_first(features, mask, weight, pre, head, total, rows):
    m = pl.program_id(0)
    own, across = features.shape[2], features.shape[3]

    @pl.when(m == 0)
    def _():
        rows[...] = jnp.zeros_like(rows)

    for r in range(own):
        rows[r * COLS : r * COLS + across, :] = features[0, 0, r]
    pre[0] = nn(rows[...] * lane(mask, OWN, slice(0, own * COLS)).astype(BF), weight[...])
    head[0] = pre[0, 0 : head.shape[1], :].astype(BF)

    count_up(pre, total, m)


def k_entry(features, mask, *refs):
    spills, (entry, rows) = refs[:-2], refs[-2:]
    m = pl.program_id(0)
    own, across = features.shape[2], features.shape[3]

    @pl.when(m == 0)
    def _():
        rows[...] = jnp.zeros_like(rows)

    for r in range(own):
        rows[r * COLS : r * COLS + across, :] = features[0, 0, r]
    for k, spill in enumerate(spills):

        @pl.when(m == k)
        def _():
            for r in range(spill.shape[0]):
                at = (own + r) * COLS
                rows[at : at + across, :] = spill[r]

    entry[0] = rows[...] * lane(mask, 0, slice(None)).astype(BF)


def join_pre_one(own, spill, pre, c):
    edge, more = own.shape[1], spill.shape[1]
    pre[0, 0:edge, :] = own[0]
    pre[0, edge : edge + more, :] = spill[0].astype(F32)
    pre[0, edge + more :, :] = jnp.zeros((pre.shape[1] - edge - more, c), F32)


def spread_trio(source, trio, cells):
    c = source.shape[1]
    trio[0:COLS, :] = jnp.zeros((COLS, 3 * c), BF)
    trio[COLS + cells : 2 * COLS + cells, :] = jnp.zeros((COLS, 3 * c), BF)
    for r in range(0, cells, CHUNK):
        for tap in range(3):
            part = source[COLS + r + tap - 1 : COLS + r + tap - 1 + CHUNK, :]
            trio[COLS + r : COLS + r + CHUNK, tap * c : (tap + 1) * c] = part.astype(BF)


def conv_rows(trio, flags, weight, cells):
    width = trio.shape[1]
    upper = lane(flags, UPPER, slice(None)).astype(BF)
    lower = lane(flags, LOWER, slice(None)).astype(BF)
    above = trio[0:cells, :] * upper
    here = trio[COLS : COLS + cells, :]
    below = trio[2 * COLS : 2 * COLS + cells, :] * lower
    total = (
        nn(above, weight[0:width, :])
        + nn(here, weight[width : 2 * width, :])
        + nn(below, weight[2 * width : 3 * width, :])
    )
    return total, (above, here, below)


def clear_ends(source, cells):
    c = source.shape[1]
    source[0:COLS, :] = jnp.zeros((COLS, c), F32)
    source[COLS + cells : 2 * COLS + cells, :] = jnp.zeros((COLS, c), F32)


def later(at, by):
    return pl.ds(pl.multiple_of(at.start + by, 8), at.size)


def k_second(count, own, spill, total, gain, bias, mask, flags, weight, pre, patch, out_total, act, trio, joined):
    m = pl.program_id(0)
    cells, c = mask.shape[1], own.shape[2]
    join_pre_one(own, spill, joined, c)
    clear_ends(act, cells)

    def step(at, lanes, v):
        x = get(joined, at, lanes) * v[0] + v[1]
        act[later(at, COLS), lanes] = flat(gelu(x) * get_mask(mask, at, lanes))

    sweep(cells, c, line(total, m, count, gain, bias), step)
    spread_trio(act, trio, cells)
    result, parts = conv_rows(trio, flags, weight, cells)
    pre[0] = result
    for k, part in enumerate(parts):
        patch[0, :, k * 3 * c : (k + 1) * 3 * c] = part
    count_up(pre, out_total, m, mask)


def k_third(count, pre_in, total, gain, bias, mask, weight, act, pre, out_total):
    m = pl.program_id(0)

    def step(at, lanes, v):
        x = get(pre_in, at, lanes) * v[0] + v[1]
        put(act, at, lanes, gelu(x) * get_mask(mask, at, lanes))

    sweep(pre_in.shape[1], pre_in.shape[2], line(total, m, count, gain, bias), step)
    pre[0] = nn(act[0], wide_of(weight)).astype(pre.dtype)
    count_up(pre, out_total, m)


def k_fourth(count, pre_in, entry, total, gain, bias, mask, weight, block, corner, pre, out_total, full):
    m = pl.program_id(0)
    wide = COLS // 2
    chunk = 4 * COLS

    def step(at, lanes, v):
        x = get(pre_in, at, lanes) * v[0] + v[1] + get(entry, at, lanes)
        y = gelu(x) * get_mask(mask, at, lanes)
        put(block, at, lanes, y)
        put_tall(full, slice(0, chunk), flat(y), lanes.start)
        pair = [get_tall(full, pl.ds(k * COLS, wide, stride=2), lanes) for k in (0, 2)]
        corner[0, pl.ds(pl.multiple_of(at.start // 4, COLS), COLS), lanes] = jnp.concatenate(pair, 0).astype(BF)

    sweep(pre_in.shape[1], pre_in.shape[2], line(total, m, count, gain, bias), step, chunk=chunk)
    pre[0] = nn(block[0], wide_of(weight)).astype(pre.dtype)
    count_up(pre, out_total, m)


def k_seventh(corner, weight, pre, out_total):
    pre[0] = nn(corner[0], wide_of(weight)).astype(pre.dtype)
    count_up(pre, out_total, pl.program_id(1))


def k_fifth(count, pre_in, total, gain, bias, mask, half_mask, inner, weight, pre, patch, out_total, act, eo, oe, oo):
    m = pl.program_id(0)
    cells, c = pre_in.shape[1], pre_in.shape[2]
    half = cells // 4
    wide = COLS // 2

    def step(at, lanes, v):
        x = get(pre_in, at, lanes) * v[0] + v[1]
        put_tall(act, at, flat(gelu(x) * get_mask(mask, at, lanes)), lanes.start)

    sweep(cells, c, line(total, m, count, gain, bias), step)
    pad = 2 * wide
    for buf in (eo, oe, oo):
        buf[0:pad, :] = jnp.zeros((pad, c), F32)
    for j in range(c // LANES):
        lanes = slice(j * LANES, (j + 1) * LANES)
        even = act[j, pl.ds(0, cells // 2, stride=2), :].reshape(half // wide, 2, wide, LANES)
        odd = act[j, pl.ds(1, cells // 2, stride=2), :].reshape(half // wide, 2, wide, LANES)
        patch[0, :, 4 * c + j * LANES : 4 * c + (j + 1) * LANES] = even[:, 0].reshape(half, LANES).astype(BF)
        oe[pad : pad + half, lanes] = even[:, 1].reshape(half, LANES)
        eo[pad : pad + half, lanes] = odd[:, 0].reshape(half, LANES)
        oo[pad : pad + half, lanes] = odd[:, 1].reshape(half, LANES)
    first = jnp.concatenate([inner[0]] * (c // LANES), 1)
    take = lambda buf, back: buf[pad - back : pad - back + half, :]
    taps = (
        take(oo, wide + 1) * first, take(oe, wide) * first, take(oo, wide) * first,
        take(eo, 1), None, take(eo, 0),
        take(oo, 1), take(oe, 0), take(oo, 0),
    )
    for k, tap in enumerate(taps):
        if tap is not None:
            patch[0, :, k * c : (k + 1) * c] = tap.astype(BF)
    pre[0] = nn(patch[0], wide_of(weight))
    count_up(pre, out_total, m, half_mask)


def k_last(count, six, seven, tot6, tot7, g6, b6, g7, b7, half_mask, cot, out, slope, total, row):
    m = pl.program_id(0)
    half, c = six.shape[1], six.shape[2]
    wide = COLS // 2
    shown, across = out.shape[2], out.shape[3]
    scale6, shift6 = line(tot6, m, count, g6, b6)
    scale7, shift7 = line(tot7, m, count, g7, b7)
    row[...] = jnp.zeros_like(row)

    def step(at, lanes, v):
        p = 2 * (at.start // (2 * wide))
        mask = get_mask(half_mask, at, lanes)
        s6, s7 = get(six, at, lanes), get(seven, at, lanes)
        joined = s6 * v[0] + s7 * v[1] + v[2]
        square = joined * joined
        t = jnp.tanh(joined * (TANH_SCALE + TANH_SCALE * TANH_CUBE * square))
        inside = joined * (TANH_SCALE + 3.0 * TANH_SCALE * TANH_CUBE * square)
        part = (0.5 + 0.5 * t) * mask
        result = flat(joined * part)
        for k in range(2):
            q = jnp.minimum(p + k, shown - 1)
            if shown % 2 == 0 or k == 0:
                out[0, 0, q, :, lanes] = result[k * wide : k * wide + across].astype(BF)
            else:

                @pl.when(p + k < shown)
                def _():
                    out[0, 0, q, :, lanes] = result[k * wide : k * wide + across].astype(BF)

            row[k * wide : k * wide + across, lanes] = cot[0, 0, q, :, lanes].astype(F32)
        d = part * (1.0 + inside * (1.0 - t)) * eight(row[:, lanes])
        put(slope, at, lanes, d)
        return d, d * s6, d * s7

    sums = sweep(half, c, (scale6, scale7, shift6 + shift7), step, 3, chunk=2 * wide, width=512)
    put_sums(total, m, *centred(tot6, m, count, sums[0], sums[1]))
    put_sums(total, m, *centred(tot7, m, count, sums[0], sums[2]), c)


def slope_sums(d_out, pre, tot, m, population, gain, bias, mask, out_total, more=None):
    def add(at, lanes, v):
        p = get(pre, at, lanes)
        d = gelu_slope(p * v[0] + v[1]) * get(d_out, at, lanes) * get_mask(mask, at, lanes)
        put(d_out, at, lanes, d)
        return d, d * p

    sums = sweep(pre.shape[1], pre.shape[2], line(tot, m, population, gain, bias), add, 2)
    put_sums(out_total, m, *centred(tot, m, population, *sums))


def norm_back(d_pre, d, pre, tot, back, m, population, gain, mask):
    def step(at, lanes, v):
        value = get(d, at, lanes) * v[0] + get(pre, at, lanes) * v[1] + v[2]
        put(d_pre, at, lanes, value * get_mask(mask, at, lanes))

    sweep(pre.shape[1], pre.shape[2], back_line(tot, back, m, population, gain), step)


def k_back_six(
    count, slope, six, seven, tot6, tot7, back, g6, g7, five, tot5, g5, b5, half_mask, weight,
    d_six, d_seven, d_five, out_total,
):
    m = pl.program_id(0)
    half, c = six.shape[1], six.shape[2]

    def step(at, lanes, v):
        d = get(slope, at, lanes)
        mask = get_mask(half_mask, at, lanes)
        put(d_six, at, lanes, (d * v[0] + get(six, at, lanes) * v[1] + v[2]) * mask)
        put(d_seven, at, lanes, (d * v[3] + get(seven, at, lanes) * v[4] + v[5]) * mask)

    vectors = back_line(tot6, back, m, count, g6) + back_line(tot7, back, m, count, g7, c)
    sweep(half, c, vectors, step)
    d_five[0] = nt(d_six[0], wide_of(weight))
    slope_sums(d_five, five, tot5, m, count, g5, b5, half_mask, out_total)


def k_corner(d_seven, weight, d_corner):
    d_corner[0] = nt(d_seven[0], wide_of(weight)).astype(d_corner.dtype)


def k_back_five(
    half_count, full_count, d_five, five, tot5, back5, g5, half_mask, inner, weight, four, tot4, g4, b4, mask,
    d_pre, d_four, out_total, grid_scratch, shifted,
):
    m = pl.program_id(0)
    half, c = five.shape[1], five.shape[2]
    cells = 4 * half
    wide = COLS // 2
    norm_back(d_pre, d_five, five, tot5, back5, m, half_count, g5, half_mask)
    d = d_pre[0]
    wide_d = d.astype(F32)
    tail = 2 * wide
    shifted[half : half + tail, :] = jnp.zeros((tail, c), F32)
    shifted[0:half, :] = wide_d
    right = shifted[1 : 1 + half, :].astype(BF)
    shifted[0:half, :] = wide_d * jnp.concatenate([inner[0]] * (c // LANES), 1)
    down = shifted[wide : wide + half, :].astype(BF)
    down_right = shifted[wide + 1 : wide + 1 + half, :].astype(BF)
    taps = wide_of(weight)
    w = lambda tap: taps[tap * c : (tap + 1) * c]
    ee = nt(d, w(4))
    eo = nt(d, w(5)) + nt(right, w(3))
    oe = nt(d, w(7)) + nt(down, w(1))
    oo = nt(d, w(8)) + nt(right, w(6)) + nt(down, w(2)) + nt(down_right, w(0))
    rows = half // wide
    even = jnp.stack([ee.reshape(rows, wide, c), oe.reshape(rows, wide, c)], 1).reshape(cells // 2, c)
    odd = jnp.stack([eo.reshape(rows, wide, c), oo.reshape(rows, wide, c)], 1).reshape(cells // 2, c)
    put_tall(grid_scratch, pl.ds(0, cells // 2, stride=2), even)
    put_tall(grid_scratch, pl.ds(1, cells // 2, stride=2), odd)

    def add(at, lanes, v):
        p = get(four, at, lanes)
        got = eight(get_tall(grid_scratch, at, lanes))
        d = gelu_slope(p * v[0] + v[1]) * got * get_mask(mask, at, lanes)
        put(d_four, at, lanes, d)
        return d, d * p

    sums = sweep(cells, c, line(tot4, m, full_count, g4, b4), add, 2)
    put_sums(out_total, m, *centred(tot4, m, full_count, *sums))


def k_back_four(
    count, d_four, four, tot4, back4, g4, mask, weight, d_corner, three, entry, tot3, g3, b3,
    d_pre, d_summed, out_total, placed, d_block,
):
    m = pl.program_id(0)
    cells, c = three.shape[1], three.shape[2]
    norm_back(d_pre, d_four, four, tot4, back4, m, count, g4, mask)
    d_block[0] = nt(d_pre[0], wide_of(weight))
    wide = COLS // 2
    placed[...] = jnp.zeros_like(placed)

    def add(at, lanes, v):
        corner_at = pl.ds(pl.multiple_of(at.start // 4, COLS), COLS)
        value = d_corner[0, corner_at, lanes].astype(F32)
        for k in range(2):
            rows = pl.ds(2 * k * COLS, wide, stride=2)
            put_tall(placed, rows, value[k * wide : (k + 1) * wide], lanes.start)
        got = get(d_block, at, lanes) + eight(get_tall(placed, slice(0, 4 * COLS), lanes))
        p = get(three, at, lanes)
        x = p * v[0] + v[1] + get(entry, at, lanes)
        d = gelu_slope(x) * got * get_mask(mask, at, lanes)
        put(d_summed, at, lanes, d)
        return d, d * p

    sums = sweep(cells, c, line(tot3, m, count, g3, b3), add, 2, chunk=4 * COLS)
    put_sums(out_total, m, *centred(tot3, m, count, *sums))


def k_back_three(count, d_summed, three, tot3, back3, g3, mask, weight, two, tot2, g2, b2, d_pre, d_two, out_total):
    m = pl.program_id(0)
    norm_back(d_pre, d_summed, three, tot3, back3, m, count, g3, mask)
    d_two[0] = nt(d_pre[0], wide_of(weight))
    slope_sums(d_two, two, tot2, m, count, g2, b2, mask, out_total)


def k_back_two(
    count, d_two, two, tot2, back2, g2, mask, flags, weight, own, spill, tot1, g1, b1,
    d_pre, d_one, out_total, source, trio, joined,
):
    m = pl.program_id(0)
    cells, c = two.shape[1], two.shape[2]
    clear_ends(source, cells)

    def step(at, lanes, v):
        value = get(d_two, at, lanes) * v[0] + get(two, at, lanes) * v[1] + v[2]
        value = value * get_mask(mask, at, lanes)
        put(d_pre, at, lanes, value)
        source[later(at, COLS), lanes] = flat(value)

    sweep(cells, c, back_line(tot2, back2, m, count, g2), step)
    spread_trio(source, trio, cells)
    upper = lane(flags, UPPER, slice(None)).astype(BF)
    lower = lane(flags, LOWER, slice(None)).astype(BF)
    shifted = (
        trio[0:cells, :] * upper,
        trio[COLS : COLS + cells, :],
        trio[2 * COLS : 2 * COLS + cells, :] * lower,
    )
    tap = lambda k: nt(shifted[k // 3][:, k % 3 * c : (k % 3 + 1) * c], weight[(8 - k) * c : (9 - k) * c, :])
    d_one[0] = sum((tap(k) for k in range(1, 9)), tap(0))
    join_pre_one(own, spill, joined, c)
    slope_sums(d_one, joined, tot1, m, count, g1, b1, mask, out_total)


def k_back_one(count, d_one, own, spill, tot1, back1, g1, mask, d_pre, joined):
    m = pl.program_id(0)
    join_pre_one(own, spill, joined, d_one.shape[2])
    norm_back(d_pre, d_one, joined, tot1, back1, m, count, g1, mask)


def k_input(d_pre, more_pre, d_summed, weight, *refs):
    more_summed, (out, both, sums) = refs[:-3], refs[-3:]
    m = pl.program_id(0)
    spilled, cells = more_pre.shape[1], both.shape[0]
    blocks = sums.shape[1] // LANES
    own = cells // COLS
    across = out.shape[1] // blocks // own
    both[...] = d_pre[0, 0:cells, :]
    both[0:spilled, :] = d_pre[0, 0:spilled, :] + more_pre[0]
    sums[...] = nt(both[...], weight[...])
    for r in range(own):
        at = r * COLS
        value = sums[at : at + COLS, :] + d_summed[0, at : at + COLS, :].astype(F32)
        if at < spilled:
            extra = more_summed[0][at : at + COLS, :].astype(F32)
            for k in range(1, len(more_summed)):
                extra = jnp.where(m == k, more_summed[k][at : at + COLS, :].astype(F32), extra)
            value = value + extra
        for j in range(blocks):
            rows = pl.ds(r * across * blocks + j, across, stride=blocks)
            out[0, rows, :] = value[:across, j * LANES : (j + 1) * LANES]


def exchange(x, mask):
    total = lax.axis_size("rows") * lax.axis_size("batch")
    return lax.ppermute(x, AXES, [(i, i ^ mask) for i in range(total)])


def from_behind(x, by):
    devices = lax.axis_size("rows")
    pairs = [(i, i + by) for i in range(devices) if 0 <= i + by < devices]
    return lax.ppermute(x, "rows", pairs)


class Chain:
    def __init__(self, steps):
        self.steps, self.flying, self.done, self.result = steps, None, False, None
        self.ready = next(steps)

    def launch(self, array):
        self.flying = self.ready[1](array)

    def land(self):
        try:
            self.ready = self.steps.send(self.flying)
        except StopIteration as end:
            self.done, self.result = True, end.value
        self.flying = None

    def value(self):
        while not self.done:
            if self.flying is None:
                self.launch(self.ready[0])
            self.land()
        return self.result


def hook(x, start=(), finish=(), need=()):
    if not (start or finish or need):
        return x
    landed = []
    for chain in finish:
        if not chain.done:
            landed.append(chain.flying)
            chain.land()
    live = [chain for chain in start if not chain.done]
    tied = lax.optimization_barrier((x, [c.ready[0] for c in live], landed, list(need)))
    for chain, array in zip(live, tied[1]):
        chain.launch(array)
    return tied[0]


def global_sum(x, b=None, c=None, d=None):
    bits = device_bits()
    split = x.shape[1] >= 2048
    if split:
        half = x.shape[1] // 2
        part = lambda bit: lax.dynamic_slice_in_dim(x, bit * half, half, 1)
        x = part(my_bit(0)) + exchange(part(1 - my_bit(0)), 1)
    else:
        x = x + exchange(x, 1)
    x = hook(x, **(b or {}))
    step = 1
    while step < bits:
        low = 1 << step
        if step + 1 < bits:
            p, q, r = exchange(x, low), exchange(x, 2 * low), exchange(x, 3 * low)
            x = (x + p) + (q + r)
        else:
            x = x + exchange(x, low)
        if step == 1:
            x = hook(x, **(c or {}))
        step += 2
    if split:
        other = exchange(x, 1)
        upper = my_bit(0) == 1
        x = jnp.concatenate([jnp.where(upper, other, x), jnp.where(upper, x, other)], 1)
    return hook(x, **(d or {}))


def device_bits():
    total = lax.axis_size("rows") * lax.axis_size("batch")
    return total.bit_length() - 1


def my_bit(bit):
    number = lax.axis_index("rows") * lax.axis_size("batch") + lax.axis_index("batch")
    return (number >> bit) & 1


def batch_bits():
    return lax.axis_size("batch").bit_length() - 1


def across(bit):
    return lambda x: exchange(x, 1 << bit)


def lanes_of(w, parts):
    x = w.reshape(parts, -1, w.shape[1] // 256, 256)
    return x.transpose(0, 2, 1, 3).reshape(parts, -1, 256)


def from_lanes(x, c):
    parts = x.shape[0]
    x = x.reshape(parts, c // 256, -1, 256)
    return x.transpose(0, 2, 1, 3).reshape(-1, c)


def ordered(mine, other, bit, axis):
    upper = my_bit(bit) == 1
    return jnp.stack([jnp.where(upper, other, mine), jnp.where(upper, mine, other)], axis)


def gather_steps(packed, parts):
    bits, low = device_bits(), batch_bits()
    number = my_bit(0) if parts == 1 else lax.axis_index("batch")
    x = lax.dynamic_index_in_dim(packed, number, 0, keepdims=False)
    for bit in list(reversed(range(low, bits))) + list(reversed(range(parts))):
        got = yield x, across(bit)
        x = ordered(x, got, bit, x.ndim - 2)
    return x.reshape((-1,) + x.shape[-2:])


def gather_offloaded(ws):
    quarters, wide = lax.axis_size("batch"), ws[0].shape[1]
    packed = jnp.concatenate([w.reshape(quarters, -1, wide) for w in ws], 1)
    part = lax.dynamic_index_in_dim(packed, lax.axis_index("batch"), 0, keepdims=False)
    whole = lax.all_gather(part, AXES, axis=0)
    out, at = [], 0
    for w in ws:
        n = w.shape[0] // quarters
        if n % 16 == 0 and at % n == 0:
            block = at // n
            spec = pl.BlockSpec(
                (whole.shape[0], n, wide), lambda m, k=block: (0, k, 0), pipeline_mode=pl.Buffered(1)
            )
            out.append((whole, spec))
        else:
            part = whole[:, at : at + n].reshape(-1, wide)
            out.append((part, pl.BlockSpec(part.shape, lambda m: (0, 0), pipeline_mode=pl.Buffered(1))))
        at += n
    return out


def sharded(grad, c):
    total = lax.axis_size("rows") * lax.axis_size("batch")
    if grad.shape[1] == c:
        return grad.reshape(total, -1, c)
    return lanes_of(grad, total)


def spread_steps(x):
    for bit in reversed(range(batch_bits())):
        got = yield x, across(bit)
        x = ordered(x, got, bit, x.ndim - 2)
    return x.reshape((-1,) + x.shape[-2:])


def reduce_steps(parts):
    bits = device_bits()
    x = jnp.concatenate(parts, 1) if len(parts) > 1 else parts[0]
    x = x.reshape((2,) * bits + x.shape[1:])
    left = list(reversed(range(bits)))
    got = None
    for bit in range(bits):
        axis = left.index(bit)
        left.remove(bit)
        half = lambda v, b: lax.dynamic_index_in_dim(v, b, axis, keepdims=False)
        keep, send = my_bit(bit), 1 - my_bit(bit)
        if got is None:
            x, give = half(x, keep), half(x, send)
        else:
            x, give = half(x, keep) + half(got, keep), half(x, send) + half(got, send)
        got = yield give, across(bit)
    return (yield from spread_steps(x + got))


def reduce_first(part):
    bits, low = device_bits(), batch_bits()
    x = part.reshape((2,) * bits + part.shape[1:])
    left = list(reversed(range(bits)))
    got = None
    for bit in [0] + list(range(low, bits - 1)):
        axis = left.index(bit)
        left.remove(bit)
        half = lambda v, b: lax.dynamic_index_in_dim(v, b, axis, keepdims=False)
        keep, send = my_bit(bit), 1 - my_bit(bit)
        if got is None:
            x, give = half(x, keep), half(x, send)
        else:
            x, give = half(x, keep) + half(got, keep), half(x, send) + half(got, send)
        got = yield give, across(bit)
    return x + got


def reduce_last(x):
    low, last = batch_bits(), device_bits() - 1
    bit = my_bit(last)
    half = lambda b: lax.dynamic_index_in_dim(x, b, 0, keepdims=False)
    got = yield half(1 - bit), across(last)
    x = half(bit) + got
    for b in range(1, low):
        got = yield x, across(b)
        x = x + got
    got = yield x, across(0)
    x = ordered(x, got, 0, x.ndim - 2)
    return x.reshape((-1,) + x.shape[-2:])


def one_step(x, send):
    return (yield x, send)


def unpack(shard, shapes):
    devices = lax.axis_size("rows")
    out, at = [], 0
    for k, c in shapes:
        n = k * c // devices // shard.shape[0] // shard.shape[2]
        part = shard[:, at : at + n]
        out.append((from_lanes(part, c) if shard.shape[2] != c else part.reshape(-1, c)).astype(F32))
        at += n
    return out


LIMIT = 26


def per_micro(shape):
    zeros = (0,) * (len(shape) - 1)
    return pl.BlockSpec((1,) + tuple(shape[1:]), lambda m: (m,) + zeros)


def whole(shape):
    zeros = (0,) * len(shape)
    return pl.BlockSpec(tuple(shape), lambda m: zeros, pipeline_mode=pl.Buffered(1))


def table(shape):
    zeros = (0,) * len(shape)
    return pl.BlockSpec(tuple(shape), lambda m: zeros)


def call(kernel, micro, ins, outs, scratch=(), limit=LIMIT, after=()):
    kind = {"m": per_micro, "w": whole, "s": lambda shape: pl.BlockSpec(memory_space=pltpu.SMEM)}
    in_specs = [k if isinstance(k, pl.BlockSpec) else kind[k](a.shape) for a, k in ins]
    in_specs += [pl.BlockSpec(memory_space=pl.ANY)] * len(after)
    out_specs = [per_micro(sh) if k == "m" else table(sh) for sh, _, k in outs]

    def run(*refs):
        kernel(*refs[: len(ins)], *refs[len(ins) + len(after) :])

    return pl.pallas_call(
        run,
        grid=(micro,),
        in_specs=in_specs,
        out_specs=out_specs,
        out_shape=[jax.ShapeDtypeStruct(sh, t) for sh, t, _ in outs],
        scratch_shapes=[pltpu.VMEM(sh, t) for sh, t in scratch],
        compiler_params=pltpu.CompilerParams(
            dimension_semantics=("arbitrary",), vmem_limit_bytes=limit * 1024 * 1024
        ),
        name=getattr(kernel, "func", kernel).__name__,
    )(*[a for a, _ in ins], *after)


def weight_term(left, right):
    k, n = left.shape[-1], right.shape[-1]
    return lax.dot_general(
        left.reshape(-1, k), right.reshape(-1, n), (((0,), (0,)), ((), ())), preferred_element_type=F32
    ).astype(BF)


def shards(
    features, view_kind, narrow_one, spatial_one, expand_one, gains_one, biases_one,
    narrow_two, spatial_two, expand_two, shortcut, gains_two, biases_two, cotangent,
):
    micro, _, own, across, channels = features.shape
    m1 = spatial_one.shape[1]
    m2 = spatial_two.shape[1]
    outward = shortcut.shape[1]
    sources = lax.axis_size("rows") * own // 52
    full_count = float(lax.axis_size("batch") * sources * 536)
    half_count = float(lax.axis_size("batch") * sources * 134)
    anchor = lax.axis_index("rows") * own
    cells, half = WIN * COLS, WIN * COLS // 4
    mine, more = own * COLS, SPILL * COLS

    chain_n1 = Chain(gather_steps(narrow_one.reshape(2, -1, m1), 1))
    pack_a = [lanes_of(w, 4) for w in (spatial_one, expand_one)]
    chain_a = Chain(gather_steps(jnp.concatenate(pack_a, 1), 2))
    spatial_b, narrow_b = gather_offloaded([spatial_two, narrow_two])
    bypass, expand_b = gather_offloaded([shortcut, expand_two])
    chain_f = [
        Chain(one_step(features[k, 0, :SPILL], lambda x: from_behind(x, -1))) for k in range(micro)
    ]
    g1, g2, g3 = (v[None] for v in jnp.split(gains_one, [m1, 2 * m1]))
    b1, b2, b3 = (v[None] for v in jnp.split(biases_one, [m1, 2 * m1]))
    cuts = [m2, 2 * m2, 2 * m2 + outward]
    g4, g5, g6, g7 = (v[None] for v in jnp.split(gains_two, cuts))
    b4, b5, b6, b7 = (v[None] for v in jnp.split(biases_two, cuts))
    mask, half_mask, flags, inner = pl.pallas_call(
        functools.partial(k_masks, own),
        in_specs=[pl.BlockSpec(memory_space=pltpu.SMEM)] * 2,
        out_shape=[
            jax.ShapeDtypeStruct((micro, cells, LANES), F32),
            jax.ShapeDtypeStruct((micro, half, LANES), F32),
        ]
        * 2,
        name="k_masks",
    )(anchor[None].astype(jnp.int32), view_kind)

    full_table = lambda c: ((8, c), F32, "t")
    per = lambda c, t=F32, n=cells: ((micro, n, c), t, "m")

    for chain in (chain_n1, chain_a):
        chain.launch(chain.ready[0])
    chain_n1.land()
    before = [mask]
    while not chain_n1.done:
        chain_n1.launch(lax.optimization_barrier((chain_n1.ready[0], before))[0])
        landed = chain_n1.flying
        chain_n1.land()
        if chain_a.flying is not None and len(before) < 3 and not chain_n1.done:
            chain_a.land()
            chain_a.launch(lax.optimization_barrier((chain_a.ready[0], landed))[0])
            before = before + [landed]
            if len(before) == 3:
                hook(landed, start=chain_f[2:])
    narrow_a = chain_n1.value().reshape(-1, m1)
    pre_one, head, t1 = call(
        k_first, micro, [(features, "m"), (flags, "m"), (narrow_a, "w")],
        [per(m1, F32, mine), per(m1, BF, more), full_table(m1)], [((mine, channels), BF)],
    )
    chain_h = Chain(one_step(head, lambda x: from_behind(x, -1)))
    t1 = global_sum(
        t1,
        b=dict(finish=[chain_a]),
        c=dict(start=[chain_a, chain_h]),
        d=dict(finish=[chain_a, chain_h], start=[chain_a] + chain_f[:1]),
    )
    pre_spill = chain_h.value()
    total_a = chain_a.value()
    spatial_a = total_a[:, : pack_a[0].shape[1]].reshape(-1, m1)
    expand_a = from_lanes(total_a[:, pack_a[0].shape[1] :], channels)
    pre_two, patch_one, t2 = call(
        functools.partial(k_second, full_count), micro,
        [(pre_one, "m"), (pre_spill, "m"), (t1, "w"), (g1, "w"), (b1, "w"), (mask, "m"),
         (flags, "m"), (spatial_a, "w")],
        [per(m1), per(9 * m1, BF), full_table(m1)],
        [((cells + 2 * COLS, m1), F32), ((cells + 2 * COLS, 3 * m1), BF), ((1, cells, m1), F32)],
    )
    t2 = global_sum(t2, b=dict(finish=chain_f[:1]), d=dict(start=chain_f[1:2]))
    act_two, pre_three, t3 = call(
        functools.partial(k_third, full_count), micro,
        [(pre_two, "m"), (t2, "w"), (g2, "w"), (b2, "w"), (mask, "m"), (expand_a, "w")],
        [per(m1, BF), per(channels, BF), full_table(channels)],
    )
    t3 = global_sum(t3, b=dict(finish=chain_f[1:]))
    (entry,) = call(
        k_entry, micro,
        [(features, "m"), (mask, "m")] + [(f.value(), "w") for f in chain_f],
        [per(channels, BF)], [((cells, channels), BF)],
    )
    block_out, corner, pre_four, t4 = call(
        functools.partial(k_fourth, full_count), micro,
        [(pre_three, "m"), (entry, "m"), (t3, "w"), (g3, "w"), (b3, "w"), (mask, "m"), narrow_b],
        [per(channels, BF), per(channels, BF, half), per(m2, BF), full_table(m2)],
        [((channels // LANES, 4 * COLS, LANES), F32)],
    )
    t4 = global_sum(t4)
    pre_five, patch_two, t5 = call(
        functools.partial(k_fifth, full_count), micro,
        [(pre_four, "m"), (t4, "w"), (g4, "w"), (b4, "w"), (mask, "m"), (half_mask, "m"), (inner, "m"),
         spatial_b],
        [per(m2, F32, half), per(9 * m2, BF, half), full_table(m2)],
        [((m2 // LANES, cells, LANES), F32)] + [((half + COLS, m2), F32)] * 3,
    )
    t5 = global_sum(t5)
    act_five, pre_six, t6 = call(
        functools.partial(k_third, half_count), micro,
        [(pre_five, "m"), (t5, "w"), (g5, "w"), (b5, "w"), (half_mask, "m"), expand_b],
        [per(m2, BF, half), per(outward, BF, half), full_table(outward)],
    )
    tile = outward // 4
    by_tile = bypass[1].block_shape[:-1] + (tile,)
    pre_seven, t7 = pl.pallas_call(
        k_seventh,
        grid=(4, micro),
        in_specs=[
            pl.BlockSpec((1, half, channels), lambda n, m: (m, 0, 0)),
            pl.BlockSpec(by_tile, lambda n, m: (0,) * (len(by_tile) - 1) + (n,)),
        ],
        out_specs=[
            pl.BlockSpec((1, half, tile), lambda n, m: (m, 0, n)),
            pl.BlockSpec((8, tile), lambda n, m: (0, n)),
        ],
        out_shape=[
            jax.ShapeDtypeStruct((micro, half, outward), BF),
            jax.ShapeDtypeStruct((8, outward), F32),
        ],
        compiler_params=pltpu.CompilerParams(vmem_limit_bytes=LIMIT * 1024 * 1024),
    )(corner, bypass[0])
    t67 = global_sum(jnp.concatenate([t6, t7], 1))
    t6, t7 = t67[:, :outward], t67[:, outward:]
    outputs, slope, u67 = call(
        functools.partial(k_last, half_count), micro,
        [(pre_six, "m"), (pre_seven, "m"), (t6, "w"), (t7, "w"), (g6, "w"), (b6, "w"), (g7, "w"), (b7, "w"),
         (half_mask, "m"), (cotangent, "m")],
        [(cotangent.shape, BF, "m"), per(outward, BF, half), full_table(2 * outward)],
        [((COLS, outward), F32)],
    )
    u67 = global_sum(u67)
    d_six, d_seven, d_five, u5 = call(
        functools.partial(k_back_six, half_count), micro,
        [(slope, "m"), (pre_six, "m"), (pre_seven, "m"), (t6, "w"), (t7, "w"), (u67, "w"), (g6, "w"), (g7, "w"),
         (pre_five, "m"), (t5, "w"), (g5, "w"), (b5, "w"), (half_mask, "m"), expand_b],
        [per(outward, BF, half), per(outward, BF, half), per(m2, F32, half), full_table(m2)],
    )
    (d_corner,) = call(
        k_corner, micro, [(d_seven, "m"), bypass], [per(channels, BF, half)]
    )
    grad_e2 = weight_term(act_five, d_six)
    grad_sc = weight_term(corner, d_seven)
    pack_b = jnp.concatenate([sharded(grad_sc, outward), sharded(grad_e2, outward)], 1).reshape(-1, outward)
    u5 = global_sum(u5, c=dict(need=[pack_b]))
    part_b = lax.psum_scatter(pack_b, AXES, scatter_dimension=0, tiled=True)
    d_pre_five, d_four, u4 = call(
        functools.partial(k_back_five, half_count, full_count), micro,
        [(d_five, "m"), (pre_five, "m"), (t5, "w"), (u5, "w"), (g5, "w"), (half_mask, "m"), (inner, "m"),
         spatial_b, (pre_four, "m"), (t4, "w"), (g4, "w"), (b4, "w"), (mask, "m")],
        [per(m2, BF, half), per(m2), full_table(m2)],
        [((m2 // LANES, cells, LANES), F32), ((half + COLS, m2), F32)],
    )
    chain_rs = Chain(reduce_steps([sharded(weight_term(patch_two, d_pre_five), m2)]))
    u4 = global_sum(u4, b=dict(start=[chain_rs]), c=dict(finish=[chain_rs], start=[chain_rs]))
    d_pre_four, d_summed, u3 = call(
        functools.partial(k_back_four, full_count), micro,
        [(d_four, "m"), (pre_four, "m"), (t4, "w"), (u4, "w"), (g4, "w"), (mask, "m"), narrow_b,
         (d_corner, "m"), (pre_three, "m"), (entry, "m"), (t3, "w"), (g3, "w"), (b3, "w")],
        [per(m2, BF), per(channels, BF), full_table(channels)],
        [((channels // LANES, 4 * COLS, LANES), F32), ((1, cells, channels), F32)],
    )
    grad_n2 = [
        sharded(weight_term(block_out, d_pre_four[..., k : k + 256]), 256) for k in range(0, m2, 256)
    ]
    spilled = d_summed[:, mine : mine + more]
    chain_ds = [Chain(one_step(spilled[k], lambda x: from_behind(x, 1))) for k in range(micro)]
    chain_r2 = Chain(reduce_first(jnp.concatenate(grad_n2, 1)))
    u3 = global_sum(
        u3,
        b=dict(finish=[chain_rs], start=[chain_r2]),
        c=dict(finish=[chain_r2], start=[chain_rs, chain_r2]),
        d=dict(finish=[chain_r2], start=[chain_r2, chain_ds[0]]),
    )
    d_pre_three, d_two, u2 = call(
        functools.partial(k_back_three, full_count), micro,
        [(d_summed, "m"), (pre_three, "m"), (t3, "w"), (u3, "w"), (g3, "w"), (mask, "m"), (expand_a, "w"),
         (pre_two, "m"), (t2, "w"), (g2, "w"), (b2, "w")],
        [per(channels, BF), per(m1), full_table(m1)],
    )
    grad_e1 = weight_term(act_two, d_pre_three)
    chain_r3 = Chain(reduce_first(sharded(grad_e1, 256)))
    u2 = global_sum(
        u2,
        b=dict(finish=[chain_rs, chain_r2, chain_ds[0]], start=[chain_r3]),
        c=dict(finish=[chain_r3], start=[chain_r3]),
        d=dict(finish=[chain_r3], start=[chain_rs, chain_r3] + chain_ds[1:2]),
    )
    d_pre_two, d_one, u1 = call(
        functools.partial(k_back_two, full_count), micro,
        [(d_two, "m"), (pre_two, "m"), (t2, "w"), (u2, "w"), (g2, "w"), (mask, "m"), (flags, "m"),
         (spatial_a, "w"), (pre_one, "m"), (pre_spill, "m"), (t1, "w"), (g1, "w"), (b1, "w")],
        [per(m1, BF), per(m1), full_table(m1)],
        [((cells + 2 * COLS, m1), F32), ((cells + 2 * COLS, 3 * m1), BF), ((1, cells, m1), F32)],
    )
    grad_s1 = weight_term(patch_one, d_pre_two)
    chain_r1 = Chain(reduce_first(sharded(grad_s1, 256)))
    u1 = global_sum(
        u1,
        b=dict(finish=[chain_r3] + chain_ds[1:2], start=[chain_r1]),
        c=dict(finish=[chain_r1, chain_rs], start=[chain_r1]),
        d=dict(finish=[chain_r1], start=[chain_r1, chain_rs]),
    )
    (d_pre_one,) = call(
        functools.partial(k_back_one, full_count), micro,
        [(d_one, "m"), (pre_one, "m"), (pre_spill, "m"), (t1, "w"), (u1, "w"), (g1, "w"), (mask, "m")],
        [per(m1, BF)], [((1, cells, m1), F32)],
    )
    chain_rn = Chain(reduce_first(sharded(weight_term(entry, d_pre_one), 256)))
    firsts = [c.value() for c in (chain_rn, chain_r1, chain_r2, chain_r3)]
    chain_last = Chain(reduce_last(jnp.concatenate(firsts, -2)))
    d_more = lax.optimization_barrier((d_pre_one[:, mine : mine + more], firsts[0]))[0]
    chain_dp = Chain(one_step(d_more, lambda x: from_behind(x, 1)))
    out_n1, out_s1, out_n2, out_e1 = unpack(
        chain_last.value(), [(channels, m1), (9 * m1, m1), (channels, m2), (m1, channels)]
    )
    (out_s2,) = unpack(chain_rs.value(), [(9 * m2, m2)])
    out_sc, out_e2 = unpack(Chain(spread_steps(part_b)).value(), [(channels, outward), (m2, outward)])
    (grad_input,) = call(
        k_input, micro,
        [(d_pre_one, "m"), (chain_dp.value(), "m"), (d_summed, "m"), (narrow_a, "w")]
        + [(c.value(), "w") for c in chain_ds],
        [((micro, own * across * channels // LANES, LANES), F32, "m")],
        [((mine, m1), BF), ((mine, channels), F32)],
    )
    grad_input = grad_input.reshape(features.shape)
    added = lambda k, us: jnp.concatenate([u[k] + u[k + 2] + u[k + 4] for u in us])
    first = (u1, u2, u3)
    later = (u4, u5, u67)
    return (
        outputs, grad_input, out_n1, out_s1, out_e1,
        added(1, first), added(0, first),
        out_n2, out_s2, out_e2, out_sc,
        added(1, later), added(0, later),
    )


def solution(mesh):
    wide = P(None, "batch", "rows", None, None)
    shard = P("rows", None)
    return jax.shard_map(
        shards,
        mesh=mesh,
        in_specs=(
            wide, P(None, "batch", None), shard, shard, shard, P(), P(),
            shard, shard, shard, shard, P(), P(), wide,
        ),
        out_specs=(
            wide, wide, shard, shard, shard, P(), P(),
            shard, shard, shard, shard, P(), P(),
        ),
        check_vma=False,
    )
```

```python
import functools

import jax
import jax.numpy as jnp
from jax import lax
from jax.experimental import pallas as pl
from jax.experimental.pallas import tpu as pltpu
from jax.sharding import PartitionSpec as P

SPILL = 12
WIN = 40
COLS = 16
EPS = 1e-05
AXES = ("rows", "batch")
BF = jnp.bfloat16
F32 = jnp.float32
CHUNK = 32
TANH_SCALE = 0.7978845608028654
TANH_CUBE = 0.044715


def gelu(x):
    t = jnp.tanh(x * (TANH_SCALE + TANH_SCALE * TANH_CUBE * (x * x)))
    return x * (0.5 + 0.5 * t)


def gelu_slope(x):
    square = x * x
    t = jnp.tanh(x * (TANH_SCALE + TANH_SCALE * TANH_CUBE * square))
    inner = x * (TANH_SCALE + 3.0 * TANH_SCALE * TANH_CUBE * square)
    return (0.5 + 0.5 * t) * (1.0 + inner * (1.0 - t))


def nn(a, b):
    return lax.dot_general(a, b, (((1,), (0,)), ((), ())), preferred_element_type=F32)


def nt(a, b):
    return lax.dot_general(a, b, (((1,), (1,)), ((), ())), preferred_element_type=F32)


def wide_of(ref):
    return ref[...].reshape(-1, ref.shape[-1])


def pick(ref, row, start=0, width=None):
    table = ref[:, start : start + (width or ref.shape[1])]
    rows = lax.broadcasted_iota(jnp.int32, table.shape, 0)
    return jnp.sum(jnp.where(rows == row, table, 0.0), axis=0, keepdims=True)


def moments(ref, m, population, start=0, width=None):
    share = 1.0 / population
    average = pick(ref, 2 * m, start, width) * share
    return average, lax.rsqrt(pick(ref, 2 * m + 1, start, width) * share - average * average + EPS)


def line(ref, m, population, gain, bias):
    average, inv = moments(ref, m, population)
    scale = inv * gain[...]
    return scale, bias[...] - average * scale


def back_line(ref, back, m, population, gain, start=0):
    average, inv = moments(ref, m, population)
    share = 1.0 / population
    width = ref.shape[1]
    mean_d = pick(back, 2 * m, start, width) * share
    mean_dn = pick(back, 2 * m + 1, start, width) * share
    by_d = gain[...] * inv
    by_p = -by_d * inv * mean_dn
    return by_d, by_p, -by_d * mean_d - by_p * average


def centred(ref, m, population, first, second):
    average, inv = moments(ref, m, population)
    first = jnp.sum(first, axis=0, keepdims=True)
    second = jnp.sum(second, axis=0, keepdims=True)
    return first, inv * (second - average * first)


def put_sums(ref, m, first, second, start=0):
    c = first.shape[1]
    at = slice(start, start + c)

    @pl.when(m == 0)
    def _():
        ref[:, at] = jnp.zeros((ref.shape[0], c), F32)

    first = jnp.sum(first, axis=0, keepdims=True)
    second = jnp.sum(second, axis=0, keepdims=True)
    rows = lax.broadcasted_iota(jnp.int32, (ref.shape[0], c), 0)
    ref[:, at] = jnp.where(rows == 2 * m, first, jnp.where(rows == 2 * m + 1, second, ref[:, at]))


def sweep(rows, c, vectors, body, sums=0, chunk=CHUNK, width=256):
    out = [[] for _ in range(sums)]
    for j in range(c // width):
        lanes = slice(j * width, (j + 1) * width)
        spread = [jnp.broadcast_to(v[:, lanes], (8, width))[None] for v in vectors]

        def step(i, carry):
            at = pl.ds(pl.multiple_of(i * chunk, chunk), chunk)
            return tuple(t + jnp.sum(v, axis=0) for t, v in zip(carry, body(at, lanes, spread) or ()))

        total = lax.fori_loop(0, rows // chunk, step, (jnp.zeros((8, width), F32),) * sums)
        for k in range(sums):
            out[k].append(total[k])
    return [jnp.concatenate(v, 1) for v in out]


def eight(x):
    return x.reshape(-1, 8, x.shape[-1])


def flat(x):
    return x.reshape(-1, x.shape[-1])


def get(ref, at, lanes):
    return eight(ref[0, at, lanes].astype(F32))


def get_mask(ref, at, lanes):
    m = eight(ref[0, at, :])
    times = (lanes.stop - lanes.start) // LANES
    return jnp.concatenate([m] * times, 2) if times > 1 else m


def put(ref, at, lanes, value):
    ref[0, at, lanes] = flat(value).astype(ref.dtype)


def count_up(ref, out_total, m, mask=None):
    def add(at, lanes, _):
        p = get(ref, at, lanes)
        q = p if mask is None else p * get_mask(mask, at, lanes)
        return q, q * p

    put_sums(out_total, m, *sweep(ref.shape[1], ref.shape[2], (), add, 2))


LANES = 128


def put_tall(ref, rows, value, first=0):
    for j in range(value.shape[1] // LANES):
        ref[first // LANES + j, rows, :] = value[:, j * LANES : (j + 1) * LANES]


def get_tall(ref, rows, lanes):
    return jnp.concatenate([ref[j, rows, :] for j in range(lanes.start // LANES, lanes.stop // LANES)], 1)


OWN, UPPER, LOWER, INNER = 0, 1, 2, 3


def lane(ref, which, rows):
    return ref[0, rows, which : which + 1]


def k_masks(own, anchor, kinds, mine_out, half_out, flags, inner):
    first = anchor[0]
    height_of = lambda m, v: 6 + 8 * kinds[m, 0, v]
    for m in range(flags.shape[0]):
        rows = flags.shape[1] // COLS
        row = first + lax.broadcasted_iota(jnp.int32, (rows, LANES), 0)

        def view(v, c):
            at, width, start, last = c
            height = height_of(m, v)
            inside = (row >= at) & (row < at + height)
            return (
                at + height,
                jnp.where(inside, height, width),
                jnp.where(inside, at, start),
                jnp.where(inside, at + height - 1, last),
            )

        zero = jnp.zeros((rows, LANES), jnp.int32)
        _, width, start, last = lax.fori_loop(0, kinds.shape[2], view, (jnp.int32(0), zero, zero, zero))
        owned = (start >= first) & (start < first + own) & (width > 0)
        mine = jnp.where(owned, width, 0)
        above = (start != row).astype(F32)
        below = (last != row).astype(F32)
        cells = lambda v, n: jnp.broadcast_to(v[:, None, :], (v.shape[0], n, LANES))
        shape = (rows, COLS, LANES)
        column = lax.broadcasted_iota(jnp.int32, shape, 1)
        lanes = lax.broadcasted_iota(jnp.int32, shape, 2)
        value = jnp.where(lanes == OWN, (column < cells(width, COLS)).astype(F32), 0.0)
        value = jnp.where(lanes == UPPER, cells(above, COLS), value)
        value = jnp.where(lanes == LOWER, cells(below, COLS), value)
        flags[m] = value.reshape(rows * COLS, LANES)
        mine_out[m] = (column < cells(mine, COLS)).astype(F32).reshape(rows * COLS, LANES)
        shape = (rows, COLS // 2, LANES)
        column = lax.broadcasted_iota(jnp.int32, shape, 1)
        even = lambda v: v.reshape(rows // 2, 2, COLS // 2, LANES)[:, 0].reshape(rows * COLS // 4, LANES)
        half_out[m] = even((2 * column < cells(mine, COLS // 2)).astype(F32))
        inner[m] = even(cells(above, COLS // 2))


def k_first(features, mask, weight, pre, head, total, rows):
    m = pl.program_id(0)
    own, across = features.shape[2], features.shape[3]

    @pl.when(m == 0)
    def _():
        rows[...] = jnp.zeros_like(rows)

    for r in range(own):
        rows[r * COLS : r * COLS + across, :] = features[0, 0, r]
    pre[0] = nn(rows[...] * lane(mask, OWN, slice(0, own * COLS)).astype(BF), weight[...])
    head[0] = pre[0, 0 : head.shape[1], :].astype(BF)

    count_up(pre, total, m)


def k_entry(features, mask, *refs):
    spills, (entry, rows) = refs[:-2], refs[-2:]
    m = pl.program_id(0)
    own, across = features.shape[2], features.shape[3]

    @pl.when(m == 0)
    def _():
        rows[...] = jnp.zeros_like(rows)

    for r in range(own):
        rows[r * COLS : r * COLS + across, :] = features[0, 0, r]
    for k, spill in enumerate(spills):

        @pl.when(m == k)
        def _():
            for r in range(spill.shape[0]):
                at = (own + r) * COLS
                rows[at : at + across, :] = spill[r]

    entry[0] = rows[...] * lane(mask, 0, slice(None)).astype(BF)


def join_pre_one(own, spill, pre, c):
    edge, more = own.shape[1], spill.shape[1]
    pre[0, 0:edge, :] = own[0]
    pre[0, edge : edge + more, :] = spill[0].astype(F32)
    pre[0, edge + more :, :] = jnp.zeros((pre.shape[1] - edge - more, c), F32)


def spread_trio(source, trio, cells):
    c = source.shape[1]
    trio[0:COLS, :] = jnp.zeros((COLS, 3 * c), BF)
    trio[COLS + cells : 2 * COLS + cells, :] = jnp.zeros((COLS, 3 * c), BF)
    for r in range(0, cells, CHUNK):
        for tap in range(3):
            part = source[COLS + r + tap - 1 : COLS + r + tap - 1 + CHUNK, :]
            trio[COLS + r : COLS + r + CHUNK, tap * c : (tap + 1) * c] = part.astype(BF)


def conv_rows(trio, flags, weight, cells):
    width = trio.shape[1]
    upper = lane(flags, UPPER, slice(None)).astype(BF)
    lower = lane(flags, LOWER, slice(None)).astype(BF)
    above = trio[0:cells, :] * upper
    here = trio[COLS : COLS + cells, :]
    below = trio[2 * COLS : 2 * COLS + cells, :] * lower
    total = (
        nn(above, weight[0:width, :])
        + nn(here, weight[width : 2 * width, :])
        + nn(below, weight[2 * width : 3 * width, :])
    )
    return total, (above, here, below)


def clear_ends(source, cells):
    c = source.shape[1]
    source[0:COLS, :] = jnp.zeros((COLS, c), F32)
    source[COLS + cells : 2 * COLS + cells, :] = jnp.zeros((COLS, c), F32)


def later(at, by):
    return pl.ds(pl.multiple_of(at.start + by, 8), at.size)


def k_second(count, own, spill, total, gain, bias, mask, flags, weight, pre, patch, out_total, act, trio, joined):
    m = pl.program_id(0)
    cells, c = mask.shape[1], own.shape[2]
    join_pre_one(own, spill, joined, c)
    clear_ends(act, cells)

    def step(at, lanes, v):
        x = get(joined, at, lanes) * v[0] + v[1]
        act[later(at, COLS), lanes] = flat(gelu(x) * get_mask(mask, at, lanes))

    sweep(cells, c, line(total, m, count, gain, bias), step)
    spread_trio(act, trio, cells)
    result, parts = conv_rows(trio, flags, weight, cells)
    pre[0] = result
    for k, part in enumerate(parts):
        patch[0, :, k * 3 * c : (k + 1) * 3 * c] = part
    count_up(pre, out_total, m, mask)


def k_third(count, pre_in, total, gain, bias, mask, weight, act, pre, out_total):
    m = pl.program_id(0)

    def step(at, lanes, v):
        x = get(pre_in, at, lanes) * v[0] + v[1]
        put(act, at, lanes, gelu(x) * get_mask(mask, at, lanes))

    sweep(pre_in.shape[1], pre_in.shape[2], line(total, m, count, gain, bias), step)
    pre[0] = nn(act[0], wide_of(weight)).astype(pre.dtype)
    count_up(pre, out_total, m)


def k_fourth(count, pre_in, entry, total, gain, bias, mask, weight, block, corner, slope, pre, out_total, full):
    m = pl.program_id(0)
    wide = COLS // 2
    chunk = 4 * COLS

    def step(at, lanes, v):
        x = get(pre_in, at, lanes) * v[0] + v[1] + get(entry, at, lanes)
        square = x * x
        t = jnp.tanh(x * (TANH_SCALE + TANH_SCALE * TANH_CUBE * square))
        inside = x * (TANH_SCALE + 3.0 * TANH_SCALE * TANH_CUBE * square)
        part = (0.5 + 0.5 * t) * get_mask(mask, at, lanes)
        y = x * part
        put(block, at, lanes, y)
        put(slope, at, lanes, part + part * inside * (1.0 - t))
        put_tall(full, slice(0, chunk), flat(y), lanes.start)
        pair = [get_tall(full, pl.ds(k * COLS, wide, stride=2), lanes) for k in (0, 2)]
        corner[0, pl.ds(pl.multiple_of(at.start // 4, COLS), COLS), lanes] = jnp.concatenate(pair, 0).astype(BF)

    sweep(pre_in.shape[1], pre_in.shape[2], line(total, m, count, gain, bias), step, chunk=chunk)
    pre[0] = nn(block[0], wide_of(weight)).astype(pre.dtype)
    count_up(pre, out_total, m)


def k_seventh(corner, weight, pre, out_total):
    micro, half, tile = pre.shape
    value = nn(corner[...].reshape(micro * half, -1), wide_of(weight))
    pre[...] = value.reshape(pre.shape).astype(pre.dtype)
    for m in range(micro):
        part = eight(value[m * half : (m + 1) * half])
        sums = [jnp.sum(v, axis=(0, 1))[None] for v in (part, part * part)]
        rows = lax.broadcasted_iota(jnp.int32, out_total.shape, 0)
        table = jnp.zeros_like(sums[0]) if m == 0 else out_total[...]
        out_total[...] = jnp.where(rows == 2 * m, sums[0], jnp.where(rows == 2 * m + 1, sums[1], table))


def k_fifth(count, pre_in, total, gain, bias, mask, half_mask, inner, weight, pre, patch, out_total, act, eo, oe, oo):
    m = pl.program_id(0)
    cells, c = pre_in.shape[1], pre_in.shape[2]
    half = cells // 4
    wide = COLS // 2

    def step(at, lanes, v):
        x = get(pre_in, at, lanes) * v[0] + v[1]
        put_tall(act, at, flat(gelu(x) * get_mask(mask, at, lanes)), lanes.start)

    sweep(cells, c, line(total, m, count, gain, bias), step)
    pad = 2 * wide
    for buf in (eo, oe, oo):
        buf[0:pad, :] = jnp.zeros((pad, c), F32)
    for j in range(c // LANES):
        lanes = slice(j * LANES, (j + 1) * LANES)
        even = act[j, pl.ds(0, cells // 2, stride=2), :].reshape(half // wide, 2, wide, LANES)
        odd = act[j, pl.ds(1, cells // 2, stride=2), :].reshape(half // wide, 2, wide, LANES)
        patch[0, :, 4 * c + j * LANES : 4 * c + (j + 1) * LANES] = even[:, 0].reshape(half, LANES).astype(BF)
        oe[pad : pad + half, lanes] = even[:, 1].reshape(half, LANES)
        eo[pad : pad + half, lanes] = odd[:, 0].reshape(half, LANES)
        oo[pad : pad + half, lanes] = odd[:, 1].reshape(half, LANES)
    first = jnp.concatenate([inner[0]] * (c // LANES), 1)
    take = lambda buf, back: buf[pad - back : pad - back + half, :]
    taps = (
        take(oo, wide + 1) * first, take(oe, wide) * first, take(oo, wide) * first,
        take(eo, 1), None, take(eo, 0),
        take(oo, 1), take(oe, 0), take(oo, 0),
    )
    for k, tap in enumerate(taps):
        if tap is not None:
            patch[0, :, k * c : (k + 1) * c] = tap.astype(BF)
    pre[0] = nn(patch[0], wide_of(weight))
    count_up(pre, out_total, m, half_mask)


def k_last(count, six, seven, tot6, tot7, g6, b6, g7, b7, half_mask, cot, out, slope, total, row):
    m = pl.program_id(0)
    half, c = six.shape[1], six.shape[2]
    wide = COLS // 2
    shown, across = out.shape[2], out.shape[3]
    scale6, shift6 = line(tot6, m, count, g6, b6)
    scale7, shift7 = line(tot7, m, count, g7, b7)
    row[...] = jnp.zeros_like(row)

    def step(at, lanes, v):
        p = 2 * (at.start // (2 * wide))
        mask = get_mask(half_mask, at, lanes)
        s6, s7 = get(six, at, lanes), get(seven, at, lanes)
        joined = s6 * v[0] + s7 * v[1] + v[2]
        square = joined * joined
        t = jnp.tanh(joined * (TANH_SCALE + TANH_SCALE * TANH_CUBE * square))
        inside = joined * (TANH_SCALE + 3.0 * TANH_SCALE * TANH_CUBE * square)
        part = (0.5 + 0.5 * t) * mask
        result = flat(joined * part)
        for k in range(2):
            q = jnp.minimum(p + k, shown - 1)
            if shown % 2 == 0 or k == 0:
                out[0, 0, q, :, lanes] = result[k * wide : k * wide + across].astype(BF)
            else:

                @pl.when(p + k < shown)
                def _():
                    out[0, 0, q, :, lanes] = result[k * wide : k * wide + across].astype(BF)

            row[k * wide : k * wide + across, lanes] = cot[0, 0, q, :, lanes].astype(F32)
        d = part * (1.0 + inside * (1.0 - t)) * eight(row[:, lanes])
        put(slope, at, lanes, d)
        return d, d * s6, d * s7

    sums = sweep(half, c, (scale6, scale7, shift6 + shift7), step, 3, chunk=2 * wide, width=512)
    put_sums(total, m, *centred(tot6, m, count, sums[0], sums[1]))
    put_sums(total, m, *centred(tot7, m, count, sums[0], sums[2]), c)


def slope_sums(d_out, pre, tot, m, population, gain, bias, mask, out_total, more=None):
    def add(at, lanes, v):
        p = get(pre, at, lanes)
        d = gelu_slope(p * v[0] + v[1]) * get(d_out, at, lanes) * get_mask(mask, at, lanes)
        put(d_out, at, lanes, d)
        return d, d * p

    sums = sweep(pre.shape[1], pre.shape[2], line(tot, m, population, gain, bias), add, 2)
    put_sums(out_total, m, *centred(tot, m, population, *sums))


def norm_back(d_pre, d, pre, tot, back, m, population, gain, mask):
    def step(at, lanes, v):
        value = get(d, at, lanes) * v[0] + get(pre, at, lanes) * v[1] + v[2]
        put(d_pre, at, lanes, value * get_mask(mask, at, lanes))

    sweep(pre.shape[1], pre.shape[2], back_line(tot, back, m, population, gain), step)


def k_back_six(
    count, slope, six, seven, tot6, tot7, back, g6, g7, five, tot5, g5, b5, half_mask, weight,
    d_six, d_seven, d_five, out_total,
):
    m = pl.program_id(0)
    half, c = six.shape[1], six.shape[2]

    def step(at, lanes, v):
        d = get(slope, at, lanes)
        mask = get_mask(half_mask, at, lanes)
        put(d_six, at, lanes, (d * v[0] + get(six, at, lanes) * v[1] + v[2]) * mask)
        put(d_seven, at, lanes, (d * v[3] + get(seven, at, lanes) * v[4] + v[5]) * mask)

    vectors = back_line(tot6, back, m, count, g6) + back_line(tot7, back, m, count, g7, c)
    sweep(half, c, vectors, step)
    d_five[0] = nt(d_six[0], wide_of(weight))
    slope_sums(d_five, five, tot5, m, count, g5, b5, half_mask, out_total)


def k_corner(d_seven, weight, d_corner):
    d_corner[0] = nt(d_seven[0], wide_of(weight)).astype(d_corner.dtype)


def k_back_five(
    half_count, full_count, d_five, five, tot5, back5, g5, half_mask, inner, weight, four, tot4, g4, b4, mask,
    d_pre, d_four, out_total, grid_scratch, shifted,
):
    m = pl.program_id(0)
    half, c = five.shape[1], five.shape[2]
    cells = 4 * half
    wide = COLS // 2
    norm_back(d_pre, d_five, five, tot5, back5, m, half_count, g5, half_mask)
    d = d_pre[0]
    wide_d = d.astype(F32)
    tail = 2 * wide
    shifted[half : half + tail, :] = jnp.zeros((tail, c), F32)
    shifted[0:half, :] = wide_d
    right = shifted[1 : 1 + half, :].astype(BF)
    shifted[0:half, :] = wide_d * jnp.concatenate([inner[0]] * (c // LANES), 1)
    down = shifted[wide : wide + half, :].astype(BF)
    down_right = shifted[wide + 1 : wide + 1 + half, :].astype(BF)
    taps = wide_of(weight)
    w = lambda tap: taps[tap * c : (tap + 1) * c]
    ee = nt(d, w(4))
    eo = nt(d, w(5)) + nt(right, w(3))
    oe = nt(d, w(7)) + nt(down, w(1))
    oo = nt(d, w(8)) + nt(right, w(6)) + nt(down, w(2)) + nt(down_right, w(0))
    rows = half // wide
    even = jnp.stack([ee.reshape(rows, wide, c), oe.reshape(rows, wide, c)], 1).reshape(cells // 2, c)
    odd = jnp.stack([eo.reshape(rows, wide, c), oo.reshape(rows, wide, c)], 1).reshape(cells // 2, c)
    put_tall(grid_scratch, pl.ds(0, cells // 2, stride=2), even)
    put_tall(grid_scratch, pl.ds(1, cells // 2, stride=2), odd)

    def add(at, lanes, v):
        p = get(four, at, lanes)
        got = eight(get_tall(grid_scratch, at, lanes))
        d = gelu_slope(p * v[0] + v[1]) * got * get_mask(mask, at, lanes)
        put(d_four, at, lanes, d)
        return d, d * p

    sums = sweep(cells, c, line(tot4, m, full_count, g4, b4), add, 2)
    put_sums(out_total, m, *centred(tot4, m, full_count, *sums))


def k_back_four(
    count, d_four, four, tot4, back4, g4, mask, weight, d_corner, three, slope, tot3,
    d_pre, d_summed, out_total, placed, d_block,
):
    m = pl.program_id(0)
    cells, c = three.shape[1], three.shape[2]
    norm_back(d_pre, d_four, four, tot4, back4, m, count, g4, mask)
    d_block[0] = nt(d_pre[0], wide_of(weight))
    wide = COLS // 2
    placed[...] = jnp.zeros_like(placed)

    def add(at, lanes, v):
        corner_at = pl.ds(pl.multiple_of(at.start // 4, COLS), COLS)
        value = d_corner[0, corner_at, lanes].astype(F32)
        for k in range(2):
            rows = pl.ds(2 * k * COLS, wide, stride=2)
            put_tall(placed, rows, value[k * wide : (k + 1) * wide], lanes.start)
        got = get(d_block, at, lanes) + eight(get_tall(placed, slice(0, 4 * COLS), lanes))
        d = get(slope, at, lanes) * got
        put(d_summed, at, lanes, d)
        return d, d * get(three, at, lanes)

    sums = sweep(cells, c, (), add, 2, chunk=4 * COLS)
    put_sums(out_total, m, *centred(tot3, m, count, *sums))


def k_back_three(count, d_summed, three, tot3, back3, g3, mask, weight, two, tot2, g2, b2, d_pre, d_two, out_total):
    m = pl.program_id(0)
    norm_back(d_pre, d_summed, three, tot3, back3, m, count, g3, mask)
    d_two[0] = nt(d_pre[0], wide_of(weight))
    slope_sums(d_two, two, tot2, m, count, g2, b2, mask, out_total)


def k_back_two(
    count, d_two, two, tot2, back2, g2, mask, flags, weight, own, spill, tot1, g1, b1,
    d_pre, d_one, out_total, source, trio, joined,
):
    m = pl.program_id(0)
    cells, c = two.shape[1], two.shape[2]
    clear_ends(source, cells)

    def step(at, lanes, v):
        value = get(d_two, at, lanes) * v[0] + get(two, at, lanes) * v[1] + v[2]
        value = value * get_mask(mask, at, lanes)
        put(d_pre, at, lanes, value)
        source[later(at, COLS), lanes] = flat(value)

    sweep(cells, c, back_line(tot2, back2, m, count, g2), step)
    spread_trio(source, trio, cells)
    upper = lane(flags, UPPER, slice(None)).astype(BF)
    lower = lane(flags, LOWER, slice(None)).astype(BF)
    shifted = (
        trio[0:cells, :] * upper,
        trio[COLS : COLS + cells, :],
        trio[2 * COLS : 2 * COLS + cells, :] * lower,
    )
    tap = lambda k: nt(shifted[k // 3][:, k % 3 * c : (k % 3 + 1) * c], weight[(8 - k) * c : (9 - k) * c, :])
    d_one[0] = sum((tap(k) for k in range(1, 9)), tap(0))
    join_pre_one(own, spill, joined, c)
    slope_sums(d_one, joined, tot1, m, count, g1, b1, mask, out_total)


def k_back_one(count, d_one, own, spill, tot1, back1, g1, mask, d_pre, joined):
    m = pl.program_id(0)
    join_pre_one(own, spill, joined, d_one.shape[2])
    norm_back(d_pre, d_one, joined, tot1, back1, m, count, g1, mask)


def k_input(d_pre, more_pre, d_summed, weight, *refs):
    more_summed, (out, both, sums) = refs[:-3], refs[-3:]
    m = pl.program_id(0)
    spilled, cells = more_pre.shape[1], both.shape[0]
    blocks = sums.shape[1] // LANES
    own = cells // COLS
    across = out.shape[1] // blocks // own
    both[...] = d_pre[0, 0:cells, :]
    both[0:spilled, :] = d_pre[0, 0:spilled, :] + more_pre[0]
    sums[...] = nt(both[...], weight[...])
    for r in range(own):
        at = r * COLS
        value = sums[at : at + COLS, :] + d_summed[0, at : at + COLS, :].astype(F32)
        if at < spilled:
            extra = more_summed[0][at : at + COLS, :].astype(F32)
            for k in range(1, len(more_summed)):
                extra = jnp.where(m == k, more_summed[k][at : at + COLS, :].astype(F32), extra)
            value = value + extra
        for j in range(blocks):
            rows = pl.ds(r * across * blocks + j, across, stride=blocks)
            out[0, rows, :] = value[:across, j * LANES : (j + 1) * LANES]


def exchange(x, mask):
    total = lax.axis_size("rows") * lax.axis_size("batch")
    return lax.ppermute(x, AXES, [(i, i ^ mask) for i in range(total)])


def from_behind(x, by):
    devices = lax.axis_size("rows")
    pairs = [(i, i + by) for i in range(devices) if 0 <= i + by < devices]
    return lax.ppermute(x, "rows", pairs)


class Chain:
    def __init__(self, steps):
        self.steps, self.flying, self.done, self.result = steps, None, False, None
        self.ready = next(steps)

    def launch(self, array):
        self.flying = self.ready[1](array)

    def land(self):
        try:
            self.ready = self.steps.send(self.flying)
        except StopIteration as end:
            self.done, self.result = True, end.value
        self.flying = None

    def value(self):
        while not self.done:
            if self.flying is None:
                self.launch(self.ready[0])
            self.land()
        return self.result


def hook(x, start=(), finish=(), need=()):
    if not (start or finish or need):
        return x
    landed = []
    for chain in finish:
        if not chain.done:
            landed.append(chain.flying)
            chain.land()
    live = [chain for chain in start if not chain.done]
    tied = lax.optimization_barrier((x, [c.ready[0] for c in live], landed, list(need)))
    for chain, array in zip(live, tied[1]):
        chain.launch(array)
    return tied[0]


def global_sum(x, b=None, c=None, d=None):
    bits = device_bits()
    split = x.shape[1] >= 2048
    if split:
        half = x.shape[1] // 2
        part = lambda bit: lax.dynamic_slice_in_dim(x, bit * half, half, 1)
        x = part(my_bit(0)) + exchange(part(1 - my_bit(0)), 1)
    else:
        x = x + exchange(x, 1)
    x = hook(x, **(b or {}))
    step = 1
    while step < bits:
        low = 1 << step
        if step + 1 < bits:
            p, q, r = exchange(x, low), exchange(x, 2 * low), exchange(x, 3 * low)
            x = (x + p) + (q + r)
        else:
            x = x + exchange(x, low)
        if step == 1:
            x = hook(x, **(c or {}))
        step += 2
    if split:
        other = exchange(x, 1)
        upper = my_bit(0) == 1
        x = jnp.concatenate([jnp.where(upper, other, x), jnp.where(upper, x, other)], 1)
    return hook(x, **(d or {}))


def device_bits():
    total = lax.axis_size("rows") * lax.axis_size("batch")
    return total.bit_length() - 1


def my_bit(bit):
    number = lax.axis_index("rows") * lax.axis_size("batch") + lax.axis_index("batch")
    return (number >> bit) & 1


def batch_bits():
    return lax.axis_size("batch").bit_length() - 1


def across(bit):
    return lambda x: exchange(x, 1 << bit)


def lanes_of(w, parts, wide=256):
    x = w.reshape(parts, -1, w.shape[1] // wide, wide)
    return x.transpose(0, 2, 1, 3).reshape(parts, -1, wide)


def from_lanes(x, c):
    parts, wide = x.shape[0], x.shape[2]
    x = x.reshape(parts, c // wide, -1, wide)
    return x.transpose(0, 2, 1, 3).reshape(-1, c)


def ordered(mine, other, bit, axis):
    upper = my_bit(bit) == 1
    return jnp.stack([jnp.where(upper, other, mine), jnp.where(upper, mine, other)], axis)


def gather_steps(packed, parts):
    bits, low = device_bits(), batch_bits()
    number = my_bit(0) if parts == 1 else lax.axis_index("batch")
    x = lax.dynamic_index_in_dim(packed, number, 0, keepdims=False)
    for bit in list(reversed(range(low, bits))) + list(reversed(range(parts))):
        got = yield x, across(bit)
        x = ordered(x, got, bit, x.ndim - 2)
    return x.reshape((-1,) + x.shape[-2:])


def gather_offloaded(ws):
    quarters, wide = lax.axis_size("batch"), ws[0].shape[1]
    packed = jnp.concatenate([w.reshape(quarters, -1, wide) for w in ws], 1)
    part = lax.dynamic_index_in_dim(packed, lax.axis_index("batch"), 0, keepdims=False)
    whole = lax.all_gather(part, AXES, axis=0)
    out, at = [], 0
    for w in ws:
        n = w.shape[0] // quarters
        if n % 16 == 0 and at % n == 0:
            block = at // n
            spec = pl.BlockSpec(
                (whole.shape[0], n, wide), lambda m, k=block: (0, k, 0), pipeline_mode=pl.Buffered(1)
            )
            out.append((whole, spec))
        else:
            part = whole[:, at : at + n].reshape(-1, wide)
            out.append((part, pl.BlockSpec(part.shape, lambda m: (0, 0), pipeline_mode=pl.Buffered(1))))
        at += n
    return out


def sharded(grad, c):
    total = lax.axis_size("rows") * lax.axis_size("batch")
    if grad.shape[1] == c:
        return grad.reshape(total, -1, c)
    return lanes_of(grad, total)


def spread_steps(x):
    for bit in reversed(range(batch_bits())):
        got = yield x, across(bit)
        x = ordered(x, got, bit, x.ndim - 2)
    return x.reshape((-1,) + x.shape[-2:])


def reduce_scattered(part, order):
    bits = device_bits()
    x = part.reshape((2,) * bits + part.shape[1:])
    left = list(reversed(range(bits)))
    got = None
    for bit in order:
        axis = left.index(bit)
        left.remove(bit)
        half = lambda v, b: lax.dynamic_index_in_dim(v, b, axis, keepdims=False)
        keep, send = my_bit(bit), 1 - my_bit(bit)
        if got is None:
            x, give = half(x, keep), half(x, send)
        else:
            x, give = half(x, keep) + half(got, keep), half(x, send) + half(got, send)
        got = yield give, across(bit)
    return x + got


def lanes_back(filter_and_spec, c):
    whole, spec = filter_and_spec
    if whole.ndim == 3:
        n, k = spec.block_shape[1], spec.index_map(0)[1]
        return from_lanes(whole[:, k * n : (k + 1) * n], c)
    return from_lanes(whole.reshape(lax.axis_size("rows") * lax.axis_size("batch"), -1, whole.shape[1]), c)


def reduce_first(part):
    bits, low = device_bits(), batch_bits()
    x = part.reshape((2,) * bits + part.shape[1:])
    left = list(reversed(range(bits)))
    got = None
    for bit in [0] + list(range(low, bits - 1)):
        axis = left.index(bit)
        left.remove(bit)
        half = lambda v, b: lax.dynamic_index_in_dim(v, b, axis, keepdims=False)
        keep, send = my_bit(bit), 1 - my_bit(bit)
        if got is None:
            x, give = half(x, keep), half(x, send)
        else:
            x, give = half(x, keep) + half(got, keep), half(x, send) + half(got, send)
        got = yield give, across(bit)
    return x + got


def reduce_last(x):
    low, last = batch_bits(), device_bits() - 1
    bit = my_bit(last)
    half = lambda b: lax.dynamic_index_in_dim(x, b, 0, keepdims=False)
    got = yield half(1 - bit), across(last)
    x = half(bit) + got
    for b in range(1, low):
        got = yield x, across(b)
        x = x + got
    got = yield x, across(0)
    x = ordered(x, got, 0, x.ndim - 2)
    return x.reshape((-1,) + x.shape[-2:])


def one_step(x, send):
    return (yield x, send)


def unpack(shard, shapes):
    devices = lax.axis_size("rows")
    out, at = [], 0
    for k, c in shapes:
        n = k * c // devices // shard.shape[0] // shard.shape[2]
        part = shard[:, at : at + n]
        out.append((from_lanes(part, c) if shard.shape[2] != c else part.reshape(-1, c)).astype(F32))
        at += n
    return out


LIMIT = 16


def per_micro(shape):
    zeros = (0,) * (len(shape) - 1)
    return pl.BlockSpec((1,) + tuple(shape[1:]), lambda m: (m,) + zeros)


def whole(shape):
    zeros = (0,) * len(shape)
    return pl.BlockSpec(tuple(shape), lambda m: zeros, pipeline_mode=pl.Buffered(1))


def table(shape):
    zeros = (0,) * len(shape)
    return pl.BlockSpec(tuple(shape), lambda m: zeros)


def call(kernel, micro, ins, outs, scratch=(), limit=LIMIT, after=()):
    kind = {"m": per_micro, "w": whole, "s": lambda shape: pl.BlockSpec(memory_space=pltpu.SMEM)}
    in_specs = [k if isinstance(k, pl.BlockSpec) else kind[k](a.shape) for a, k in ins]
    in_specs += [pl.BlockSpec(memory_space=pl.ANY)] * len(after)
    out_specs = [per_micro(sh) if k == "m" else table(sh) for sh, _, k in outs]

    def run(*refs):
        kernel(*refs[: len(ins)], *refs[len(ins) + len(after) :])

    return pl.pallas_call(
        run,
        grid=(micro,),
        in_specs=in_specs,
        out_specs=out_specs,
        out_shape=[jax.ShapeDtypeStruct(sh, t) for sh, t, _ in outs],
        scratch_shapes=[pltpu.VMEM(sh, t) for sh, t in scratch],
        compiler_params=pltpu.CompilerParams(
            dimension_semantics=("arbitrary",), vmem_limit_bytes=limit * 1024 * 1024
        ),
        name=getattr(kernel, "func", kernel).__name__,
    )(*[a for a, _ in ins], *after)


def weight_term(left, right):
    k, n = left.shape[-1], right.shape[-1]
    return lax.dot_general(
        left.reshape(-1, k), right.reshape(-1, n), (((0,), (0,)), ((), ())), preferred_element_type=F32
    ).astype(BF)


def shards(
    features, view_kind, narrow_one, spatial_one, expand_one, gains_one, biases_one,
    narrow_two, spatial_two, expand_two, shortcut, gains_two, biases_two, cotangent,
):
    micro, _, own, across, channels = features.shape
    m1 = spatial_one.shape[1]
    m2 = spatial_two.shape[1]
    outward = shortcut.shape[1]
    sources = lax.axis_size("rows") * own // 52
    full_count = float(lax.axis_size("batch") * sources * 536)
    half_count = float(lax.axis_size("batch") * sources * 134)
    anchor = lax.axis_index("rows") * own
    cells, half = WIN * COLS, WIN * COLS // 4
    mine, more = own * COLS, SPILL * COLS

    chain_n1 = Chain(gather_steps(narrow_one.reshape(2, -1, m1), 1))
    chain_a = Chain(gather_steps(spatial_one.reshape(4, -1, m1), 2))
    thin = [lanes_of(expand_one, 4, m2).reshape(-1, m2)]
    spatial_b, narrow_b, thin_a = gather_offloaded([spatial_two, narrow_two] + thin)
    expand_a = lanes_back(thin_a, channels)
    bypass, expand_b = gather_offloaded([shortcut, expand_two])
    chain_f = [
        Chain(one_step(features[k, 0, :SPILL], lambda x: from_behind(x, -1))) for k in range(micro)
    ]
    g1, g2, g3 = (v[None] for v in jnp.split(gains_one, [m1, 2 * m1]))
    b1, b2, b3 = (v[None] for v in jnp.split(biases_one, [m1, 2 * m1]))
    cuts = [m2, 2 * m2, 2 * m2 + outward]
    g4, g5, g6, g7 = (v[None] for v in jnp.split(gains_two, cuts))
    b4, b5, b6, b7 = (v[None] for v in jnp.split(biases_two, cuts))
    mask, half_mask, flags, inner = pl.pallas_call(
        functools.partial(k_masks, own),
        in_specs=[pl.BlockSpec(memory_space=pltpu.SMEM)] * 2,
        out_shape=[
            jax.ShapeDtypeStruct((micro, cells, LANES), F32),
            jax.ShapeDtypeStruct((micro, half, LANES), F32),
        ]
        * 2,
        name="k_masks",
    )(anchor[None].astype(jnp.int32), view_kind)

    full_table = lambda c: ((8, c), F32, "t")
    per = lambda c, t=F32, n=cells: ((micro, n, c), t, "m")

    for chain in (chain_n1, chain_a):
        chain.launch(chain.ready[0])
    chain_n1.land()
    before = [mask]
    while not chain_n1.done:
        chain_n1.launch(lax.optimization_barrier((chain_n1.ready[0], before))[0])
        landed = chain_n1.flying
        chain_n1.land()
        if chain_a.flying is not None and len(before) < 3 and not chain_n1.done:
            chain_a.land()
            chain_a.launch(lax.optimization_barrier((chain_a.ready[0], landed))[0])
            before = before + [landed]
            if len(before) == 3:
                hook(landed, start=chain_f)
    narrow_a = chain_n1.value().reshape(-1, m1)
    pre_one, head, t1 = call(
        k_first, micro, [(features, "m"), (flags, "m"), (narrow_a, "w")],
        [per(m1, F32, mine), per(m1, BF, more), full_table(m1)], [((mine, channels), BF)],
    )
    chain_h = Chain(one_step(head, lambda x: from_behind(x, -1)))
    t1 = global_sum(
        t1,
        b=dict(finish=[chain_a]),
        c=dict(start=[chain_a, chain_h]),
        d=dict(finish=[chain_a, chain_h], start=[chain_a]),
    )
    pre_spill = chain_h.value()
    spatial_a = chain_a.value().reshape(-1, m1)
    pre_two, patch_one, t2 = call(
        functools.partial(k_second, full_count), micro,
        [(pre_one, "m"), (pre_spill, "m"), (t1, "w"), (g1, "w"), (b1, "w"), (mask, "m"),
         (flags, "m"), (spatial_a, "w")],
        [per(m1), per(9 * m1, BF), full_table(m1)],
        [((cells + 2 * COLS, m1), F32), ((cells + 2 * COLS, 3 * m1), BF), ((1, cells, m1), F32)],
        limit=20,
    )
    (entry,) = call(
        k_entry, micro,
        [(features, "m"), (mask, "m")] + [(f.value(), "w") for f in chain_f],
        [per(channels, BF)], [((cells, channels), BF)],
    )
    t2 = global_sum(t2, c=dict(need=[entry]))
    act_two, pre_three, t3 = call(
        functools.partial(k_third, full_count), micro,
        [(pre_two, "m"), (t2, "w"), (g2, "w"), (b2, "w"), (mask, "m"), (expand_a, "w")],
        [per(m1, BF), per(channels, BF), full_table(channels)],
    )
    t3 = global_sum(t3)
    block_out, corner, slope_three, pre_four, t4 = call(
        functools.partial(k_fourth, full_count), micro,
        [(pre_three, "m"), (entry, "m"), (t3, "w"), (g3, "w"), (b3, "w"), (mask, "m"), narrow_b],
        [per(channels, BF), per(channels, BF, half), per(channels, BF), per(m2, BF), full_table(m2)],
        [((channels // LANES, 4 * COLS, LANES), F32)],
    )
    t4 = global_sum(t4)
    pre_five, patch_two, t5 = call(
        functools.partial(k_fifth, full_count), micro,
        [(pre_four, "m"), (t4, "w"), (g4, "w"), (b4, "w"), (mask, "m"), (half_mask, "m"), (inner, "m"),
         spatial_b],
        [per(m2, F32, half), per(9 * m2, BF, half), full_table(m2)],
        [((m2 // LANES, cells, LANES), F32)] + [((half + COLS, m2), F32)] * 3,
        limit=20,
    )
    t5 = global_sum(t5)
    act_five, pre_six, t6 = call(
        functools.partial(k_third, half_count), micro,
        [(pre_five, "m"), (t5, "w"), (g5, "w"), (b5, "w"), (half_mask, "m"), expand_b],
        [per(m2, BF, half), per(outward, BF, half), full_table(outward)],
    )
    tile = outward // 4
    by_tile = bypass[1].block_shape[:-1] + (tile,)
    pre_seven, t7 = pl.pallas_call(
        k_seventh,
        grid=(4,),
        in_specs=[
            pl.BlockSpec(corner.shape, lambda n: (0, 0, 0)),
            pl.BlockSpec(by_tile, lambda n: (0,) * (len(by_tile) - 1) + (n,)),
        ],
        out_specs=[
            pl.BlockSpec((micro, half, tile), lambda n: (0, 0, n)),
            pl.BlockSpec((8, tile), lambda n: (0, n)),
        ],
        out_shape=[
            jax.ShapeDtypeStruct((micro, half, outward), BF),
            jax.ShapeDtypeStruct((8, outward), F32),
        ],
        compiler_params=pltpu.CompilerParams(vmem_limit_bytes=LIMIT * 1024 * 1024),
        name="k_seventh",
    )(corner, bypass[0])
    t67 = global_sum(jnp.concatenate([t6, t7], 1))
    t6, t7 = t67[:, :outward], t67[:, outward:]
    outputs, slope, u67 = call(
        functools.partial(k_last, half_count), micro,
        [(pre_six, "m"), (pre_seven, "m"), (t6, "w"), (t7, "w"), (g6, "w"), (b6, "w"), (g7, "w"), (b7, "w"),
         (half_mask, "m"), (cotangent, "m")],
        [(cotangent.shape, BF, "m"), per(outward, BF, half), full_table(2 * outward)],
        [((COLS, outward), F32)],
    )
    u67 = global_sum(u67)
    d_six, d_seven, d_five, u5 = call(
        functools.partial(k_back_six, half_count), micro,
        [(slope, "m"), (pre_six, "m"), (pre_seven, "m"), (t6, "w"), (t7, "w"), (u67, "w"), (g6, "w"), (g7, "w"),
         (pre_five, "m"), (t5, "w"), (g5, "w"), (b5, "w"), (half_mask, "m"), expand_b],
        [per(outward, BF, half), per(outward, BF, half), per(m2, F32, half), full_table(m2)],
    )
    (d_corner,) = call(
        k_corner, micro, [(d_seven, "m"), bypass], [per(channels, BF, half)]
    )
    grad_e2 = weight_term(act_five, d_six)
    grad_sc = weight_term(corner, d_seven)
    pack_b = jnp.concatenate([sharded(grad_sc, outward), sharded(grad_e2, outward)], 1).reshape(-1, outward)
    u5 = global_sum(u5, c=dict(need=[pack_b]))
    part_b = lax.psum_scatter(pack_b, AXES, scatter_dimension=0, tiled=True)
    d_pre_five, d_four, u4 = call(
        functools.partial(k_back_five, half_count, full_count), micro,
        [(d_five, "m"), (pre_five, "m"), (t5, "w"), (u5, "w"), (g5, "w"), (half_mask, "m"), (inner, "m"),
         spatial_b, (pre_four, "m"), (t4, "w"), (g4, "w"), (b4, "w"), (mask, "m")],
        [per(m2, BF, half), per(m2), full_table(m2)],
        [((m2 // LANES, cells, LANES), F32), ((half + COLS, m2), F32)],
        limit=22,
    )
    grad_s2 = sharded(weight_term(patch_two, d_pre_five), m2)
    cut = grad_s2.shape[1] // 32 * 16 or grad_s2.shape[1] // 2
    low = batch_bits()
    chain_rs = [
        Chain(reduce_scattered(grad_s2[:, :cut], list(range(device_bits())))),
        Chain(reduce_scattered(grad_s2[:, cut:], [0, low] + list(range(1, low)) + list(range(low + 1, device_bits())))),
    ]
    u4 = global_sum(u4, b=dict(start=chain_rs), c=dict(finish=chain_rs, start=chain_rs))
    d_pre_four, d_summed, u3 = call(
        functools.partial(k_back_four, full_count), micro,
        [(d_four, "m"), (pre_four, "m"), (t4, "w"), (u4, "w"), (g4, "w"), (mask, "m"), narrow_b,
         (d_corner, "m"), (pre_three, "m"), (slope_three, "m"), (t3, "w")],
        [per(m2, BF), per(channels, BF), full_table(channels)],
        [((channels // LANES, 4 * COLS, LANES), F32), ((1, cells, channels), F32)],
        limit=24,
    )
    grad_n2 = [
        sharded(weight_term(block_out, d_pre_four[..., k : k + 256]), 256) for k in range(0, m2, 256)
    ]
    spilled = d_summed[:, mine : mine + more]
    chain_ds = [Chain(one_step(spilled[k], lambda x: from_behind(x, 1))) for k in range(micro)]
    chain_r2 = Chain(reduce_first(jnp.concatenate(grad_n2, 1)))
    u3 = global_sum(
        u3,
        b=dict(start=[chain_r2]),
        c=dict(finish=chain_rs + [chain_r2], start=chain_rs + [chain_r2]),
        d=dict(start=[chain_ds[0]]),
    )
    d_pre_three, d_two, u2 = call(
        functools.partial(k_back_three, full_count), micro,
        [(d_summed, "m"), (pre_three, "m"), (t3, "w"), (u3, "w"), (g3, "w"), (mask, "m"), (expand_a, "w"),
         (pre_two, "m"), (t2, "w"), (g2, "w"), (b2, "w")],
        [per(channels, BF), per(m1), full_table(m1)],
    )
    grad_e1 = weight_term(act_two, d_pre_three)
    chain_r3 = Chain(reduce_first(sharded(grad_e1, 256)))
    u2 = global_sum(
        u2,
        b=dict(finish=[chain_r2], start=[chain_r3]),
        c=dict(finish=chain_rs + [chain_ds[0], chain_r3], start=[chain_r3]),
        d=dict(start=chain_rs + [chain_r2] + chain_ds[1:2]),
    )
    d_pre_two, d_one, u1 = call(
        functools.partial(k_back_two, full_count), micro,
        [(d_two, "m"), (pre_two, "m"), (t2, "w"), (u2, "w"), (g2, "w"), (mask, "m"), (flags, "m"),
         (spatial_a, "w"), (pre_one, "m"), (pre_spill, "m"), (t1, "w"), (g1, "w"), (b1, "w")],
        [per(m1, BF), per(m1), full_table(m1)],
        [((cells + 2 * COLS, m1), F32), ((cells + 2 * COLS, 3 * m1), BF), ((1, cells, m1), F32)],
        limit=20,
    )
    grad_s1 = weight_term(patch_one, d_pre_two)
    chain_r1 = Chain(reduce_first(sharded(grad_s1, 256)))
    u1 = global_sum(
        u1,
        b=dict(finish=[chain_r3], start=[chain_r1]),
        c=dict(finish=chain_rs + [chain_r2, chain_r1] + chain_ds[1:2], start=[chain_r1]),
        d=dict(start=chain_rs + [chain_r3] + chain_ds[2:]),
    )
    (d_pre_one,) = call(
        functools.partial(k_back_one, full_count), micro,
        [(d_one, "m"), (pre_one, "m"), (pre_spill, "m"), (t1, "w"), (u1, "w"), (g1, "w"), (mask, "m")],
        [per(m1, BF)], [((1, cells, m1), F32)],
    )
    chain_rn = Chain(reduce_first(sharded(weight_term(entry, d_pre_one), 256)))
    chain_rb = Chain(spread_steps(part_b))
    chain_rn.launch(chain_rn.ready[0])
    landed = chain_rn.flying
    chain_rn.land()
    hook(landed, finish=[chain_r1], start=[chain_r1])
    while not chain_rn.done:
        chain_rn.launch(chain_rn.ready[0])
        landed = chain_rn.flying
        chain_rn.land()
    firsts = [c.value() for c in (chain_rn, chain_r1, chain_r2, chain_r3)]
    chain_last = Chain(reduce_last(jnp.concatenate(firsts, -2)))
    chain_dp = Chain(one_step(d_pre_one[:, mine : mine + more], lambda x: from_behind(x, 1)))
    chain_last.launch(chain_last.ready[0])
    hook(landed, start=[chain_dp])
    landed = chain_last.flying
    chain_last.land()
    chain_r4 = Chain(spread_steps(jnp.concatenate([c.value() for c in chain_rs], 0)))
    hook(landed, start=[chain_rb, chain_r4])
    chain_last.launch(chain_last.ready[0])
    landed = chain_last.flying
    chain_last.land()
    out_n1, out_s1, out_n2, out_e1 = unpack(
        chain_last.value(), [(channels, m1), (9 * m1, m1), (channels, m2), (m1, channels)]
    )
    (out_s2,) = unpack(chain_r4.value(), [(9 * m2, m2)])
    out_sc, out_e2 = unpack(chain_rb.value(), [(channels, outward), (m2, outward)])
    (grad_input,) = call(
        k_input, micro,
        [(d_pre_one, "m"), (chain_dp.value(), "m"), (d_summed, "m"), (narrow_a, "w")]
        + [(c.value(), "w") for c in chain_ds],
        [((micro, own * across * channels // LANES, LANES), F32, "m")],
        [((mine, m1), BF), ((mine, channels), F32)],
        after=[landed],
    )
    grad_input = grad_input.reshape(features.shape)
    added = lambda k, us: jnp.concatenate([u[k] + u[k + 2] + u[k + 4] for u in us])
    first = (u1, u2, u3)
    later = (u4, u5, u67)
    return (
        outputs, grad_input, out_n1, out_s1, out_e1,
        added(1, first), added(0, first),
        out_n2, out_s2, out_e2, out_sc,
        added(1, later), added(0, later),
    )


def solution(mesh):
    wide = P(None, "batch", "rows", None, None)
    shard = P("rows", None)
    return jax.shard_map(
        shards,
        mesh=mesh,
        in_specs=(
            wide, P(None, "batch", None), shard, shard, shard, P(), P(),
            shard, shard, shard, shard, P(), P(), wide,
        ),
        out_specs=(
            wide, wide, shard, shard, shard, P(), P(),
            shard, shard, shard, shard, P(), P(),
        ),
        check_vma=False,
    )
```

```python
import functools

import jax
import jax.numpy as jnp
from jax import lax
from jax.experimental import pallas as pl
from jax.experimental.pallas import tpu as pltpu
from jax.sharding import PartitionSpec as P

SPILL = 12
WIN = 40
COLS = 16
EPS = 1e-05
AXES = ("rows", "batch")
BF = jnp.bfloat16
F32 = jnp.float32
CHUNK = 32
TANH_SCALE = 0.7978845608028654
TANH_CUBE = 0.044715


def gelu(x):
    t = jnp.tanh(x * (TANH_SCALE + TANH_SCALE * TANH_CUBE * (x * x)))
    return x * (0.5 + 0.5 * t)


def gelu_slope(x):
    square = x * x
    t = jnp.tanh(x * (TANH_SCALE + TANH_SCALE * TANH_CUBE * square))
    inner = x * (TANH_SCALE + 3.0 * TANH_SCALE * TANH_CUBE * square)
    return (0.5 + 0.5 * t) * (1.0 + inner * (1.0 - t))


def nn(a, b):
    return lax.dot_general(a, b, (((1,), (0,)), ((), ())), preferred_element_type=F32)


def nt(a, b):
    return lax.dot_general(a, b, (((1,), (1,)), ((), ())), preferred_element_type=F32)


def wide_of(ref):
    return ref[...].reshape(-1, ref.shape[-1])


def pick(ref, row, start=0, width=None):
    table = ref[:, start : start + (width or ref.shape[1])]
    rows = lax.broadcasted_iota(jnp.int32, table.shape, 0)
    return jnp.sum(jnp.where(rows == row, table, 0.0), axis=0, keepdims=True)


def moments(ref, m, population, start=0, width=None):
    share = 1.0 / population
    average = pick(ref, 2 * m, start, width) * share
    return average, lax.rsqrt(pick(ref, 2 * m + 1, start, width) * share - average * average + EPS)


def line(ref, m, population, gain, bias):
    average, inv = moments(ref, m, population)
    scale = inv * gain[...]
    return scale, bias[...] - average * scale


def back_line(ref, back, m, population, gain, start=0):
    average, inv = moments(ref, m, population)
    share = 1.0 / population
    width = ref.shape[1]
    mean_d = pick(back, 2 * m, start, width) * share
    mean_dn = pick(back, 2 * m + 1, start, width) * share
    by_d = gain[...] * inv
    by_p = -by_d * inv * mean_dn
    return by_d, by_p, -by_d * mean_d - by_p * average


def centred(ref, m, population, first, second):
    average, inv = moments(ref, m, population)
    first = jnp.sum(first, axis=0, keepdims=True)
    second = jnp.sum(second, axis=0, keepdims=True)
    return first, inv * (second - average * first)


def put_sums(ref, m, first, second, start=0):
    c = first.shape[1]
    at = slice(start, start + c)

    @pl.when(m == 0)
    def _():
        ref[:, at] = jnp.zeros((ref.shape[0], c), F32)

    first = jnp.sum(first, axis=0, keepdims=True)
    second = jnp.sum(second, axis=0, keepdims=True)
    rows = lax.broadcasted_iota(jnp.int32, (ref.shape[0], c), 0)
    ref[:, at] = jnp.where(rows == 2 * m, first, jnp.where(rows == 2 * m + 1, second, ref[:, at]))


def sweep(rows, c, vectors, body, sums=0, chunk=CHUNK, width=256):
    out = [[] for _ in range(sums)]
    for j in range(c // width):
        lanes = slice(j * width, (j + 1) * width)
        spread = [jnp.broadcast_to(v[:, lanes], (8, width))[None] for v in vectors]

        def step(i, carry):
            at = pl.ds(pl.multiple_of(i * chunk, chunk), chunk)
            return tuple(t + jnp.sum(v, axis=0) for t, v in zip(carry, body(at, lanes, spread) or ()))

        total = lax.fori_loop(0, rows // chunk, step, (jnp.zeros((8, width), F32),) * sums)
        for k in range(sums):
            out[k].append(total[k])
    return [jnp.concatenate(v, 1) for v in out]


def eight(x):
    return x.reshape(-1, 8, x.shape[-1])


def flat(x):
    return x.reshape(-1, x.shape[-1])


def get(ref, at, lanes):
    return eight(ref[0, at, lanes].astype(F32))


def get_mask(ref, at, lanes):
    m = eight(ref[0, at, :])
    times = (lanes.stop - lanes.start) // LANES
    return jnp.concatenate([m] * times, 2) if times > 1 else m


def put(ref, at, lanes, value):
    ref[0, at, lanes] = flat(value).astype(ref.dtype)


def count_up(ref, out_total, m, mask=None):
    def add(at, lanes, _):
        p = get(ref, at, lanes)
        q = p if mask is None else p * get_mask(mask, at, lanes)
        return q, q * p

    put_sums(out_total, m, *sweep(ref.shape[1], ref.shape[2], (), add, 2))


LANES = 128


def put_tall(ref, rows, value, first=0):
    for j in range(value.shape[1] // LANES):
        ref[first // LANES + j, rows, :] = value[:, j * LANES : (j + 1) * LANES]


def get_tall(ref, rows, lanes):
    return jnp.concatenate([ref[j, rows, :] for j in range(lanes.start // LANES, lanes.stop // LANES)], 1)


OWN, UPPER, LOWER, INNER = 0, 1, 2, 3


def lane(ref, which, rows):
    return ref[0, rows, which : which + 1]


def k_masks(own, anchor, kinds, mine_out, half_out, flags, inner):
    first = anchor[0]
    height_of = lambda m, v: 6 + 8 * kinds[m, 0, v]
    for m in range(flags.shape[0]):
        rows = flags.shape[1] // COLS
        row = first + lax.broadcasted_iota(jnp.int32, (rows, LANES), 0)

        def view(v, c):
            at, width, start, last = c
            height = height_of(m, v)
            inside = (row >= at) & (row < at + height)
            return (
                at + height,
                jnp.where(inside, height, width),
                jnp.where(inside, at, start),
                jnp.where(inside, at + height - 1, last),
            )

        zero = jnp.zeros((rows, LANES), jnp.int32)
        _, width, start, last = lax.fori_loop(0, kinds.shape[2], view, (jnp.int32(0), zero, zero, zero))
        owned = (start >= first) & (start < first + own) & (width > 0)
        mine = jnp.where(owned, width, 0)
        above = (start != row).astype(F32)
        below = (last != row).astype(F32)
        cells = lambda v, n: jnp.broadcast_to(v[:, None, :], (v.shape[0], n, LANES))
        shape = (rows, COLS, LANES)
        column = lax.broadcasted_iota(jnp.int32, shape, 1)
        lanes = lax.broadcasted_iota(jnp.int32, shape, 2)
        value = jnp.where(lanes == OWN, (column < cells(width, COLS)).astype(F32), 0.0)
        value = jnp.where(lanes == UPPER, cells(above, COLS), value)
        value = jnp.where(lanes == LOWER, cells(below, COLS), value)
        flags[m] = value.reshape(rows * COLS, LANES)
        mine_out[m] = (column < cells(mine, COLS)).astype(F32).reshape(rows * COLS, LANES)
        shape = (rows, COLS // 2, LANES)
        column = lax.broadcasted_iota(jnp.int32, shape, 1)
        even = lambda v: v.reshape(rows // 2, 2, COLS // 2, LANES)[:, 0].reshape(rows * COLS // 4, LANES)
        half_out[m] = even((2 * column < cells(mine, COLS // 2)).astype(F32))
        inner[m] = even(cells(above, COLS // 2))


def k_first(features, mask, weight, pre, head, total, rows):
    m = pl.program_id(0)
    own, across = features.shape[2], features.shape[3]

    @pl.when(m == 0)
    def _():
        rows[...] = jnp.zeros_like(rows)

    for r in range(own):
        rows[r * COLS : r * COLS + across, :] = features[0, 0, r]
    pre[0] = nn(rows[...] * lane(mask, OWN, slice(0, own * COLS)).astype(BF), weight[...])
    head[0] = pre[0, 0 : head.shape[1], :].astype(BF)

    count_up(pre, total, m)


def k_entry(features, mask, *refs):
    spills, (entry, rows) = refs[:-2], refs[-2:]
    m = pl.program_id(0)
    own, across = features.shape[2], features.shape[3]

    @pl.when(m == 0)
    def _():
        rows[...] = jnp.zeros_like(rows)

    for r in range(own):
        rows[r * COLS : r * COLS + across, :] = features[0, 0, r]
    for k, spill in enumerate(spills):

        @pl.when(m == k)
        def _():
            for r in range(spill.shape[0]):
                at = (own + r) * COLS
                rows[at : at + across, :] = spill[r]

    entry[0] = rows[...] * lane(mask, 0, slice(None)).astype(BF)


def join_pre_one(own, spill, pre, c):
    edge, more = own.shape[1], spill.shape[1]
    pre[0, 0:edge, :] = own[0]
    pre[0, edge : edge + more, :] = spill[0].astype(F32)
    pre[0, edge + more :, :] = jnp.zeros((pre.shape[1] - edge - more, c), F32)


def spread_trio(source, trio, cells):
    c = source.shape[1]
    trio[0:COLS, :] = jnp.zeros((COLS, 3 * c), BF)
    trio[COLS + cells : 2 * COLS + cells, :] = jnp.zeros((COLS, 3 * c), BF)
    for r in range(0, cells, CHUNK):
        for tap in range(3):
            part = source[COLS + r + tap - 1 : COLS + r + tap - 1 + CHUNK, :]
            trio[COLS + r : COLS + r + CHUNK, tap * c : (tap + 1) * c] = part.astype(BF)


def conv_rows(trio, flags, weight, cells):
    width = trio.shape[1]
    upper = lane(flags, UPPER, slice(None)).astype(BF)
    lower = lane(flags, LOWER, slice(None)).astype(BF)
    above = trio[0:cells, :] * upper
    here = trio[COLS : COLS + cells, :]
    below = trio[2 * COLS : 2 * COLS + cells, :] * lower
    total = (
        nn(above, weight[0:width, :])
        + nn(here, weight[width : 2 * width, :])
        + nn(below, weight[2 * width : 3 * width, :])
    )
    return total, (above, here, below)


def clear_ends(source, cells):
    c = source.shape[1]
    source[0:COLS, :] = jnp.zeros((COLS, c), F32)
    source[COLS + cells : 2 * COLS + cells, :] = jnp.zeros((COLS, c), F32)


def later(at, by):
    return pl.ds(pl.multiple_of(at.start + by, 8), at.size)


def k_second(count, own, spill, total, gain, bias, mask, flags, weight, pre, patch, out_total, act, trio, joined):
    m = pl.program_id(0)
    cells, c = mask.shape[1], own.shape[2]
    join_pre_one(own, spill, joined, c)
    clear_ends(act, cells)

    def step(at, lanes, v):
        x = get(joined, at, lanes) * v[0] + v[1]
        act[later(at, COLS), lanes] = flat(gelu(x) * get_mask(mask, at, lanes))

    sweep(cells, c, line(total, m, count, gain, bias), step)
    spread_trio(act, trio, cells)
    result, parts = conv_rows(trio, flags, weight, cells)
    pre[0] = result
    for k, part in enumerate(parts):
        patch[0, :, k * 3 * c : (k + 1) * 3 * c] = part
    count_up(pre, out_total, m, mask)


def k_third(count, pre_in, total, gain, bias, mask, weight, act, pre, out_total):
    m = pl.program_id(0)

    def step(at, lanes, v):
        x = get(pre_in, at, lanes) * v[0] + v[1]
        put(act, at, lanes, gelu(x) * get_mask(mask, at, lanes))

    sweep(pre_in.shape[1], pre_in.shape[2], line(total, m, count, gain, bias), step)
    pre[0] = nn(act[0], wide_of(weight)).astype(pre.dtype)
    count_up(pre, out_total, m)


def k_fourth(count, pre_in, entry, total, gain, bias, mask, weight, block, corner, slope, pre, out_total, full):
    m = pl.program_id(0)
    wide = COLS // 2
    chunk = 4 * COLS

    def step(at, lanes, v):
        x = get(pre_in, at, lanes) * v[0] + v[1] + get(entry, at, lanes)
        square = x * x
        t = jnp.tanh(x * (TANH_SCALE + TANH_SCALE * TANH_CUBE * square))
        inside = x * (TANH_SCALE + 3.0 * TANH_SCALE * TANH_CUBE * square)
        part = (0.5 + 0.5 * t) * get_mask(mask, at, lanes)
        y = x * part
        put(block, at, lanes, y)
        put(slope, at, lanes, part + part * inside * (1.0 - t))
        put_tall(full, slice(0, chunk), flat(y), lanes.start)
        pair = [get_tall(full, pl.ds(k * COLS, wide, stride=2), lanes) for k in (0, 2)]
        corner[0, pl.ds(pl.multiple_of(at.start // 4, COLS), COLS), lanes] = jnp.concatenate(pair, 0).astype(BF)

    sweep(pre_in.shape[1], pre_in.shape[2], line(total, m, count, gain, bias), step, chunk=chunk)
    pre[0] = nn(block[0], wide_of(weight)).astype(pre.dtype)
    count_up(pre, out_total, m)


def k_seventh(corner, weight, pre, out_total):
    micro, half, tile = pre.shape
    value = nn(corner[...].reshape(micro * half, -1), wide_of(weight))
    pre[...] = value.reshape(pre.shape).astype(pre.dtype)
    for m in range(micro):
        part = eight(value[m * half : (m + 1) * half])
        sums = [jnp.sum(v, axis=(0, 1))[None] for v in (part, part * part)]
        rows = lax.broadcasted_iota(jnp.int32, out_total.shape, 0)
        table = jnp.zeros_like(sums[0]) if m == 0 else out_total[...]
        out_total[...] = jnp.where(rows == 2 * m, sums[0], jnp.where(rows == 2 * m + 1, sums[1], table))


def k_fifth(count, pre_in, total, gain, bias, mask, half_mask, inner, weight, pre, patch, out_total, act, eo, oe, oo):
    m = pl.program_id(0)
    cells, c = pre_in.shape[1], pre_in.shape[2]
    half = cells // 4
    wide = COLS // 2

    def step(at, lanes, v):
        x = get(pre_in, at, lanes) * v[0] + v[1]
        put_tall(act, at, flat(gelu(x) * get_mask(mask, at, lanes)), lanes.start)

    sweep(cells, c, line(total, m, count, gain, bias), step)
    pad = 2 * wide
    for buf in (eo, oe, oo):
        buf[0:pad, :] = jnp.zeros((pad, c), F32)
    for j in range(c // LANES):
        lanes = slice(j * LANES, (j + 1) * LANES)
        even = act[j, pl.ds(0, cells // 2, stride=2), :].reshape(half // wide, 2, wide, LANES)
        odd = act[j, pl.ds(1, cells // 2, stride=2), :].reshape(half // wide, 2, wide, LANES)
        patch[0, :, 4 * c + j * LANES : 4 * c + (j + 1) * LANES] = even[:, 0].reshape(half, LANES).astype(BF)
        oe[pad : pad + half, lanes] = even[:, 1].reshape(half, LANES)
        eo[pad : pad + half, lanes] = odd[:, 0].reshape(half, LANES)
        oo[pad : pad + half, lanes] = odd[:, 1].reshape(half, LANES)
    first = jnp.concatenate([inner[0]] * (c // LANES), 1)
    take = lambda buf, back: buf[pad - back : pad - back + half, :]
    taps = (
        take(oo, wide + 1) * first, take(oe, wide) * first, take(oo, wide) * first,
        take(eo, 1), None, take(eo, 0),
        take(oo, 1), take(oe, 0), take(oo, 0),
    )
    for k, tap in enumerate(taps):
        if tap is not None:
            patch[0, :, k * c : (k + 1) * c] = tap.astype(BF)
    pre[0] = nn(patch[0], wide_of(weight))
    count_up(pre, out_total, m, half_mask)


def k_last(count, six, seven, tot6, tot7, g6, b6, g7, b7, half_mask, cot, out, slope, total, row):
    m = pl.program_id(0)
    half, c = six.shape[1], six.shape[2]
    wide = COLS // 2
    shown, across = out.shape[2], out.shape[3]
    scale6, shift6 = line(tot6, m, count, g6, b6)
    scale7, shift7 = line(tot7, m, count, g7, b7)
    row[...] = jnp.zeros_like(row)

    def step(at, lanes, v):
        p = 2 * (at.start // (2 * wide))
        mask = get_mask(half_mask, at, lanes)
        s6, s7 = get(six, at, lanes), get(seven, at, lanes)
        joined = s6 * v[0] + s7 * v[1] + v[2]
        square = joined * joined
        t = jnp.tanh(joined * (TANH_SCALE + TANH_SCALE * TANH_CUBE * square))
        inside = joined * (TANH_SCALE + 3.0 * TANH_SCALE * TANH_CUBE * square)
        part = (0.5 + 0.5 * t) * mask
        result = flat(joined * part)
        for k in range(2):
            q = jnp.minimum(p + k, shown - 1)
            if shown % 2 == 0 or k == 0:
                out[0, 0, q, :, lanes] = result[k * wide : k * wide + across].astype(BF)
            else:

                @pl.when(p + k < shown)
                def _():
                    out[0, 0, q, :, lanes] = result[k * wide : k * wide + across].astype(BF)

            row[k * wide : k * wide + across, lanes] = cot[0, 0, q, :, lanes].astype(F32)
        d = part * (1.0 + inside * (1.0 - t)) * eight(row[:, lanes])
        put(slope, at, lanes, d)
        return d, d * s6, d * s7

    sums = sweep(half, c, (scale6, scale7, shift6 + shift7), step, 3, chunk=2 * wide, width=512)
    put_sums(total, m, *centred(tot6, m, count, sums[0], sums[1]))
    put_sums(total, m, *centred(tot7, m, count, sums[0], sums[2]), c)


def slope_sums(d_out, pre, tot, m, population, gain, bias, mask, out_total, more=None):
    def add(at, lanes, v):
        p = get(pre, at, lanes)
        d = gelu_slope(p * v[0] + v[1]) * get(d_out, at, lanes) * get_mask(mask, at, lanes)
        put(d_out, at, lanes, d)
        return d, d * p

    sums = sweep(pre.shape[1], pre.shape[2], line(tot, m, population, gain, bias), add, 2)
    put_sums(out_total, m, *centred(tot, m, population, *sums))


def norm_back(d_pre, d, pre, tot, back, m, population, gain, mask):
    def step(at, lanes, v):
        value = get(d, at, lanes) * v[0] + get(pre, at, lanes) * v[1] + v[2]
        put(d_pre, at, lanes, value * get_mask(mask, at, lanes))

    sweep(pre.shape[1], pre.shape[2], back_line(tot, back, m, population, gain), step)


def k_back_six(
    count, slope, six, seven, tot6, tot7, back, g6, g7, five, tot5, g5, b5, half_mask, weight,
    d_six, d_seven, d_five, out_total,
):
    m = pl.program_id(0)
    half, c = six.shape[1], six.shape[2]

    def step(at, lanes, v):
        d = get(slope, at, lanes)
        mask = get_mask(half_mask, at, lanes)
        put(d_six, at, lanes, (d * v[0] + get(six, at, lanes) * v[1] + v[2]) * mask)
        put(d_seven, at, lanes, (d * v[3] + get(seven, at, lanes) * v[4] + v[5]) * mask)

    vectors = back_line(tot6, back, m, count, g6) + back_line(tot7, back, m, count, g7, c)
    sweep(half, c, vectors, step)
    d_five[0] = nt(d_six[0], wide_of(weight))
    slope_sums(d_five, five, tot5, m, count, g5, b5, half_mask, out_total)


def k_corner(d_seven, weight, d_corner):
    d_corner[0] = nt(d_seven[0], wide_of(weight)).astype(d_corner.dtype)


def k_back_five(
    half_count, full_count, d_five, five, tot5, back5, g5, half_mask, inner, weight, four, tot4, g4, b4, mask,
    d_pre, d_four, out_total, grid_scratch, shifted,
):
    m = pl.program_id(0)
    half, c = five.shape[1], five.shape[2]
    cells = 4 * half
    wide = COLS // 2
    norm_back(d_pre, d_five, five, tot5, back5, m, half_count, g5, half_mask)
    d = d_pre[0]
    wide_d = d.astype(F32)
    tail = 2 * wide
    shifted[half : half + tail, :] = jnp.zeros((tail, c), F32)
    shifted[0:half, :] = wide_d
    right = shifted[1 : 1 + half, :].astype(BF)
    shifted[0:half, :] = wide_d * jnp.concatenate([inner[0]] * (c // LANES), 1)
    down = shifted[wide : wide + half, :].astype(BF)
    down_right = shifted[wide + 1 : wide + 1 + half, :].astype(BF)
    taps = wide_of(weight)
    w = lambda tap: taps[tap * c : (tap + 1) * c]
    ee = nt(d, w(4))
    eo = nt(d, w(5)) + nt(right, w(3))
    oe = nt(d, w(7)) + nt(down, w(1))
    oo = nt(d, w(8)) + nt(right, w(6)) + nt(down, w(2)) + nt(down_right, w(0))
    rows = half // wide
    even = jnp.stack([ee.reshape(rows, wide, c), oe.reshape(rows, wide, c)], 1).reshape(cells // 2, c)
    odd = jnp.stack([eo.reshape(rows, wide, c), oo.reshape(rows, wide, c)], 1).reshape(cells // 2, c)
    put_tall(grid_scratch, pl.ds(0, cells // 2, stride=2), even)
    put_tall(grid_scratch, pl.ds(1, cells // 2, stride=2), odd)

    def add(at, lanes, v):
        p = get(four, at, lanes)
        got = eight(get_tall(grid_scratch, at, lanes))
        d = gelu_slope(p * v[0] + v[1]) * got * get_mask(mask, at, lanes)
        put(d_four, at, lanes, d)
        return d, d * p

    sums = sweep(cells, c, line(tot4, m, full_count, g4, b4), add, 2)
    put_sums(out_total, m, *centred(tot4, m, full_count, *sums))


def k_back_four(
    count, d_four, four, tot4, back4, g4, mask, weight, d_corner, three, slope, tot3,
    d_pre, d_summed, out_total, placed, d_block,
):
    m = pl.program_id(0)
    cells, c = three.shape[1], three.shape[2]
    norm_back(d_pre, d_four, four, tot4, back4, m, count, g4, mask)
    d_block[0] = nt(d_pre[0], wide_of(weight))
    wide = COLS // 2
    placed[...] = jnp.zeros_like(placed)

    def add(at, lanes, v):
        corner_at = pl.ds(pl.multiple_of(at.start // 4, COLS), COLS)
        value = d_corner[0, corner_at, lanes].astype(F32)
        for k in range(2):
            rows = pl.ds(2 * k * COLS, wide, stride=2)
            put_tall(placed, rows, value[k * wide : (k + 1) * wide], lanes.start)
        got = get(d_block, at, lanes) + eight(get_tall(placed, slice(0, 4 * COLS), lanes))
        d = get(slope, at, lanes) * got
        put(d_summed, at, lanes, d)
        return d, d * get(three, at, lanes)

    sums = sweep(cells, c, (), add, 2, chunk=4 * COLS)
    put_sums(out_total, m, *centred(tot3, m, count, *sums))


def k_back_three(count, d_summed, three, tot3, back3, g3, mask, weight, two, tot2, g2, b2, d_pre, d_two, out_total):
    m = pl.program_id(0)
    norm_back(d_pre, d_summed, three, tot3, back3, m, count, g3, mask)
    d_two[0] = nt(d_pre[0], wide_of(weight))
    slope_sums(d_two, two, tot2, m, count, g2, b2, mask, out_total)


def k_back_two(
    count, d_two, two, tot2, back2, g2, mask, flags, weight, own, spill, tot1, g1, b1,
    d_pre, d_one, out_total, source, trio, joined,
):
    m = pl.program_id(0)
    cells, c = two.shape[1], two.shape[2]
    clear_ends(source, cells)

    def step(at, lanes, v):
        value = get(d_two, at, lanes) * v[0] + get(two, at, lanes) * v[1] + v[2]
        value = value * get_mask(mask, at, lanes)
        put(d_pre, at, lanes, value)
        source[later(at, COLS), lanes] = flat(value)

    sweep(cells, c, back_line(tot2, back2, m, count, g2), step)
    spread_trio(source, trio, cells)
    upper = lane(flags, UPPER, slice(None)).astype(BF)
    lower = lane(flags, LOWER, slice(None)).astype(BF)
    shifted = (
        trio[0:cells, :] * upper,
        trio[COLS : COLS + cells, :],
        trio[2 * COLS : 2 * COLS + cells, :] * lower,
    )
    tap = lambda k: nt(shifted[k // 3][:, k % 3 * c : (k % 3 + 1) * c], weight[(8 - k) * c : (9 - k) * c, :])
    d_one[0] = sum((tap(k) for k in range(1, 9)), tap(0))
    join_pre_one(own, spill, joined, c)
    slope_sums(d_one, joined, tot1, m, count, g1, b1, mask, out_total)


def k_back_one(count, d_one, own, spill, tot1, back1, g1, mask, d_pre, joined):
    m = pl.program_id(0)
    join_pre_one(own, spill, joined, d_one.shape[2])
    norm_back(d_pre, d_one, joined, tot1, back1, m, count, g1, mask)


def k_input(d_pre, more_pre, d_summed, weight, *refs):
    more_summed, (out, both, sums) = refs[:-3], refs[-3:]
    m = pl.program_id(0)
    spilled, cells = more_pre.shape[1], both.shape[0]
    blocks = sums.shape[1] // LANES
    own = cells // COLS
    across = out.shape[1] // blocks // own
    both[...] = d_pre[0, 0:cells, :]
    both[0:spilled, :] = d_pre[0, 0:spilled, :] + more_pre[0]
    sums[...] = nt(both[...], weight[...])
    for r in range(own):
        at = r * COLS
        value = sums[at : at + COLS, :] + d_summed[0, at : at + COLS, :].astype(F32)
        if at < spilled:
            extra = more_summed[0][at : at + COLS, :].astype(F32)
            for k in range(1, len(more_summed)):
                extra = jnp.where(m == k, more_summed[k][at : at + COLS, :].astype(F32), extra)
            value = value + extra
        for j in range(blocks):
            rows = pl.ds(r * across * blocks + j, across, stride=blocks)
            out[0, rows, :] = value[:across, j * LANES : (j + 1) * LANES]


def exchange(x, mask):
    total = lax.axis_size("rows") * lax.axis_size("batch")
    return lax.ppermute(x, AXES, [(i, i ^ mask) for i in range(total)])


def from_behind(x, by):
    devices = lax.axis_size("rows")
    pairs = [(i, i + by) for i in range(devices) if 0 <= i + by < devices]
    return lax.ppermute(x, "rows", pairs)


class Chain:
    def __init__(self, steps):
        self.steps, self.flying, self.done, self.result = steps, None, False, None
        self.ready = next(steps)

    def launch(self, array):
        self.flying = self.ready[1](array)

    def land(self):
        try:
            self.ready = self.steps.send(self.flying)
        except StopIteration as end:
            self.done, self.result = True, end.value
        self.flying = None

    def value(self):
        while not self.done:
            if self.flying is None:
                self.launch(self.ready[0])
            self.land()
        return self.result


def hook(x, start=(), finish=(), need=()):
    if not (start or finish or need):
        return x
    landed = []
    for chain in finish:
        if not chain.done:
            landed.append(chain.flying)
            chain.land()
    live = [chain for chain in start if not chain.done]
    tied = lax.optimization_barrier((x, [c.ready[0] for c in live], landed, list(need)))
    for chain, array in zip(live, tied[1]):
        chain.launch(array)
    return tied[0]


def global_sum(x, b=None, c=None, d=None):
    bits = device_bits()
    split = x.shape[1] >= 2048
    if split:
        half = x.shape[1] // 2
        part = lambda bit: lax.dynamic_slice_in_dim(x, bit * half, half, 1)
        x = part(my_bit(0)) + exchange(part(1 - my_bit(0)), 1)
    else:
        x = x + exchange(x, 1)
    x = hook(x, **(b or {}))
    step = 1
    while step < bits:
        low = 1 << step
        if step + 1 < bits:
            p, q, r = exchange(x, low), exchange(x, 2 * low), exchange(x, 3 * low)
            x = (x + p) + (q + r)
        else:
            x = x + exchange(x, low)
        if step == 1:
            x = hook(x, **(c or {}))
        step += 2
    if split:
        other = exchange(x, 1)
        upper = my_bit(0) == 1
        x = jnp.concatenate([jnp.where(upper, other, x), jnp.where(upper, x, other)], 1)
    return hook(x, **(d or {}))


def device_bits():
    total = lax.axis_size("rows") * lax.axis_size("batch")
    return total.bit_length() - 1


def my_bit(bit):
    number = lax.axis_index("rows") * lax.axis_size("batch") + lax.axis_index("batch")
    return (number >> bit) & 1


def batch_bits():
    return lax.axis_size("batch").bit_length() - 1


def across(bit):
    return lambda x: exchange(x, 1 << bit)


def lanes_of(w, parts, wide=256):
    x = w.reshape(parts, -1, w.shape[1] // wide, wide)
    return x.transpose(0, 2, 1, 3).reshape(parts, -1, wide)


def from_lanes(x, c):
    parts, wide = x.shape[0], x.shape[2]
    x = x.reshape(parts, c // wide, -1, wide)
    return x.transpose(0, 2, 1, 3).reshape(-1, c)


def ordered(mine, other, bit, axis):
    upper = my_bit(bit) == 1
    return jnp.stack([jnp.where(upper, other, mine), jnp.where(upper, mine, other)], axis)


def gather_steps(packed, parts):
    bits, low = device_bits(), batch_bits()
    number = my_bit(0) if parts == 1 else lax.axis_index("batch")
    x = lax.dynamic_index_in_dim(packed, number, 0, keepdims=False)
    for bit in list(reversed(range(low, bits))) + list(reversed(range(parts))):
        got = yield x, across(bit)
        x = ordered(x, got, bit, x.ndim - 2)
    return x.reshape((-1,) + x.shape[-2:])


def gather_offloaded(ws):
    quarters, wide = lax.axis_size("batch"), ws[0].shape[1]
    packed = jnp.concatenate([w.reshape(quarters, -1, wide) for w in ws], 1)
    part = lax.dynamic_index_in_dim(packed, lax.axis_index("batch"), 0, keepdims=False)
    whole = lax.all_gather(part, AXES, axis=0)
    out, at = [], 0
    for w in ws:
        n = w.shape[0] // quarters
        if n % 16 == 0 and at % n == 0:
            block = at // n
            spec = pl.BlockSpec(
                (whole.shape[0], n, wide), lambda m, k=block: (0, k, 0), pipeline_mode=pl.Buffered(1)
            )
            out.append((whole, spec))
        else:
            part = whole[:, at : at + n].reshape(-1, wide)
            out.append((part, pl.BlockSpec(part.shape, lambda m: (0, 0), pipeline_mode=pl.Buffered(1))))
        at += n
    return out


def sharded(grad, c):
    total = lax.axis_size("rows") * lax.axis_size("batch")
    if grad.shape[1] == c:
        return grad.reshape(total, -1, c)
    return lanes_of(grad, total)


def spread_steps(x):
    for bit in reversed(range(batch_bits())):
        got = yield x, across(bit)
        x = ordered(x, got, bit, x.ndim - 2)
    return x.reshape((-1,) + x.shape[-2:])


def reduce_scattered(part, order):
    bits = device_bits()
    x = part.reshape((2,) * bits + part.shape[1:])
    left = list(reversed(range(bits)))
    got = None
    for bit in order:
        axis = left.index(bit)
        left.remove(bit)
        half = lambda v, b: lax.dynamic_index_in_dim(v, b, axis, keepdims=False)
        keep, send = my_bit(bit), 1 - my_bit(bit)
        if got is None:
            x, give = half(x, keep), half(x, send)
        else:
            x, give = half(x, keep) + half(got, keep), half(x, send) + half(got, send)
        got = yield give, across(bit)
    return x + got


def lanes_back(filter_and_spec, c):
    whole, spec = filter_and_spec
    if whole.ndim == 3:
        n, k = spec.block_shape[1], spec.index_map(0)[1]
        return from_lanes(whole[:, k * n : (k + 1) * n], c)
    return from_lanes(whole.reshape(lax.axis_size("rows") * lax.axis_size("batch"), -1, whole.shape[1]), c)


def reduce_first(part):
    bits, low = device_bits(), batch_bits()
    x = part.reshape((2,) * bits + part.shape[1:])
    left = list(reversed(range(bits)))
    got = None
    for bit in [0] + list(range(low, bits - 1)):
        axis = left.index(bit)
        left.remove(bit)
        half = lambda v, b: lax.dynamic_index_in_dim(v, b, axis, keepdims=False)
        keep, send = my_bit(bit), 1 - my_bit(bit)
        if got is None:
            x, give = half(x, keep), half(x, send)
        else:
            x, give = half(x, keep) + half(got, keep), half(x, send) + half(got, send)
        got = yield give, across(bit)
    return x + got


def reduce_last(x):
    low, last = batch_bits(), device_bits() - 1
    bit = my_bit(last)
    half = lambda b: lax.dynamic_index_in_dim(x, b, 0, keepdims=False)
    got = yield half(1 - bit), across(last)
    x = half(bit) + got
    for b in range(1, low):
        got = yield x, across(b)
        x = x + got
    got = yield x, across(0)
    x = ordered(x, got, 0, x.ndim - 2)
    return x.reshape((-1,) + x.shape[-2:])


def one_step(x, send):
    return (yield x, send)


def unpack(shard, shapes):
    devices = lax.axis_size("rows")
    out, at = [], 0
    for k, c in shapes:
        n = k * c // devices // shard.shape[0] // shard.shape[2]
        part = shard[:, at : at + n]
        out.append((from_lanes(part, c) if shard.shape[2] != c else part.reshape(-1, c)).astype(F32))
        at += n
    return out


LIMIT = 16


def per_micro(shape):
    zeros = (0,) * (len(shape) - 1)
    return pl.BlockSpec((1,) + tuple(shape[1:]), lambda m: (m,) + zeros)


def whole(shape):
    zeros = (0,) * len(shape)
    return pl.BlockSpec(tuple(shape), lambda m: zeros, pipeline_mode=pl.Buffered(1))


def table(shape):
    zeros = (0,) * len(shape)
    return pl.BlockSpec(tuple(shape), lambda m: zeros)


def call(kernel, micro, ins, outs, scratch=(), limit=LIMIT, after=()):
    kind = {"m": per_micro, "w": whole, "s": lambda shape: pl.BlockSpec(memory_space=pltpu.SMEM)}
    in_specs = [k if isinstance(k, pl.BlockSpec) else kind[k](a.shape) for a, k in ins]
    in_specs += [pl.BlockSpec(memory_space=pl.ANY)] * len(after)
    out_specs = [per_micro(sh) if k == "m" else table(sh) for sh, _, k in outs]

    def run(*refs):
        kernel(*refs[: len(ins)], *refs[len(ins) + len(after) :])

    return pl.pallas_call(
        run,
        grid=(micro,),
        in_specs=in_specs,
        out_specs=out_specs,
        out_shape=[jax.ShapeDtypeStruct(sh, t) for sh, t, _ in outs],
        scratch_shapes=[pltpu.VMEM(sh, t) for sh, t in scratch],
        compiler_params=pltpu.CompilerParams(
            dimension_semantics=("arbitrary",), vmem_limit_bytes=limit * 1024 * 1024
        ),
        name=getattr(kernel, "func", kernel).__name__,
    )(*[a for a, _ in ins], *after)


def weight_term(left, right):
    k, n = left.shape[-1], right.shape[-1]
    return lax.dot_general(
        left.reshape(-1, k), right.reshape(-1, n), (((0,), (0,)), ((), ())), preferred_element_type=F32
    ).astype(BF)


def shards(
    features, view_kind, narrow_one, spatial_one, expand_one, gains_one, biases_one,
    narrow_two, spatial_two, expand_two, shortcut, gains_two, biases_two, cotangent,
):
    micro, _, own, across, channels = features.shape
    m1 = spatial_one.shape[1]
    m2 = spatial_two.shape[1]
    outward = shortcut.shape[1]
    sources = lax.axis_size("rows") * own // 52
    full_count = float(lax.axis_size("batch") * sources * 536)
    half_count = float(lax.axis_size("batch") * sources * 134)
    anchor = lax.axis_index("rows") * own
    cells, half = WIN * COLS, WIN * COLS // 4
    mine, more = own * COLS, SPILL * COLS

    chain_n1 = Chain(gather_steps(narrow_one.reshape(2, -1, m1), 1))
    chain_a = Chain(gather_steps(spatial_one.reshape(4, -1, m1), 2))
    thin = [lanes_of(expand_one, 4, m2).reshape(-1, m2)]
    spatial_b, narrow_b, thin_a = gather_offloaded([spatial_two, narrow_two] + thin)
    expand_a = lanes_back(thin_a, channels)
    bypass, expand_b = gather_offloaded([shortcut, expand_two])
    chain_f = [
        Chain(one_step(features[k, 0, :SPILL], lambda x: from_behind(x, -1))) for k in range(micro)
    ]
    g1, g2, g3 = (v[None] for v in jnp.split(gains_one, [m1, 2 * m1]))
    b1, b2, b3 = (v[None] for v in jnp.split(biases_one, [m1, 2 * m1]))
    cuts = [m2, 2 * m2, 2 * m2 + outward]
    g4, g5, g6, g7 = (v[None] for v in jnp.split(gains_two, cuts))
    b4, b5, b6, b7 = (v[None] for v in jnp.split(biases_two, cuts))
    mask, half_mask, flags, inner = pl.pallas_call(
        functools.partial(k_masks, own),
        in_specs=[pl.BlockSpec(memory_space=pltpu.SMEM)] * 2,
        out_shape=[
            jax.ShapeDtypeStruct((micro, cells, LANES), F32),
            jax.ShapeDtypeStruct((micro, half, LANES), F32),
        ]
        * 2,
        name="k_masks",
    )(anchor[None].astype(jnp.int32), view_kind)

    full_table = lambda c: ((8, c), F32, "t")
    per = lambda c, t=F32, n=cells: ((micro, n, c), t, "m")

    for chain in (chain_n1, chain_a):
        chain.launch(chain.ready[0])
    chain_n1.land()
    before = [mask]
    while not chain_n1.done:
        chain_n1.launch(lax.optimization_barrier((chain_n1.ready[0], before))[0])
        landed = chain_n1.flying
        chain_n1.land()
        if chain_a.flying is not None and len(before) < 3 and not chain_n1.done:
            chain_a.land()
            chain_a.launch(lax.optimization_barrier((chain_a.ready[0], landed))[0])
            before = before + [landed]
            if len(before) == 3:
                hook(landed, start=chain_f)
    narrow_a = chain_n1.value().reshape(-1, m1)
    pre_one, head, t1 = call(
        k_first, micro, [(features, "m"), (flags, "m"), (narrow_a, "w")],
        [per(m1, F32, mine), per(m1, BF, more), full_table(m1)], [((mine, channels), BF)],
    )
    chain_h = Chain(one_step(head, lambda x: from_behind(x, -1)))
    t1 = global_sum(
        t1,
        b=dict(finish=[chain_a]),
        c=dict(start=[chain_a, chain_h]),
        d=dict(finish=[chain_a, chain_h], start=[chain_a]),
    )
    pre_spill = chain_h.value()
    spatial_a = chain_a.value().reshape(-1, m1)
    pre_two, patch_one, t2 = call(
        functools.partial(k_second, full_count), micro,
        [(pre_one, "m"), (pre_spill, "m"), (t1, "w"), (g1, "w"), (b1, "w"), (mask, "m"),
         (flags, "m"), (spatial_a, "w")],
        [per(m1), per(9 * m1, BF), full_table(m1)],
        [((cells + 2 * COLS, m1), F32), ((cells + 2 * COLS, 3 * m1), BF), ((1, cells, m1), F32)],
        limit=20,
    )
    (entry,) = call(
        k_entry, micro,
        [(features, "m"), (mask, "m")] + [(f.value(), "w") for f in chain_f],
        [per(channels, BF)], [((cells, channels), BF)],
    )
    t2 = global_sum(t2, c=dict(need=[entry]))
    act_two, pre_three, t3 = call(
        functools.partial(k_third, full_count), micro,
        [(pre_two, "m"), (t2, "w"), (g2, "w"), (b2, "w"), (mask, "m"), (expand_a, "w")],
        [per(m1, BF), per(channels, BF), full_table(channels)],
    )
    t3 = global_sum(t3)
    block_out, corner, slope_three, pre_four, t4 = call(
        functools.partial(k_fourth, full_count), micro,
        [(pre_three, "m"), (entry, "m"), (t3, "w"), (g3, "w"), (b3, "w"), (mask, "m"), narrow_b],
        [per(channels, BF), per(channels, BF, half), per(channels, BF), per(m2, BF), full_table(m2)],
        [((channels // LANES, 4 * COLS, LANES), F32)],
    )
    t4 = global_sum(t4)
    pre_five, patch_two, t5 = call(
        functools.partial(k_fifth, full_count), micro,
        [(pre_four, "m"), (t4, "w"), (g4, "w"), (b4, "w"), (mask, "m"), (half_mask, "m"), (inner, "m"),
         spatial_b],
        [per(m2, F32, half), per(9 * m2, BF, half), full_table(m2)],
        [((m2 // LANES, cells, LANES), F32)] + [((half + COLS, m2), F32)] * 3,
        limit=20,
    )
    t5 = global_sum(t5)
    act_five, pre_six, t6 = call(
        functools.partial(k_third, half_count), micro,
        [(pre_five, "m"), (t5, "w"), (g5, "w"), (b5, "w"), (half_mask, "m"), expand_b],
        [per(m2, BF, half), per(outward, BF, half), full_table(outward)],
    )
    tile = outward // 4
    by_tile = bypass[1].block_shape[:-1] + (tile,)
    pre_seven, t7 = pl.pallas_call(
        k_seventh,
        grid=(4,),
        in_specs=[
            pl.BlockSpec(corner.shape, lambda n: (0, 0, 0)),
            pl.BlockSpec(by_tile, lambda n: (0,) * (len(by_tile) - 1) + (n,)),
        ],
        out_specs=[
            pl.BlockSpec((micro, half, tile), lambda n: (0, 0, n)),
            pl.BlockSpec((8, tile), lambda n: (0, n)),
        ],
        out_shape=[
            jax.ShapeDtypeStruct((micro, half, outward), BF),
            jax.ShapeDtypeStruct((8, outward), F32),
        ],
        compiler_params=pltpu.CompilerParams(vmem_limit_bytes=LIMIT * 1024 * 1024),
        name="k_seventh",
    )(corner, bypass[0])
    t67 = global_sum(jnp.concatenate([t6, t7], 1))
    t6, t7 = t67[:, :outward], t67[:, outward:]
    outputs, slope, u67 = call(
        functools.partial(k_last, half_count), micro,
        [(pre_six, "m"), (pre_seven, "m"), (t6, "w"), (t7, "w"), (g6, "w"), (b6, "w"), (g7, "w"), (b7, "w"),
         (half_mask, "m"), (cotangent, "m")],
        [(cotangent.shape, BF, "m"), per(outward, BF, half), full_table(2 * outward)],
        [((COLS, outward), F32)],
    )
    u67 = global_sum(u67)
    d_six, d_seven, d_five, u5 = call(
        functools.partial(k_back_six, half_count), micro,
        [(slope, "m"), (pre_six, "m"), (pre_seven, "m"), (t6, "w"), (t7, "w"), (u67, "w"), (g6, "w"), (g7, "w"),
         (pre_five, "m"), (t5, "w"), (g5, "w"), (b5, "w"), (half_mask, "m"), expand_b],
        [per(outward, BF, half), per(outward, BF, half), per(m2, F32, half), full_table(m2)],
    )
    (d_corner,) = call(
        k_corner, micro, [(d_seven, "m"), bypass], [per(channels, BF, half)]
    )
    grad_e2 = weight_term(act_five, d_six)
    grad_sc = weight_term(corner, d_seven)
    pack_b = jnp.concatenate([sharded(grad_sc, outward), sharded(grad_e2, outward)], 1).reshape(-1, outward)
    u5 = global_sum(u5, c=dict(need=[pack_b]))
    part_b = lax.psum_scatter(pack_b, AXES, scatter_dimension=0, tiled=True)
    d_pre_five, d_four, u4 = call(
        functools.partial(k_back_five, half_count, full_count), micro,
        [(d_five, "m"), (pre_five, "m"), (t5, "w"), (u5, "w"), (g5, "w"), (half_mask, "m"), (inner, "m"),
         spatial_b, (pre_four, "m"), (t4, "w"), (g4, "w"), (b4, "w"), (mask, "m")],
        [per(m2, BF, half), per(m2), full_table(m2)],
        [((m2 // LANES, cells, LANES), F32), ((half + COLS, m2), F32)],
        limit=22,
    )
    grad_s2 = sharded(weight_term(patch_two, d_pre_five), m2)
    cut = grad_s2.shape[1] // 32 * 16 or grad_s2.shape[1] // 2
    low = batch_bits()
    chain_rs = [
        Chain(reduce_scattered(grad_s2[:, :cut], list(range(device_bits())))),
        Chain(reduce_scattered(grad_s2[:, cut:], [0, low] + list(range(1, low)) + list(range(low + 1, device_bits())))),
    ]
    u4 = global_sum(u4, b=dict(start=chain_rs), c=dict(finish=chain_rs, start=chain_rs))
    d_pre_four, d_summed, u3 = call(
        functools.partial(k_back_four, full_count), micro,
        [(d_four, "m"), (pre_four, "m"), (t4, "w"), (u4, "w"), (g4, "w"), (mask, "m"), narrow_b,
         (d_corner, "m"), (pre_three, "m"), (slope_three, "m"), (t3, "w")],
        [per(m2, BF), per(channels, BF), full_table(channels)],
        [((channels // LANES, 4 * COLS, LANES), F32), ((1, cells, channels), F32)],
        limit=24,
    )
    grad_n2 = [
        sharded(weight_term(block_out, d_pre_four[..., k : k + 256]), 256) for k in range(0, m2, 256)
    ]
    spilled = d_summed[:, mine : mine + more]
    chain_ds = [Chain(one_step(spilled[k], lambda x: from_behind(x, 1))) for k in range(micro)]
    chain_r2 = Chain(reduce_first(jnp.concatenate(grad_n2, 1)))
    u3 = global_sum(
        u3,
        b=dict(start=[chain_r2]),
        c=dict(finish=chain_rs + [chain_r2], start=chain_rs + [chain_r2]),
    )
    d_pre_three, d_two, u2 = call(
        functools.partial(k_back_three, full_count), micro,
        [(d_summed, "m"), (pre_three, "m"), (t3, "w"), (u3, "w"), (g3, "w"), (mask, "m"), (expand_a, "w"),
         (pre_two, "m"), (t2, "w"), (g2, "w"), (b2, "w")],
        [per(channels, BF), per(m1), full_table(m1)],
    )
    grad_e1 = weight_term(act_two, d_pre_three)
    chain_r3 = Chain(reduce_first(sharded(grad_e1, 256)))
    u2 = global_sum(
        u2,
        b=dict(finish=[chain_r2], start=[chain_r3]),
        c=dict(finish=chain_rs + [chain_r3], start=[chain_r3]),
        d=dict(start=chain_rs + [chain_r2]),
    )
    d_pre_two, d_one, u1 = call(
        functools.partial(k_back_two, full_count), micro,
        [(d_two, "m"), (pre_two, "m"), (t2, "w"), (u2, "w"), (g2, "w"), (mask, "m"), (flags, "m"),
         (spatial_a, "w"), (pre_one, "m"), (pre_spill, "m"), (t1, "w"), (g1, "w"), (b1, "w")],
        [per(m1, BF), per(m1), full_table(m1)],
        [((cells + 2 * COLS, m1), F32), ((cells + 2 * COLS, 3 * m1), BF), ((1, cells, m1), F32)],
        limit=20,
    )
    grad_s1 = weight_term(patch_one, d_pre_two)
    chain_r1 = Chain(reduce_first(sharded(grad_s1, 256)))
    u1 = global_sum(
        u1,
        b=dict(finish=[chain_r3], start=[chain_r1]),
        c=dict(finish=chain_rs + [chain_r2, chain_r1], start=[chain_r1]),
        d=dict(start=chain_rs + [chain_r3] + chain_ds[:1]),
    )
    (d_pre_one,) = call(
        functools.partial(k_back_one, full_count), micro,
        [(d_one, "m"), (pre_one, "m"), (pre_spill, "m"), (t1, "w"), (u1, "w"), (g1, "w"), (mask, "m")],
        [per(m1, BF)], [((1, cells, m1), F32)],
    )
    chain_rn = Chain(reduce_first(sharded(weight_term(entry, d_pre_one), 256)))
    chain_rb = Chain(spread_steps(part_b))
    chain_rn.launch(chain_rn.ready[0])
    landed = chain_rn.flying
    chain_rn.land()
    hook(landed, finish=[chain_r1], start=[chain_r1])
    while not chain_rn.done:
        chain_rn.launch(chain_rn.ready[0])
        landed = chain_rn.flying
        chain_rn.land()
    firsts = [c.value() for c in (chain_rn, chain_r1, chain_r2, chain_r3)]
    chain_last = Chain(reduce_last(jnp.concatenate(firsts, -2)))
    chain_dp = Chain(one_step(d_pre_one[:, mine : mine + more], lambda x: from_behind(x, 1)))
    chain_last.launch(chain_last.ready[0])
    landed = chain_last.flying
    chain_last.land()
    hook(landed, start=[chain_dp] + chain_ds[1:])
    chain_r4 = Chain(spread_steps(jnp.concatenate([c.value() for c in chain_rs], 0)))
    hook(landed, start=[chain_rb, chain_r4])
    chain_last.launch(chain_last.ready[0])
    landed = chain_last.flying
    chain_last.land()
    out_n1, out_s1, out_n2, out_e1 = unpack(
        chain_last.value(), [(channels, m1), (9 * m1, m1), (channels, m2), (m1, channels)]
    )
    (out_s2,) = unpack(chain_r4.value(), [(9 * m2, m2)])
    out_sc, out_e2 = unpack(chain_rb.value(), [(channels, outward), (m2, outward)])
    (grad_input,) = call(
        k_input, micro,
        [(d_pre_one, "m"), (chain_dp.value(), "m"), (d_summed, "m"), (narrow_a, "w")]
        + [(c.value(), "w") for c in chain_ds],
        [((micro, own * across * channels // LANES, LANES), F32, "m")],
        [((mine, m1), BF), ((mine, channels), F32)],
        after=[landed, chain_last.value(), chain_r4.value(), chain_rb.value()],
    )
    grad_input = grad_input.reshape(features.shape)
    added = lambda k, us: jnp.concatenate([u[k] + u[k + 2] + u[k + 4] for u in us])
    first = (u1, u2, u3)
    later = (u4, u5, u67)
    return (
        outputs, grad_input, out_n1, out_s1, out_e1,
        added(1, first), added(0, first),
        out_n2, out_s2, out_e2, out_sc,
        added(1, later), added(0, later),
    )


def solution(mesh):
    wide = P(None, "batch", "rows", None, None)
    shard = P("rows", None)
    return jax.shard_map(
        shards,
        mesh=mesh,
        in_specs=(
            wide, P(None, "batch", None), shard, shard, shard, P(), P(),
            shard, shard, shard, shard, P(), P(), wide,
        ),
        out_specs=(
            wide, wide, shard, shard, shard, P(), P(),
            shard, shard, shard, shard, P(), P(),
        ),
        check_vma=False,
    )
```

```python
import functools

import jax
import jax.numpy as jnp
from jax import lax
from jax.experimental import pallas as pl
from jax.experimental.pallas import tpu as pltpu
from jax.sharding import PartitionSpec as P

SPILL = 12
WIN = 40
COLS = 16
EPS = 1e-05
AXES = ("rows", "batch")
BF = jnp.bfloat16
F32 = jnp.float32
CHUNK = 32
TANH_SCALE = 0.7978845608028654
TANH_CUBE = 0.044715


def gelu(x):
    t = jnp.tanh(x * (TANH_SCALE + TANH_SCALE * TANH_CUBE * (x * x)))
    return x * (0.5 + 0.5 * t)


def gelu_slope(x):
    square = x * x
    t = jnp.tanh(x * (TANH_SCALE + TANH_SCALE * TANH_CUBE * square))
    inner = x * (TANH_SCALE + 3.0 * TANH_SCALE * TANH_CUBE * square)
    return (0.5 + 0.5 * t) * (1.0 + inner * (1.0 - t))


def nn(a, b):
    return lax.dot_general(a, b, (((1,), (0,)), ((), ())), preferred_element_type=F32)


def nt(a, b):
    return lax.dot_general(a, b, (((1,), (1,)), ((), ())), preferred_element_type=F32)


def wide_of(ref):
    return ref[...].reshape(-1, ref.shape[-1])


def pick(ref, row, start=0, width=None):
    table = ref[:, start : start + (width or ref.shape[1])]
    rows = lax.broadcasted_iota(jnp.int32, table.shape, 0)
    return jnp.sum(jnp.where(rows == row, table, 0.0), axis=0, keepdims=True)


def moments(ref, m, population, start=0, width=None):
    share = 1.0 / population
    average = pick(ref, 2 * m, start, width) * share
    return average, lax.rsqrt(pick(ref, 2 * m + 1, start, width) * share - average * average + EPS)


def line(ref, m, population, gain, bias):
    average, inv = moments(ref, m, population)
    scale = inv * gain[...]
    return scale, bias[...] - average * scale


def back_line(ref, back, m, population, gain, start=0):
    average, inv = moments(ref, m, population)
    share = 1.0 / population
    width = ref.shape[1]
    mean_d = pick(back, 2 * m, start, width) * share
    mean_dn = pick(back, 2 * m + 1, start, width) * share
    by_d = gain[...] * inv
    by_p = -by_d * inv * mean_dn
    return by_d, by_p, -by_d * mean_d - by_p * average


def centred(ref, m, population, first, second):
    average, inv = moments(ref, m, population)
    first = jnp.sum(first, axis=0, keepdims=True)
    second = jnp.sum(second, axis=0, keepdims=True)
    return first, inv * (second - average * first)


def put_sums(ref, m, first, second, start=0):
    c = first.shape[1]
    at = slice(start, start + c)

    @pl.when(m == 0)
    def _():
        ref[:, at] = jnp.zeros((ref.shape[0], c), F32)

    first = jnp.sum(first, axis=0, keepdims=True)
    second = jnp.sum(second, axis=0, keepdims=True)
    rows = lax.broadcasted_iota(jnp.int32, (ref.shape[0], c), 0)
    ref[:, at] = jnp.where(rows == 2 * m, first, jnp.where(rows == 2 * m + 1, second, ref[:, at]))


def sweep(rows, c, vectors, body, sums=0, chunk=CHUNK, width=256):
    out = [[] for _ in range(sums)]
    for j in range(c // width):
        lanes = slice(j * width, (j + 1) * width)
        spread = [jnp.broadcast_to(v[:, lanes], (8, width))[None] for v in vectors]

        def step(i, carry):
            at = pl.ds(pl.multiple_of(i * chunk, chunk), chunk)
            return tuple(t + jnp.sum(v, axis=0) for t, v in zip(carry, body(at, lanes, spread) or ()))

        total = lax.fori_loop(0, rows // chunk, step, (jnp.zeros((8, width), F32),) * sums)
        for k in range(sums):
            out[k].append(total[k])
    return [jnp.concatenate(v, 1) for v in out]


def eight(x):
    return x.reshape(-1, 8, x.shape[-1])


def flat(x):
    return x.reshape(-1, x.shape[-1])


def get(ref, at, lanes):
    return eight(ref[0, at, lanes].astype(F32))


def get_mask(ref, at, lanes):
    m = eight(ref[0, at, :])
    times = (lanes.stop - lanes.start) // LANES
    return jnp.concatenate([m] * times, 2) if times > 1 else m


def put(ref, at, lanes, value):
    ref[0, at, lanes] = flat(value).astype(ref.dtype)


def count_up(ref, out_total, m, mask=None):
    def add(at, lanes, _):
        p = get(ref, at, lanes)
        q = p if mask is None else p * get_mask(mask, at, lanes)
        return q, q * p

    put_sums(out_total, m, *sweep(ref.shape[1], ref.shape[2], (), add, 2))


LANES = 128


def put_tall(ref, rows, value, first=0):
    for j in range(value.shape[1] // LANES):
        ref[first // LANES + j, rows, :] = value[:, j * LANES : (j + 1) * LANES]


def get_tall(ref, rows, lanes):
    return jnp.concatenate([ref[j, rows, :] for j in range(lanes.start // LANES, lanes.stop // LANES)], 1)


OWN, UPPER, LOWER, INNER = 0, 1, 2, 3


def lane(ref, which, rows):
    return ref[0, rows, which : which + 1]


def k_masks(own, anchor, kinds, mine_out, half_out, flags, inner):
    first = anchor[0]
    height_of = lambda m, v: 6 + 8 * kinds[m, 0, v]
    for m in range(flags.shape[0]):
        rows = flags.shape[1] // COLS
        row = first + lax.broadcasted_iota(jnp.int32, (rows, LANES), 0)

        def view(v, c):
            at, width, start, last = c
            height = height_of(m, v)
            inside = (row >= at) & (row < at + height)
            return (
                at + height,
                jnp.where(inside, height, width),
                jnp.where(inside, at, start),
                jnp.where(inside, at + height - 1, last),
            )

        zero = jnp.zeros((rows, LANES), jnp.int32)
        _, width, start, last = lax.fori_loop(0, kinds.shape[2], view, (jnp.int32(0), zero, zero, zero))
        owned = (start >= first) & (start < first + own) & (width > 0)
        mine = jnp.where(owned, width, 0)
        above = (start != row).astype(F32)
        below = (last != row).astype(F32)
        cells = lambda v, n: jnp.broadcast_to(v[:, None, :], (v.shape[0], n, LANES))
        shape = (rows, COLS, LANES)
        column = lax.broadcasted_iota(jnp.int32, shape, 1)
        lanes = lax.broadcasted_iota(jnp.int32, shape, 2)
        value = jnp.where(lanes == OWN, (column < cells(width, COLS)).astype(F32), 0.0)
        value = jnp.where(lanes == UPPER, cells(above, COLS), value)
        value = jnp.where(lanes == LOWER, cells(below, COLS), value)
        flags[m] = value.reshape(rows * COLS, LANES)
        mine_out[m] = (column < cells(mine, COLS)).astype(F32).reshape(rows * COLS, LANES)
        shape = (rows, COLS // 2, LANES)
        column = lax.broadcasted_iota(jnp.int32, shape, 1)
        even = lambda v: v.reshape(rows // 2, 2, COLS // 2, LANES)[:, 0].reshape(rows * COLS // 4, LANES)
        half_out[m] = even((2 * column < cells(mine, COLS // 2)).astype(F32))
        inner[m] = even(cells(above, COLS // 2))


def k_first(features, mask, weight, pre, head, total, rows):
    m = pl.program_id(0)
    own, across = features.shape[2], features.shape[3]

    @pl.when(m == 0)
    def _():
        rows[...] = jnp.zeros_like(rows)

    for r in range(own):
        rows[r * COLS : r * COLS + across, :] = features[0, 0, r]
    pre[0] = nn(rows[...] * lane(mask, OWN, slice(0, own * COLS)).astype(BF), weight[...])
    head[0] = pre[0, 0 : head.shape[1], :].astype(BF)

    count_up(pre, total, m)


def k_entry(features, mask, *refs):
    spills, (entry, rows) = refs[:-2], refs[-2:]
    m = pl.program_id(0)
    own, across = features.shape[2], features.shape[3]

    @pl.when(m == 0)
    def _():
        rows[...] = jnp.zeros_like(rows)

    for r in range(own):
        rows[r * COLS : r * COLS + across, :] = features[0, 0, r]
    for k, spill in enumerate(spills):

        @pl.when(m == k)
        def _():
            for r in range(spill.shape[0]):
                at = (own + r) * COLS
                rows[at : at + across, :] = spill[r]

    entry[0] = rows[...] * lane(mask, 0, slice(None)).astype(BF)


def join_pre_one(own, spill, pre, c):
    edge, more = own.shape[1], spill.shape[1]
    pre[0, 0:edge, :] = own[0]
    pre[0, edge : edge + more, :] = spill[0].astype(F32)
    pre[0, edge + more :, :] = jnp.zeros((pre.shape[1] - edge - more, c), F32)


def spread_trio(source, trio, cells):
    c = source.shape[1]
    trio[0:COLS, :] = jnp.zeros((COLS, 3 * c), BF)
    trio[COLS + cells : 2 * COLS + cells, :] = jnp.zeros((COLS, 3 * c), BF)
    for r in range(0, cells, CHUNK):
        for tap in range(3):
            part = source[COLS + r + tap - 1 : COLS + r + tap - 1 + CHUNK, :]
            trio[COLS + r : COLS + r + CHUNK, tap * c : (tap + 1) * c] = part.astype(BF)


def conv_rows(trio, flags, weight, cells):
    width = trio.shape[1]
    upper = lane(flags, UPPER, slice(None)).astype(BF)
    lower = lane(flags, LOWER, slice(None)).astype(BF)
    above = trio[0:cells, :] * upper
    here = trio[COLS : COLS + cells, :]
    below = trio[2 * COLS : 2 * COLS + cells, :] * lower
    total = (
        nn(above, weight[0:width, :])
        + nn(here, weight[width : 2 * width, :])
        + nn(below, weight[2 * width : 3 * width, :])
    )
    return total, (above, here, below)


def clear_ends(source, cells):
    c = source.shape[1]
    source[0:COLS, :] = jnp.zeros((COLS, c), F32)
    source[COLS + cells : 2 * COLS + cells, :] = jnp.zeros((COLS, c), F32)


def later(at, by):
    return pl.ds(pl.multiple_of(at.start + by, 8), at.size)


def k_second(count, own, spill, total, gain, bias, mask, flags, weight, pre, patch, out_total, act, trio, joined):
    m = pl.program_id(0)
    cells, c = mask.shape[1], own.shape[2]
    join_pre_one(own, spill, joined, c)
    clear_ends(act, cells)

    def step(at, lanes, v):
        x = get(joined, at, lanes) * v[0] + v[1]
        act[later(at, COLS), lanes] = flat(gelu(x) * get_mask(mask, at, lanes))

    sweep(cells, c, line(total, m, count, gain, bias), step)
    spread_trio(act, trio, cells)
    result, parts = conv_rows(trio, flags, weight, cells)
    pre[0] = result
    for k, part in enumerate(parts):
        patch[0, :, k * 3 * c : (k + 1) * 3 * c] = part
    count_up(pre, out_total, m, mask)


def k_third(count, pre_in, total, gain, bias, mask, weight, act, pre, out_total):
    m = pl.program_id(0)

    def step(at, lanes, v):
        x = get(pre_in, at, lanes) * v[0] + v[1]
        put(act, at, lanes, gelu(x) * get_mask(mask, at, lanes))

    sweep(pre_in.shape[1], pre_in.shape[2], line(total, m, count, gain, bias), step)
    pre[0] = nn(act[0], wide_of(weight)).astype(pre.dtype)
    count_up(pre, out_total, m)


def k_fourth(count, pre_in, entry, total, gain, bias, mask, weight, block, corner, slope, pre, out_total, full):
    m = pl.program_id(0)
    wide = COLS // 2
    chunk = 4 * COLS

    def step(at, lanes, v):
        x = get(pre_in, at, lanes) * v[0] + v[1] + get(entry, at, lanes)
        square = x * x
        t = jnp.tanh(x * (TANH_SCALE + TANH_SCALE * TANH_CUBE * square))
        inside = x * (TANH_SCALE + 3.0 * TANH_SCALE * TANH_CUBE * square)
        part = (0.5 + 0.5 * t) * get_mask(mask, at, lanes)
        y = x * part
        put(block, at, lanes, y)
        put(slope, at, lanes, part + part * inside * (1.0 - t))
        put_tall(full, slice(0, chunk), flat(y), lanes.start)
        pair = [get_tall(full, pl.ds(k * COLS, wide, stride=2), lanes) for k in (0, 2)]
        corner[0, pl.ds(pl.multiple_of(at.start // 4, COLS), COLS), lanes] = jnp.concatenate(pair, 0).astype(BF)

    sweep(pre_in.shape[1], pre_in.shape[2], line(total, m, count, gain, bias), step, chunk=chunk)
    pre[0] = nn(block[0], wide_of(weight)).astype(pre.dtype)
    count_up(pre, out_total, m)


def k_seventh(corner, weight, pre, out_total):
    micro, half, tile = pre.shape
    value = nn(corner[...].reshape(micro * half, -1), wide_of(weight))
    pre[...] = value.reshape(pre.shape).astype(pre.dtype)
    for m in range(micro):
        part = eight(value[m * half : (m + 1) * half])
        sums = [jnp.sum(v, axis=(0, 1))[None] for v in (part, part * part)]
        rows = lax.broadcasted_iota(jnp.int32, out_total.shape, 0)
        table = jnp.zeros_like(sums[0]) if m == 0 else out_total[...]
        out_total[...] = jnp.where(rows == 2 * m, sums[0], jnp.where(rows == 2 * m + 1, sums[1], table))


def k_fifth(count, pre_in, total, gain, bias, mask, half_mask, inner, weight, pre, patch, out_total, act, eo, oe, oo):
    m = pl.program_id(0)
    cells, c = pre_in.shape[1], pre_in.shape[2]
    half = cells // 4
    wide = COLS // 2

    def step(at, lanes, v):
        x = get(pre_in, at, lanes) * v[0] + v[1]
        put_tall(act, at, flat(gelu(x) * get_mask(mask, at, lanes)), lanes.start)

    sweep(cells, c, line(total, m, count, gain, bias), step)
    pad = 2 * wide
    for buf in (eo, oe, oo):
        buf[0:pad, :] = jnp.zeros((pad, c), F32)
    for j in range(c // LANES):
        lanes = slice(j * LANES, (j + 1) * LANES)
        even = act[j, pl.ds(0, cells // 2, stride=2), :].reshape(half // wide, 2, wide, LANES)
        odd = act[j, pl.ds(1, cells // 2, stride=2), :].reshape(half // wide, 2, wide, LANES)
        patch[0, :, 4 * c + j * LANES : 4 * c + (j + 1) * LANES] = even[:, 0].reshape(half, LANES).astype(BF)
        oe[pad : pad + half, lanes] = even[:, 1].reshape(half, LANES)
        eo[pad : pad + half, lanes] = odd[:, 0].reshape(half, LANES)
        oo[pad : pad + half, lanes] = odd[:, 1].reshape(half, LANES)
    first = jnp.concatenate([inner[0]] * (c // LANES), 1)
    take = lambda buf, back: buf[pad - back : pad - back + half, :]
    taps = (
        take(oo, wide + 1) * first, take(oe, wide) * first, take(oo, wide) * first,
        take(eo, 1), None, take(eo, 0),
        take(oo, 1), take(oe, 0), take(oo, 0),
    )
    for k, tap in enumerate(taps):
        if tap is not None:
            patch[0, :, k * c : (k + 1) * c] = tap.astype(BF)
    pre[0] = nn(patch[0], wide_of(weight))
    count_up(pre, out_total, m, half_mask)


def k_last(count, six, seven, tot6, tot7, g6, b6, g7, b7, half_mask, cot, out, slope, total, row):
    m = pl.program_id(0)
    half, c = six.shape[1], six.shape[2]
    wide = COLS // 2
    shown, across = out.shape[2], out.shape[3]
    scale6, shift6 = line(tot6, m, count, g6, b6)
    scale7, shift7 = line(tot7, m, count, g7, b7)
    row[...] = jnp.zeros_like(row)

    def step(at, lanes, v):
        p = 2 * (at.start // (2 * wide))
        mask = get_mask(half_mask, at, lanes)
        s6, s7 = get(six, at, lanes), get(seven, at, lanes)
        joined = s6 * v[0] + s7 * v[1] + v[2]
        square = joined * joined
        t = jnp.tanh(joined * (TANH_SCALE + TANH_SCALE * TANH_CUBE * square))
        inside = joined * (TANH_SCALE + 3.0 * TANH_SCALE * TANH_CUBE * square)
        part = (0.5 + 0.5 * t) * mask
        result = flat(joined * part)
        for k in range(2):
            q = jnp.minimum(p + k, shown - 1)
            if shown % 2 == 0 or k == 0:
                out[0, 0, q, :, lanes] = result[k * wide : k * wide + across].astype(BF)
            else:

                @pl.when(p + k < shown)
                def _():
                    out[0, 0, q, :, lanes] = result[k * wide : k * wide + across].astype(BF)

            row[k * wide : k * wide + across, lanes] = cot[0, 0, q, :, lanes].astype(F32)
        d = part * (1.0 + inside * (1.0 - t)) * eight(row[:, lanes])
        put(slope, at, lanes, d)
        return d, d * s6, d * s7

    sums = sweep(half, c, (scale6, scale7, shift6 + shift7), step, 3, chunk=2 * wide, width=512)
    put_sums(total, m, *centred(tot6, m, count, sums[0], sums[1]))
    put_sums(total, m, *centred(tot7, m, count, sums[0], sums[2]), c)


def slope_sums(d_out, pre, tot, m, population, gain, bias, mask, out_total, more=None):
    def add(at, lanes, v):
        p = get(pre, at, lanes)
        d = gelu_slope(p * v[0] + v[1]) * get(d_out, at, lanes) * get_mask(mask, at, lanes)
        put(d_out, at, lanes, d)
        return d, d * p

    sums = sweep(pre.shape[1], pre.shape[2], line(tot, m, population, gain, bias), add, 2)
    put_sums(out_total, m, *centred(tot, m, population, *sums))


def norm_back(d_pre, d, pre, tot, back, m, population, gain, mask):
    def step(at, lanes, v):
        value = get(d, at, lanes) * v[0] + get(pre, at, lanes) * v[1] + v[2]
        put(d_pre, at, lanes, value * get_mask(mask, at, lanes))

    sweep(pre.shape[1], pre.shape[2], back_line(tot, back, m, population, gain), step)


def k_back_six(
    count, slope, six, seven, tot6, tot7, back, g6, g7, five, tot5, g5, b5, half_mask, weight,
    d_six, d_seven, d_five, out_total,
):
    m = pl.program_id(0)
    half, c = six.shape[1], six.shape[2]

    def step(at, lanes, v):
        d = get(slope, at, lanes)
        mask = get_mask(half_mask, at, lanes)
        put(d_six, at, lanes, (d * v[0] + get(six, at, lanes) * v[1] + v[2]) * mask)
        put(d_seven, at, lanes, (d * v[3] + get(seven, at, lanes) * v[4] + v[5]) * mask)

    vectors = back_line(tot6, back, m, count, g6) + back_line(tot7, back, m, count, g7, c)
    sweep(half, c, vectors, step)
    d_five[0] = nt(d_six[0], wide_of(weight))
    slope_sums(d_five, five, tot5, m, count, g5, b5, half_mask, out_total)


def k_corner(d_seven, weight, d_corner):
    d_corner[0] = nt(d_seven[0], wide_of(weight)).astype(d_corner.dtype)


def k_back_five(
    half_count, full_count, d_five, five, tot5, back5, g5, half_mask, inner, weight, four, tot4, g4, b4, mask,
    d_pre, d_four, out_total, grid_scratch, shifted,
):
    m = pl.program_id(0)
    half, c = five.shape[1], five.shape[2]
    cells = 4 * half
    wide = COLS // 2
    norm_back(d_pre, d_five, five, tot5, back5, m, half_count, g5, half_mask)
    d = d_pre[0]
    wide_d = d.astype(F32)
    tail = 2 * wide
    shifted[half : half + tail, :] = jnp.zeros((tail, c), F32)
    shifted[0:half, :] = wide_d
    right = shifted[1 : 1 + half, :].astype(BF)
    shifted[0:half, :] = wide_d * jnp.concatenate([inner[0]] * (c // LANES), 1)
    down = shifted[wide : wide + half, :].astype(BF)
    down_right = shifted[wide + 1 : wide + 1 + half, :].astype(BF)
    taps = wide_of(weight)
    w = lambda tap: taps[tap * c : (tap + 1) * c]
    ee = nt(d, w(4))
    eo = nt(d, w(5)) + nt(right, w(3))
    oe = nt(d, w(7)) + nt(down, w(1))
    oo = nt(d, w(8)) + nt(right, w(6)) + nt(down, w(2)) + nt(down_right, w(0))
    rows = half // wide
    even = jnp.stack([ee.reshape(rows, wide, c), oe.reshape(rows, wide, c)], 1).reshape(cells // 2, c)
    odd = jnp.stack([eo.reshape(rows, wide, c), oo.reshape(rows, wide, c)], 1).reshape(cells // 2, c)
    put_tall(grid_scratch, pl.ds(0, cells // 2, stride=2), even)
    put_tall(grid_scratch, pl.ds(1, cells // 2, stride=2), odd)

    def add(at, lanes, v):
        p = get(four, at, lanes)
        got = eight(get_tall(grid_scratch, at, lanes))
        d = gelu_slope(p * v[0] + v[1]) * got * get_mask(mask, at, lanes)
        put(d_four, at, lanes, d)
        return d, d * p

    sums = sweep(cells, c, line(tot4, m, full_count, g4, b4), add, 2)
    put_sums(out_total, m, *centred(tot4, m, full_count, *sums))


def k_back_four(
    count, d_four, four, tot4, back4, g4, mask, weight, d_corner, three, slope, tot3,
    d_pre, d_summed, out_total, placed, d_block,
):
    m = pl.program_id(0)
    cells, c = three.shape[1], three.shape[2]
    norm_back(d_pre, d_four, four, tot4, back4, m, count, g4, mask)
    d_block[0] = nt(d_pre[0], wide_of(weight))
    wide = COLS // 2
    placed[...] = jnp.zeros_like(placed)

    def add(at, lanes, v):
        corner_at = pl.ds(pl.multiple_of(at.start // 4, COLS), COLS)
        value = d_corner[0, corner_at, lanes].astype(F32)
        for k in range(2):
            rows = pl.ds(2 * k * COLS, wide, stride=2)
            put_tall(placed, rows, value[k * wide : (k + 1) * wide], lanes.start)
        got = get(d_block, at, lanes) + eight(get_tall(placed, slice(0, 4 * COLS), lanes))
        d = get(slope, at, lanes) * got
        put(d_summed, at, lanes, d)
        return d, d * get(three, at, lanes)

    sums = sweep(cells, c, (), add, 2, chunk=4 * COLS)
    put_sums(out_total, m, *centred(tot3, m, count, *sums))


def k_back_three(count, d_summed, three, tot3, back3, g3, mask, weight, two, tot2, g2, b2, d_pre, d_two, out_total):
    m = pl.program_id(0)
    norm_back(d_pre, d_summed, three, tot3, back3, m, count, g3, mask)
    d_two[0] = nt(d_pre[0], wide_of(weight))
    slope_sums(d_two, two, tot2, m, count, g2, b2, mask, out_total)


def k_back_two(
    count, d_two, two, tot2, back2, g2, mask, flags, weight, own, spill, tot1, g1, b1,
    d_pre, d_one, out_total, source, trio, joined,
):
    m = pl.program_id(0)
    cells, c = two.shape[1], two.shape[2]
    clear_ends(source, cells)

    def step(at, lanes, v):
        value = get(d_two, at, lanes) * v[0] + get(two, at, lanes) * v[1] + v[2]
        value = value * get_mask(mask, at, lanes)
        put(d_pre, at, lanes, value)
        source[later(at, COLS), lanes] = flat(value)

    sweep(cells, c, back_line(tot2, back2, m, count, g2), step)
    spread_trio(source, trio, cells)
    upper = lane(flags, UPPER, slice(None)).astype(BF)
    lower = lane(flags, LOWER, slice(None)).astype(BF)
    shifted = (
        trio[0:cells, :] * upper,
        trio[COLS : COLS + cells, :],
        trio[2 * COLS : 2 * COLS + cells, :] * lower,
    )
    tap = lambda k: nt(shifted[k // 3][:, k % 3 * c : (k % 3 + 1) * c], weight[(8 - k) * c : (9 - k) * c, :])
    d_one[0] = sum((tap(k) for k in range(1, 9)), tap(0))
    join_pre_one(own, spill, joined, c)
    slope_sums(d_one, joined, tot1, m, count, g1, b1, mask, out_total)


def k_back_one(count, d_one, own, spill, tot1, back1, g1, mask, d_pre, joined):
    m = pl.program_id(0)
    join_pre_one(own, spill, joined, d_one.shape[2])
    norm_back(d_pre, d_one, joined, tot1, back1, m, count, g1, mask)


def k_input(d_pre, more_pre, d_summed, weight, *refs):
    more_summed, (out, both, sums) = refs[:-3], refs[-3:]
    m = pl.program_id(0)
    spilled, cells = more_pre.shape[1], both.shape[0]
    blocks = sums.shape[1] // LANES
    own = cells // COLS
    across = out.shape[1] // blocks // own
    both[...] = d_pre[0, 0:cells, :]
    both[0:spilled, :] = d_pre[0, 0:spilled, :] + more_pre[0]
    sums[...] = nt(both[...], weight[...])
    for r in range(own):
        at = r * COLS
        value = sums[at : at + COLS, :] + d_summed[0, at : at + COLS, :].astype(F32)
        if at < spilled:
            extra = more_summed[0][at : at + COLS, :].astype(F32)
            for k in range(1, len(more_summed)):
                extra = jnp.where(m == k, more_summed[k][at : at + COLS, :].astype(F32), extra)
            value = value + extra
        for j in range(blocks):
            rows = pl.ds(r * across * blocks + j, across, stride=blocks)
            out[0, rows, :] = value[:across, j * LANES : (j + 1) * LANES]


def exchange(x, mask):
    total = lax.axis_size("rows") * lax.axis_size("batch")
    return lax.ppermute(x, AXES, [(i, i ^ mask) for i in range(total)])


def from_behind(x, by):
    devices = lax.axis_size("rows")
    pairs = [(i, i + by) for i in range(devices) if 0 <= i + by < devices]
    return lax.ppermute(x, "rows", pairs)


class Chain:
    def __init__(self, steps):
        self.steps, self.flying, self.done, self.result = steps, None, False, None
        self.ready = next(steps)

    def launch(self, array):
        self.flying = self.ready[1](array)

    def land(self):
        try:
            self.ready = self.steps.send(self.flying)
        except StopIteration as end:
            self.done, self.result = True, end.value
        self.flying = None

    def value(self):
        while not self.done:
            if self.flying is None:
                self.launch(self.ready[0])
            self.land()
        return self.result


def hook(x, start=(), finish=(), need=()):
    if not (start or finish or need):
        return x
    landed = []
    for chain in finish:
        if not chain.done:
            landed.append(chain.flying)
            chain.land()
    live = [chain for chain in start if not chain.done]
    tied = lax.optimization_barrier((x, [c.ready[0] for c in live], landed, list(need)))
    for chain, array in zip(live, tied[1]):
        chain.launch(array)
    return tied[0]


def global_sum(x, b=None, c=None, d=None):
    bits = device_bits()
    split = x.shape[1] >= 2048
    if split:
        half = x.shape[1] // 2
        part = lambda bit: lax.dynamic_slice_in_dim(x, bit * half, half, 1)
        x = part(my_bit(0)) + exchange(part(1 - my_bit(0)), 1)
    else:
        x = x + exchange(x, 1)
    x = hook(x, **(b or {}))
    step = 1
    while step < bits:
        low = 1 << step
        if step + 1 < bits:
            p, q, r = exchange(x, low), exchange(x, 2 * low), exchange(x, 3 * low)
            x = (x + p) + (q + r)
        else:
            x = x + exchange(x, low)
        if step == 1:
            x = hook(x, **(c or {}))
        step += 2
    if split:
        other = exchange(x, 1)
        upper = my_bit(0) == 1
        x = jnp.concatenate([jnp.where(upper, other, x), jnp.where(upper, x, other)], 1)
    return hook(x, **(d or {}))


def device_bits():
    total = lax.axis_size("rows") * lax.axis_size("batch")
    return total.bit_length() - 1


def my_bit(bit):
    number = lax.axis_index("rows") * lax.axis_size("batch") + lax.axis_index("batch")
    return (number >> bit) & 1


def batch_bits():
    return lax.axis_size("batch").bit_length() - 1


def across(bit):
    return lambda x: exchange(x, 1 << bit)


def lanes_of(w, parts, wide=256):
    x = w.reshape(parts, -1, w.shape[1] // wide, wide)
    return x.transpose(0, 2, 1, 3).reshape(parts, -1, wide)


def from_lanes(x, c):
    parts, wide = x.shape[0], x.shape[2]
    x = x.reshape(parts, c // wide, -1, wide)
    return x.transpose(0, 2, 1, 3).reshape(-1, c)


def ordered(mine, other, bit, axis):
    upper = my_bit(bit) == 1
    return jnp.stack([jnp.where(upper, other, mine), jnp.where(upper, mine, other)], axis)


def gather_steps(packed, parts):
    bits, low = device_bits(), batch_bits()
    number = my_bit(0) if parts == 1 else lax.axis_index("batch")
    x = lax.dynamic_index_in_dim(packed, number, 0, keepdims=False)
    for bit in list(reversed(range(low, bits))) + list(reversed(range(parts))):
        got = yield x, across(bit)
        x = ordered(x, got, bit, x.ndim - 2)
    return x.reshape((-1,) + x.shape[-2:])


def gather_offloaded(ws):
    quarters, wide = lax.axis_size("batch"), ws[0].shape[1]
    packed = jnp.concatenate([w.reshape(quarters, -1, wide) for w in ws], 1)
    part = lax.dynamic_index_in_dim(packed, lax.axis_index("batch"), 0, keepdims=False)
    whole = lax.all_gather(part, AXES, axis=0)
    out, at = [], 0
    for w in ws:
        n = w.shape[0] // quarters
        if n % 16 == 0 and at % n == 0:
            block = at // n
            spec = pl.BlockSpec(
                (whole.shape[0], n, wide), lambda m, k=block: (0, k, 0), pipeline_mode=pl.Buffered(1)
            )
            out.append((whole, spec))
        else:
            part = whole[:, at : at + n].reshape(-1, wide)
            out.append((part, pl.BlockSpec(part.shape, lambda m: (0, 0), pipeline_mode=pl.Buffered(1))))
        at += n
    return out


def sharded(grad, c):
    total = lax.axis_size("rows") * lax.axis_size("batch")
    if grad.shape[1] == c:
        return grad.reshape(total, -1, c)
    return lanes_of(grad, total)


def spread_steps(x):
    for bit in reversed(range(batch_bits())):
        got = yield x, across(bit)
        x = ordered(x, got, bit, x.ndim - 2)
    return x.reshape((-1,) + x.shape[-2:])


def reduce_scattered(part, order):
    bits = device_bits()
    x = part.reshape((2,) * bits + part.shape[1:])
    left = list(reversed(range(bits)))
    got = None
    for bit in order:
        axis = left.index(bit)
        left.remove(bit)
        half = lambda v, b: lax.dynamic_index_in_dim(v, b, axis, keepdims=False)
        keep, send = my_bit(bit), 1 - my_bit(bit)
        if got is None:
            x, give = half(x, keep), half(x, send)
        else:
            x, give = half(x, keep) + half(got, keep), half(x, send) + half(got, send)
        got = yield give, across(bit)
    return x + got


def lanes_back(filter_and_spec, c):
    whole, spec = filter_and_spec
    if whole.ndim == 3:
        n, k = spec.block_shape[1], spec.index_map(0)[1]
        return from_lanes(whole[:, k * n : (k + 1) * n], c)
    return from_lanes(whole.reshape(lax.axis_size("rows") * lax.axis_size("batch"), -1, whole.shape[1]), c)


def reduce_first(part):
    bits, low = device_bits(), batch_bits()
    x = part.reshape((2,) * bits + part.shape[1:])
    left = list(reversed(range(bits)))
    got = None
    for bit in [0] + list(range(low, bits - 1)):
        axis = left.index(bit)
        left.remove(bit)
        half = lambda v, b: lax.dynamic_index_in_dim(v, b, axis, keepdims=False)
        keep, send = my_bit(bit), 1 - my_bit(bit)
        if got is None:
            x, give = half(x, keep), half(x, send)
        else:
            x, give = half(x, keep) + half(got, keep), half(x, send) + half(got, send)
        got = yield give, across(bit)
    return x + got


def reduce_last(x):
    low, last = batch_bits(), device_bits() - 1
    bit = my_bit(last)
    half = lambda b: lax.dynamic_index_in_dim(x, b, 0, keepdims=False)
    got = yield half(1 - bit), across(last)
    x = half(bit) + got
    for b in range(1, low):
        got = yield x, across(b)
        x = x + got
    got = yield x, across(0)
    x = ordered(x, got, 0, x.ndim - 2)
    return x.reshape((-1,) + x.shape[-2:])


def one_step(x, send):
    return (yield x, send)


def unpack(shard, shapes):
    devices = lax.axis_size("rows")
    out, at = [], 0
    for k, c in shapes:
        n = k * c // devices // shard.shape[0] // shard.shape[2]
        part = shard[:, at : at + n]
        out.append((from_lanes(part, c) if shard.shape[2] != c else part.reshape(-1, c)).astype(F32))
        at += n
    return out


LIMIT = 16


def per_micro(shape):
    zeros = (0,) * (len(shape) - 1)
    return pl.BlockSpec((1,) + tuple(shape[1:]), lambda m: (m,) + zeros)


def whole(shape):
    zeros = (0,) * len(shape)
    return pl.BlockSpec(tuple(shape), lambda m: zeros, pipeline_mode=pl.Buffered(1))


def table(shape):
    zeros = (0,) * len(shape)
    return pl.BlockSpec(tuple(shape), lambda m: zeros)


def call(kernel, micro, ins, outs, scratch=(), limit=LIMIT, after=()):
    kind = {"m": per_micro, "w": whole, "s": lambda shape: pl.BlockSpec(memory_space=pltpu.SMEM)}
    in_specs = [k if isinstance(k, pl.BlockSpec) else kind[k](a.shape) for a, k in ins]
    in_specs += [pl.BlockSpec(memory_space=pl.ANY)] * len(after)
    out_specs = [per_micro(sh) if k == "m" else table(sh) for sh, _, k in outs]

    def run(*refs):
        kernel(*refs[: len(ins)], *refs[len(ins) + len(after) :])

    return pl.pallas_call(
        run,
        grid=(micro,),
        in_specs=in_specs,
        out_specs=out_specs,
        out_shape=[jax.ShapeDtypeStruct(sh, t) for sh, t, _ in outs],
        scratch_shapes=[pltpu.VMEM(sh, t) for sh, t in scratch],
        compiler_params=pltpu.CompilerParams(
            dimension_semantics=("arbitrary",), vmem_limit_bytes=limit * 1024 * 1024
        ),
        name=getattr(kernel, "func", kernel).__name__,
    )(*[a for a, _ in ins], *after)


def weight_term(left, right):
    k, n = left.shape[-1], right.shape[-1]
    return lax.dot_general(
        left.reshape(-1, k), right.reshape(-1, n), (((0,), (0,)), ((), ())), preferred_element_type=F32
    ).astype(BF)


def shards(
    features, view_kind, narrow_one, spatial_one, expand_one, gains_one, biases_one,
    narrow_two, spatial_two, expand_two, shortcut, gains_two, biases_two, cotangent,
):
    micro, _, own, across, channels = features.shape
    m1 = spatial_one.shape[1]
    m2 = spatial_two.shape[1]
    outward = shortcut.shape[1]
    sources = lax.axis_size("rows") * own // 52
    full_count = float(lax.axis_size("batch") * sources * 536)
    half_count = float(lax.axis_size("batch") * sources * 134)
    anchor = lax.axis_index("rows") * own
    cells, half = WIN * COLS, WIN * COLS // 4
    mine, more = own * COLS, SPILL * COLS

    chain_n1 = Chain(gather_steps(narrow_one.reshape(2, -1, m1), 1))
    chain_a = Chain(gather_steps(spatial_one.reshape(4, -1, m1), 2))
    thin = [lanes_of(expand_one, 4, m2).reshape(-1, m2)]
    spatial_b, narrow_b, thin_a = gather_offloaded([spatial_two, narrow_two] + thin)
    expand_a = lanes_back(thin_a, channels)
    bypass, expand_b = gather_offloaded([shortcut, expand_two])
    chain_f = [
        Chain(one_step(features[k, 0, :SPILL], lambda x: from_behind(x, -1))) for k in range(micro)
    ]
    g1, g2, g3 = (v[None] for v in jnp.split(gains_one, [m1, 2 * m1]))
    b1, b2, b3 = (v[None] for v in jnp.split(biases_one, [m1, 2 * m1]))
    cuts = [m2, 2 * m2, 2 * m2 + outward]
    g4, g5, g6, g7 = (v[None] for v in jnp.split(gains_two, cuts))
    b4, b5, b6, b7 = (v[None] for v in jnp.split(biases_two, cuts))
    mask, half_mask, flags, inner = pl.pallas_call(
        functools.partial(k_masks, own),
        in_specs=[pl.BlockSpec(memory_space=pltpu.SMEM)] * 2,
        out_shape=[
            jax.ShapeDtypeStruct((micro, cells, LANES), F32),
            jax.ShapeDtypeStruct((micro, half, LANES), F32),
        ]
        * 2,
        name="k_masks",
    )(anchor[None].astype(jnp.int32), view_kind)

    full_table = lambda c: ((8, c), F32, "t")
    per = lambda c, t=F32, n=cells: ((micro, n, c), t, "m")

    for chain in (chain_n1, chain_a):
        chain.launch(chain.ready[0])
    chain_n1.land()
    before = [mask]
    while not chain_n1.done:
        chain_n1.launch(lax.optimization_barrier((chain_n1.ready[0], before))[0])
        landed = chain_n1.flying
        chain_n1.land()
        if chain_a.flying is not None and len(before) < 3 and not chain_n1.done:
            chain_a.land()
            chain_a.launch(lax.optimization_barrier((chain_a.ready[0], landed))[0])
            before = before + [landed]
            if len(before) == 3:
                hook(landed, start=chain_f)
    narrow_a = chain_n1.value().reshape(-1, m1)
    pre_one, head, t1 = call(
        k_first, micro, [(features, "m"), (flags, "m"), (narrow_a, "w")],
        [per(m1, F32, mine), per(m1, BF, more), full_table(m1)], [((mine, channels), BF)],
    )
    chain_h = Chain(one_step(head, lambda x: from_behind(x, -1)))
    t1 = global_sum(
        t1,
        b=dict(finish=[chain_a]),
        c=dict(start=[chain_a, chain_h]),
        d=dict(finish=[chain_a, chain_h], start=[chain_a]),
    )
    pre_spill = chain_h.value()
    spatial_a = chain_a.value().reshape(-1, m1)
    pre_two, patch_one, t2 = call(
        functools.partial(k_second, full_count), micro,
        [(pre_one, "m"), (pre_spill, "m"), (t1, "w"), (g1, "w"), (b1, "w"), (mask, "m"),
         (flags, "m"), (spatial_a, "w")],
        [per(m1), per(9 * m1, BF), full_table(m1)],
        [((cells + 2 * COLS, m1), F32), ((cells + 2 * COLS, 3 * m1), BF), ((1, cells, m1), F32)],
        limit=20,
    )
    (entry,) = call(
        k_entry, micro,
        [(features, "m"), (mask, "m")] + [(f.value(), "w") for f in chain_f],
        [per(channels, BF)], [((cells, channels), BF)],
    )
    t2 = global_sum(t2, c=dict(need=[entry]))
    act_two, pre_three, t3 = call(
        functools.partial(k_third, full_count), micro,
        [(pre_two, "m"), (t2, "w"), (g2, "w"), (b2, "w"), (mask, "m"), (expand_a, "w")],
        [per(m1, BF), per(channels, BF), full_table(channels)],
    )
    t3 = global_sum(t3)
    block_out, corner, slope_three, pre_four, t4 = call(
        functools.partial(k_fourth, full_count), micro,
        [(pre_three, "m"), (entry, "m"), (t3, "w"), (g3, "w"), (b3, "w"), (mask, "m"), narrow_b],
        [per(channels, BF), per(channels, BF, half), per(channels, BF), per(m2, BF), full_table(m2)],
        [((channels // LANES, 4 * COLS, LANES), F32)],
    )
    t4 = global_sum(t4)
    pre_five, patch_two, t5 = call(
        functools.partial(k_fifth, full_count), micro,
        [(pre_four, "m"), (t4, "w"), (g4, "w"), (b4, "w"), (mask, "m"), (half_mask, "m"), (inner, "m"),
         spatial_b],
        [per(m2, F32, half), per(9 * m2, BF, half), full_table(m2)],
        [((m2 // LANES, cells, LANES), F32)] + [((half + COLS, m2), F32)] * 3,
        limit=20,
    )
    t5 = global_sum(t5)
    act_five, pre_six, t6 = call(
        functools.partial(k_third, half_count), micro,
        [(pre_five, "m"), (t5, "w"), (g5, "w"), (b5, "w"), (half_mask, "m"), expand_b],
        [per(m2, BF, half), per(outward, BF, half), full_table(outward)],
    )
    tile = outward // 4
    by_tile = bypass[1].block_shape[:-1] + (tile,)
    pre_seven, t7 = pl.pallas_call(
        k_seventh,
        grid=(4,),
        in_specs=[
            pl.BlockSpec(corner.shape, lambda n: (0, 0, 0)),
            pl.BlockSpec(by_tile, lambda n: (0,) * (len(by_tile) - 1) + (n,)),
        ],
        out_specs=[
            pl.BlockSpec((micro, half, tile), lambda n: (0, 0, n)),
            pl.BlockSpec((8, tile), lambda n: (0, n)),
        ],
        out_shape=[
            jax.ShapeDtypeStruct((micro, half, outward), BF),
            jax.ShapeDtypeStruct((8, outward), F32),
        ],
        compiler_params=pltpu.CompilerParams(vmem_limit_bytes=LIMIT * 1024 * 1024),
        name="k_seventh",
    )(corner, bypass[0])
    t67 = global_sum(jnp.concatenate([t6, t7], 1))
    t6, t7 = t67[:, :outward], t67[:, outward:]
    outputs, slope, u67 = call(
        functools.partial(k_last, half_count), micro,
        [(pre_six, "m"), (pre_seven, "m"), (t6, "w"), (t7, "w"), (g6, "w"), (b6, "w"), (g7, "w"), (b7, "w"),
         (half_mask, "m"), (cotangent, "m")],
        [(cotangent.shape, BF, "m"), per(outward, BF, half), full_table(2 * outward)],
        [((COLS, outward), F32)],
    )
    u67 = global_sum(u67)
    d_six, d_seven, d_five, u5 = call(
        functools.partial(k_back_six, half_count), micro,
        [(slope, "m"), (pre_six, "m"), (pre_seven, "m"), (t6, "w"), (t7, "w"), (u67, "w"), (g6, "w"), (g7, "w"),
         (pre_five, "m"), (t5, "w"), (g5, "w"), (b5, "w"), (half_mask, "m"), expand_b],
        [per(outward, BF, half), per(outward, BF, half), per(m2, F32, half), full_table(m2)],
    )
    (d_corner,) = call(
        k_corner, micro, [(d_seven, "m"), bypass], [per(channels, BF, half)]
    )
    grad_e2 = weight_term(act_five, d_six)
    grad_sc = weight_term(corner, d_seven)
    pack_b = jnp.concatenate([sharded(grad_sc, outward), sharded(grad_e2, outward)], 1).reshape(-1, outward)
    u5 = global_sum(u5, c=dict(need=[pack_b]))
    part_b = lax.psum_scatter(pack_b, AXES, scatter_dimension=0, tiled=True)
    d_pre_five, d_four, u4 = call(
        functools.partial(k_back_five, half_count, full_count), micro,
        [(d_five, "m"), (pre_five, "m"), (t5, "w"), (u5, "w"), (g5, "w"), (half_mask, "m"), (inner, "m"),
         spatial_b, (pre_four, "m"), (t4, "w"), (g4, "w"), (b4, "w"), (mask, "m")],
        [per(m2, BF, half), per(m2), full_table(m2)],
        [((m2 // LANES, cells, LANES), F32), ((half + COLS, m2), F32)],
        limit=22,
    )
    grad_s2 = sharded(weight_term(patch_two, d_pre_five), m2)
    cut = grad_s2.shape[1] // 32 * 16 or grad_s2.shape[1] // 2
    low = batch_bits()
    chain_rs = [
        Chain(reduce_scattered(grad_s2[:, :cut], list(range(device_bits())))),
        Chain(reduce_scattered(grad_s2[:, cut:], [0, low] + list(range(1, low)) + list(range(low + 1, device_bits())))),
    ]
    u4 = global_sum(u4, b=dict(start=chain_rs), c=dict(finish=chain_rs, start=chain_rs))
    d_pre_four, d_summed, u3 = call(
        functools.partial(k_back_four, full_count), micro,
        [(d_four, "m"), (pre_four, "m"), (t4, "w"), (u4, "w"), (g4, "w"), (mask, "m"), narrow_b,
         (d_corner, "m"), (pre_three, "m"), (slope_three, "m"), (t3, "w")],
        [per(m2, BF), per(channels, BF), full_table(channels)],
        [((channels // LANES, 4 * COLS, LANES), F32), ((1, cells, channels), F32)],
        limit=24,
    )
    grad_n2 = [
        sharded(weight_term(block_out, d_pre_four[..., k : k + 256]), 256) for k in range(0, m2, 256)
    ]
    spilled = d_summed[:, mine : mine + more]
    chain_ds = [Chain(one_step(spilled[k], lambda x: from_behind(x, 1))) for k in range(micro)]
    chain_r2 = Chain(reduce_first(jnp.concatenate(grad_n2, 1)))
    u3 = global_sum(
        u3,
        b=dict(start=[chain_r2]),
        c=dict(finish=chain_rs + [chain_r2], start=chain_rs + [chain_r2]),
    )
    d_pre_three, d_two, u2 = call(
        functools.partial(k_back_three, full_count), micro,
        [(d_summed, "m"), (pre_three, "m"), (t3, "w"), (u3, "w"), (g3, "w"), (mask, "m"), (expand_a, "w"),
         (pre_two, "m"), (t2, "w"), (g2, "w"), (b2, "w")],
        [per(channels, BF), per(m1), full_table(m1)],
    )
    grad_e1 = weight_term(act_two, d_pre_three)
    chain_r3 = Chain(reduce_first(sharded(grad_e1, 256)))
    u2 = global_sum(
        u2,
        b=dict(finish=[chain_r2], start=[chain_r3]),
        c=dict(finish=chain_rs + [chain_r3], start=[chain_r3]),
        d=dict(start=chain_rs + [chain_r2]),
    )
    d_pre_two, d_one, u1 = call(
        functools.partial(k_back_two, full_count), micro,
        [(d_two, "m"), (pre_two, "m"), (t2, "w"), (u2, "w"), (g2, "w"), (mask, "m"), (flags, "m"),
         (spatial_a, "w"), (pre_one, "m"), (pre_spill, "m"), (t1, "w"), (g1, "w"), (b1, "w")],
        [per(m1, BF), per(m1), full_table(m1)],
        [((cells + 2 * COLS, m1), F32), ((cells + 2 * COLS, 3 * m1), BF), ((1, cells, m1), F32)],
        limit=20,
    )
    grad_s1 = weight_term(patch_one, d_pre_two)
    chain_r1 = Chain(reduce_first(sharded(grad_s1, 256)))
    u1 = global_sum(
        u1,
        b=dict(finish=[chain_r3], start=[chain_r1]),
        c=dict(finish=chain_rs + [chain_r2, chain_r1], start=[chain_r1]),
        d=dict(start=chain_rs + [chain_r3] + chain_ds[:1]),
    )
    (d_pre_one,) = call(
        functools.partial(k_back_one, full_count), micro,
        [(d_one, "m"), (pre_one, "m"), (pre_spill, "m"), (t1, "w"), (u1, "w"), (g1, "w"), (mask, "m")],
        [per(m1, BF)], [((1, cells, m1), F32)],
    )
    chain_rn = Chain(reduce_first(sharded(weight_term(entry, d_pre_one), 256)))
    chain_rb = Chain(spread_steps(part_b))
    chain_rn.launch(chain_rn.ready[0])
    landed = chain_rn.flying
    chain_rn.land()
    chain_r4 = Chain(spread_steps(jnp.concatenate([c.value() for c in chain_rs], 0)))
    hook(landed, finish=[chain_r1], start=[chain_r1, chain_rb, chain_r4])
    while not chain_rn.done:
        chain_rn.launch(chain_rn.ready[0])
        landed = chain_rn.flying
        chain_rn.land()
    firsts = [c.value() for c in (chain_rn, chain_r1, chain_r2, chain_r3)]
    chain_last = Chain(reduce_last(jnp.concatenate(firsts, -2)))
    chain_dp = Chain(one_step(d_pre_one[:, mine : mine + more], lambda x: from_behind(x, 1)))
    chain_last.launch(chain_last.ready[0])
    landed = chain_last.flying
    chain_last.land()
    hook(landed, start=[chain_dp] + chain_ds[1:])
    hook(landed, finish=[chain_rb, chain_r4], start=[chain_rb, chain_r4])
    chain_last.launch(chain_last.ready[0])
    landed = chain_last.flying
    chain_last.land()
    out_n1, out_s1, out_n2, out_e1 = unpack(
        chain_last.value(), [(channels, m1), (9 * m1, m1), (channels, m2), (m1, channels)]
    )
    (out_s2,) = unpack(chain_r4.value(), [(9 * m2, m2)])
    out_sc, out_e2 = unpack(chain_rb.value(), [(channels, outward), (m2, outward)])
    (grad_input,) = call(
        k_input, micro,
        [(d_pre_one, "m"), (chain_dp.value(), "m"), (d_summed, "m"), (narrow_a, "w")]
        + [(c.value(), "w") for c in chain_ds],
        [((micro, own * across * channels // LANES, LANES), F32, "m")],
        [((mine, m1), BF), ((mine, channels), F32)],
        after=[landed, chain_last.value(), chain_r4.value(), chain_rb.value()],
    )
    grad_input = grad_input.reshape(features.shape)
    added = lambda k, us: jnp.concatenate([u[k] + u[k + 2] + u[k + 4] for u in us])
    first = (u1, u2, u3)
    later = (u4, u5, u67)
    return (
        outputs, grad_input, out_n1, out_s1, out_e1,
        added(1, first), added(0, first),
        out_n2, out_s2, out_e2, out_sc,
        added(1, later), added(0, later),
    )


def solution(mesh):
    wide = P(None, "batch", "rows", None, None)
    shard = P("rows", None)
    return jax.shard_map(
        shards,
        mesh=mesh,
        in_specs=(
            wide, P(None, "batch", None), shard, shard, shard, P(), P(),
            shard, shard, shard, shard, P(), P(), wide,
        ),
        out_specs=(
            wide, wide, shard, shard, shard, P(), P(),
            shard, shard, shard, shard, P(), P(),
        ),
        check_vma=False,
    )
```
